256 devices in a mesh: lat: 16 (over z_hi, x, core), lev: 16 (over y, z_lo).
Axes of the slice: x: 4, y: 4, z: 8 (z_hi: 2, z_lo: 4; z = z_hi * 4 + z_lo), core: 2. Of those that a mesh axis runs over, the one named last changes fastest.
Arguments:
- tracers: float32 [9, 256, 32, 1152], P(None, 'lat', 'lev'), may hold values from -6 to 6
- thickness: float32 [256, 32, 1152], P('lat', 'lev'), may hold values from 0.5 to 2
- courant_x: float32 [256, 32, 1152], P('lat', 'lev'), may hold values from -0.24 to 0.24
- courant_y: float32 [256, 32, 1152], P('lat', 'lev'), may hold values from -0.24 to 0.24
- level_index: int32 [31, 256, 1152], P(None, 'lat', 'lev'), may hold values from 0 to 31, as said below
- level_offset: int32 [31, 256, 1152], P(None, 'lat', 'lev'), may hold values from 0 to 31, as said below
- level_phase: float32 [31, 256, 1152], P(None, 'lat', 'lev'), may hold values from 0 to 1
Outputs:
- layer_mass: float32 [10, 256, 32, 1152], P(None, 'lat', 'lev')
The draws below stay inside these ranges and needn't reach their ends.
Inputs may be any that keep to these rules, and one draw needn't show every extreme that they name: Along the interfaces of a column, 32 level_index + level_offset rises strictly; each column follows a stretched target grid of its own. `level_offset`: see level_index.
All inputs are finite; a program needn't handle non-finite values.
Results may differ from the reference program's by a relative error of at most 0.0003.
Values sent between devices are 32-bit elements; how exact they have to be, the bound alone decides.
No kernel may reach another device: no remote copies, remote signals or barrier semaphores. Data moves between devices by JAX's collectives and lax.ppermute only.
A program may use at most 128 MiB of HBM per device.

```python
import jax
import jax.numpy as jnp
from jax import lax

NTR = 9
NLON = 1152
NLAT = 256
NLEV = 32


def target_positions(key):
    stretch = jax.random.randint(key, (1, NLAT, NLON), 0, NLEV // 2)
    level = jnp.arange(1, NLEV, dtype=jnp.int32)[:, None, None]
    return 32 * level * (level * stretch + NLEV * (NLEV - stretch)) // (NLEV * NLEV)


def draw_level_index(key, part):
    return (target_positions(key) // 32).astype(jnp.int32)


def draw_level_offset(key, part):
    return (target_positions(key) % 32).astype(jnp.int32)


def shard_levels(own_key, shape, shards, least, high):
    loudness, own = 1.0, jax.random.fold_in(own_key, 6)
    for position, shards_of in shards:
        draws = jnp.exp(jax.random.uniform(jax.random.fold_in(own, position), (shards_of,), jnp.float32, least / len(shards), high / len(shards)))
        loudness = loudness * jnp.repeat(draws, shape[position] // shards_of).reshape([-1 if axis == position else 1 for axis in range(len(shape))])
    return loudness


def normal_values(key, dims, scale, bound, shards=(), held_as=jnp.bfloat16):
    level = shard_levels(key, dims, shards, -0.22, 0.18) if shards else 1.0
    values = jax.random.normal(key, dims, jnp.float32) * scale * level
    return jnp.minimum(jnp.maximum(values, -bound), bound).astype(held_as)


def setup_inputs(seed: int = 0) -> dict:
    key_list = jax.random.split(jax.random.key(seed), 8)
    tracers = normal_values(key_list[0], (NTR, NLAT, NLEV, NLON), 1.0, 6.0, ((1, 16), (2, 16)), jnp.float32)
    thickness = jnp.clip(0.5 + 1.5 * jax.random.uniform(key_list[1], (NLAT, NLEV, NLON), jnp.float32) ** shard_levels(key_list[1], (NLAT, NLEV, NLON), ((0, 16), (1, 16)), -0.2, 0.2), 0.5, 2.0)
    courant_x = jnp.clip(jax.random.uniform(key_list[2], (NLAT, NLEV, NLON), jnp.float32, -0.24, 0.24) * shard_levels(key_list[2], (NLAT, NLEV, NLON), ((0, 16), (1, 16)), -0.4, 0.0), -0.24, 0.24)
    courant_y = jnp.clip(jax.random.uniform(key_list[3], (NLAT, NLEV, NLON), jnp.float32, -0.24, 0.24) * shard_levels(key_list[3], (NLAT, NLEV, NLON), ((0, 16), (1, 16)), -0.4, 0.0), -0.24, 0.24)
    level_index = draw_level_index(jax.random.fold_in(key_list[7], 71), 0)
    level_offset = draw_level_offset(jax.random.fold_in(key_list[7], 71), 0)
    level_phase = jnp.clip(1.0 * jax.random.uniform(key_list[6], (NLEV - 1, NLAT, NLON), jnp.float32) ** shard_levels(key_list[6], (NLEV - 1, NLAT, NLON), ((1, 16), (2, 16)), -0.2, 0.2), 0.0, 1.0)
    return dict(tracers=tracers, thickness=thickness, courant_x=courant_x, courant_y=courant_y, level_index=level_index, level_offset=level_offset, level_phase=level_phase)


sub_units = 32.0


def face_values(courant, q_low, slope_low, q_high, slope_high):
    return jnp.where(courant > 0, q_low + 0.5 * (1.0 - courant) * slope_low, q_high - 0.5 * (1.0 + courant) * slope_high)


def remap_columns(m, index, offset, phase):
    left = jnp.concatenate([m[:, :1], 0.5 * (m[:, :-1] + m[:, 1:])], 1)
    right = jnp.concatenate([left[:, 1:], m[:, -1:]], 1)
    slope = right - left
    curve = 6.0 * (m - 0.5 * (left + right))
    below = jnp.cumsum(m, axis=1) - m
    pick = jnp.broadcast_to(index[None], (m.shape[0],) + index.shape)
    frac = (offset.astype(jnp.float32) + phase) / sub_units
    part = jnp.take_along_axis(left, pick, axis=1) * frac
    part = part + jnp.take_along_axis(slope, pick, axis=1) * frac * frac * 0.5
    part = part + jnp.take_along_axis(curve, pick, axis=1) * (frac * frac * 0.5 - frac * frac * frac / 3.0)
    inner = jnp.take_along_axis(below, pick, axis=1) + part
    total = below[:, -1:] + m[:, -1:]
    edges = jnp.concatenate([jnp.zeros_like(total), inner, total], 1)
    return edges[:, 1:] - edges[:, :-1]


def reference(tracers, thickness, courant_x, courant_y, level_index, level_offset, level_phase):
    index_cols = level_index.reshape(NLEV - 1, NLAT * NLON)
    offset_cols = level_offset.reshape(NLEV - 1, NLAT * NLON)
    phase_cols = level_phase.reshape(NLEV - 1, NLAT * NLON)

    def remap_field(field):
        cols = jnp.transpose(field, (1, 0, 2)).reshape(NLEV, NLAT * NLON)
        result = remap_columns(cols[None], index_cols, offset_cols, phase_cols)[0]
        return jnp.transpose(result.reshape(NLEV, NLAT, NLON), (1, 0, 2))

    cy = courant_y.at[0].set(0.0)
    faces_y = jnp.pad(cy, ((0, 1), (0, 0), (0, 0)))
    dp_pad = jnp.pad(thickness, ((1, 1), (0, 0), (0, 0)))
    west = jnp.roll(thickness, 1, axis=2)
    mass_x = jnp.where(courant_x > 0, courant_x * west, courant_x * thickness)
    mass_y = jnp.where(faces_y > 0, faces_y * dp_pad[:-1], faces_y * dp_pad[1:])
    air = thickness + mass_x - jnp.roll(mass_x, -1, axis=2) + mass_y[:-1] - mass_y[1:]

    def one_tracer(q):
        slope_x = (jnp.roll(q, -1, axis=2) - jnp.roll(q, 1, axis=2)) * 0.5
        flux_x = mass_x * face_values(courant_x, jnp.roll(q, 1, axis=2), jnp.roll(slope_x, 1, axis=2), q, slope_x)
        padded = jnp.pad(q, ((2, 2), (0, 0), (0, 0)))
        near = padded[1:-1]
        slope_y = (padded[2:] - padded[:-2]) * 0.5
        flux_y = mass_y * face_values(faces_y, near[:-1], slope_y[:-1], near[1:], slope_y[1:])
        mass = thickness * q + flux_x - jnp.roll(flux_x, -1, axis=2) + flux_y[:-1] - flux_y[1:]
        return remap_field(mass)

    moved = lax.map(one_tracer, tracers)
    return jnp.concatenate([moved, remap_field(air)[None]], 0)
```

```python
import functools

import jax
import jax.numpy as jnp
from jax import lax
from jax.experimental import pallas as pl
from jax.experimental.pallas import tpu as pltpu
from jax.sharding import PartitionSpec as P

F32 = jnp.float32
NTR = 9
ROWS = 16
LEVS = 2
LANES = 128
TILES = 9
CHUNK = 72
GROUPS = 16
HELD = ROWS + 4
STEP = TILES * LEVS
FIELD = HELD * STEP
VMEM_LIMIT = 40 * 1024 * 1024

PARTS = ((8, 1, True), (0, 4, False), (4, 4, False))


def fields_of(part):
    return part[1] + int(part[2])


def depth_of(part):
    return fields_of(part) * LEVS * 8 + 8


def lane_index():
    return lax.broadcasted_iota(jnp.int32, (8, LANES), 1)


def row_index():
    return lax.broadcasted_iota(jnp.int32, (8, LANES), 0)


def turn(x, shift, axis):
    shift = shift % x.shape[axis]
    return x if shift == 0 else pltpu.roll(x, shift, axis)


def west_of(tiles, lane):
    rolled = [turn(x, 1, 1) for x in tiles]
    return [jnp.where(lane == 0, rolled[c - 1], rolled[c]) for c in range(TILES)]


def east_of(tiles, lane):
    rolled = [turn(x, -1, 1) for x in tiles]
    return [jnp.where(lane == LANES - 1, rolled[(c + 1) % TILES], rolled[c]) for c in range(TILES)]


def span_of(group):
    return divmod(CHUNK * group, LANES)


def halo_kernel(tracers, thickness, courant_y, low, high, sem):
    copies = []
    for edge, (out, first) in enumerate(((low, 0), (high, ROWS - 2))):
        rows = pl.ds(first, 2)
        copies.append(pltpu.make_async_copy(tracers.at[:, rows], out.at[pl.ds(0, NTR)], sem.at[edge, 0]))
        copies.append(pltpu.make_async_copy(thickness.at[rows], out.at[NTR], sem.at[edge, 1]))
        copies.append(pltpu.make_async_copy(courant_y.at[rows], out.at[NTR + 1], sem.at[edge, 2]))
    for copy in copies:
        copy.start()
    for copy in copies:
        copy.wait()


def transport_kernel(part, lat, tracers, thickness, courant_x, courant_y, low, high, out, held, mx, ax, my, ay, fy, sem):
    first, count, with_air = part
    depth = depth_of(part)
    rest = depth - 8
    lane, row = lane_index(), row_index()
    view = held.reshape(count + 3, HELD, TILES, LEVS, LANES)
    copies = []
    for c in range(TILES):
        cut = pl.ds(LANES * c, LANES)
        own = pl.ds(2, ROWS)
        for source, target in (
            (thickness.at[:, :, cut], view.at[0, own, c]),
            (courant_y.at[:, :, cut], view.at[1, own, c]),
            (courant_x.at[:, :, cut], view.at[2, own, c]),
            (tracers.at[pl.ds(first, count), :, :, cut], view.at[pl.ds(3, count), own, c]),
            (low.at[NTR, :, :, cut], view.at[0, pl.ds(0, 2), c]),
            (low.at[pl.ds(first, count), :, :, cut], view.at[pl.ds(3, count), pl.ds(0, 2), c]),
            (high.at[pl.ds(NTR, 2), :, :, cut], view.at[pl.ds(0, 2), pl.ds(ROWS + 2, 2), c]),
            (high.at[pl.ds(first, count), :, :, cut], view.at[pl.ds(3, count), pl.ds(ROWS + 2, 2), c]),
        ):
            copies.append(pltpu.make_async_copy(source, target, sem.at[len(copies)]))
    for copy in copies:
        copy.start()
    for g in range(GROUPS):
        out[g, pl.ds(rest, 8), :] = jnp.zeros((8, LANES), F32)
    for copy in copies:
        copy.wait()

    def rows_of(array, j, c, l):
        return held[pl.ds(array * FIELD + (j + 2) * STEP + c * LEVS + l, 8, stride=STEP), :]

    def whole_row(array, j):
        return held[pl.ds(array * FIELD + (j + 2) * STEP, STEP), :]

    def place(l, c, h):
        return pl.ds((c * LEVS + l) * ROWS + 8 * h, 8)

    def factors(courant, before, after):
        mass = jnp.where(courant > 0, courant * before, courant * after)
        return mass, mass * jnp.where(courant > 0, 0.25 - 0.25 * courant, -0.25 - 0.25 * courant)

    keep = (row > 0) | (lat[0] > 0)
    for l in range(LEVS):
        for h in range(2):
            thick = [rows_of(0, 8 * h, c, l) for c in range(TILES)]
            west = west_of(thick, lane)
            for c in range(TILES):
                mass, tilt = factors(rows_of(2, 8 * h, c, l), west[c], thick[c])
                mx[place(l, c, h), :] = mass
                ax[place(l, c, h), :] = tilt
                courant = rows_of(1, 8 * h, c, l)
                if h == 0:
                    courant = jnp.where(keep, courant, 0.0)
                mass, tilt = factors(courant, rows_of(0, 8 * h - 1, c, l), thick[c])
                my[place(l, c, h), :] = mass
                ay[place(l, c, h), :] = tilt
    last_mass, last_tilt = factors(whole_row(1, ROWS), whole_row(0, ROWS - 1), whole_row(0, ROWS))

    def send(field, l, tiles):
        slot = l * 4 + field
        for g in range(GROUPS):
            t, o = span_of(g)
            a = turn(tiles[0][t], -o, 1)
            b = turn(tiles[1][t], CHUNK - o, 1)
            if o + CHUNK > LANES:
                a = jnp.where(lane < LANES - o, a, turn(tiles[0][t + 1], -o, 1))
                lon = jnp.where(lane >= CHUNK, lane - CHUNK, lane + (LANES - CHUNK))
                b = jnp.where(lon < LANES - o, b, turn(tiles[1][t + 1], CHUNK - o, 1))
            out[g, pl.ds(pl.multiple_of((field * LEVS + l) * 8, 8), 8), :] = jnp.where(lane < CHUNK, a, b)
            moved = pltpu.roll(b, slot * 16, 1)
            out[g, pl.ds(rest, 8), :] = jnp.where((lane >> 4) == slot, moved, out[g, pl.ds(rest, 8), :])

    def tracer(field, _):
        array = 3 + field
        edge_q = [whole_row(array, ROWS + k) for k in (-2, -1, 0, 1)]
        up = last_mass > 0
        value = jnp.where(up, edge_q[1], edge_q[2])
        rise = jnp.where(up, edge_q[2] - edge_q[0], edge_q[3] - edge_q[1])
        fy[pl.ds(ROWS, STEP, stride=24), :] = last_mass * value + last_tilt * rise
        for l in range(LEVS):
            tiles = []
            for h in range(2):
                q = [rows_of(array, 8 * h, c, l) for c in range(TILES)]
                qw = west_of(q, lane)
                qe = east_of(q, lane)
                d = [qe[c] - qw[c] for c in range(TILES)]
                dw = west_of(d, lane)
                flux = []
                for c in range(TILES):
                    mass = mx[place(l, c, h), :]
                    up = mass > 0
                    flux.append(mass * jnp.where(up, qw[c], q[c]) + ax[place(l, c, h), :] * jnp.where(up, dw[c], d[c]))
                flux_e = east_of(flux, lane)
                now = []
                for c in range(TILES):
                    mass = my[place(l, c, h), :]
                    up = mass > 0
                    q2, q1, q3 = (rows_of(array, 8 * h + k, c, l) for k in (-2, -1, 1))
                    value = jnp.where(up, q1, q[c])
                    rise = jnp.where(up, q[c] - q2, q3 - q1)
                    flux_y = mass * value + ay[place(l, c, h), :] * rise
                    fy[pl.ds((c * LEVS + l) * 24 + 8 * h, 8), :] = flux_y
                    thick = rows_of(0, 8 * h, c, l)
                    now.append(thick * q[c] + (flux[c] - flux_e[c]) + flux_y)
                tiles.append(now)
            for h in range(2):
                for c in range(TILES):
                    tiles[h][c] = tiles[h][c] - fy[pl.ds((c * LEVS + l) * 24 + 8 * h + 1, 8), :]
            send(field, l, tiles)
        return 0

    if count == 1:
        tracer(0, 0)
    else:
        lax.fori_loop(0, count, tracer, 0)
    if with_air:
        fy[pl.ds(ROWS, STEP, stride=24), :] = last_mass
        for l in range(LEVS):
            tiles = []
            for c in range(TILES):
                for h in range(2):
                    fy[pl.ds((c * LEVS + l) * 24 + 8 * h, 8), :] = my[place(l, c, h), :]
            for h in range(2):
                flux = [mx[place(l, c, h), :] for c in range(TILES)]
                flux_e = east_of(flux, lane)
                tiles.append(
                    [
                        rows_of(0, 8 * h, c, l)
                        + (flux[c] - flux_e[c])
                        + (my[place(l, c, h), :] - fy[pl.ds((c * LEVS + l) * 24 + 8 * h + 1, 8), :])
                        for c in range(TILES)
                    ]
                )
            send(count, l, tiles)


def target_kernel(index, offset, phase, level, frac):
    lane = lane_index()

    def spread(x0, x1, zero):
        moved = pltpu.roll(x1, CHUNK, 1)
        main = jnp.where(lane < CHUNK, x0, moved)
        tail = jnp.where(lane < 16, moved, zero)
        tail = tail + pltpu.roll(tail, 16, 1)
        tail = tail + pltpu.roll(tail, 32, 1)
        other = pltpu.roll(pltpu.roll(tail, 64, 1), 4, 0)
        return main, jnp.where(lane < 64, tail, other)

    level[pl.ds(0, 16), :] = jnp.zeros((16, LANES), jnp.int32)
    frac[pl.ds(0, 16), :] = jnp.zeros((16, LANES), F32)
    blank = jnp.zeros((8, LANES - CHUNK), F32)

    def wide(x):
        return jnp.concatenate([x, blank.astype(x.dtype)], 1)

    def one(n, _):
        halves = [wide(index[n, pl.ds(8 * h, 8), :]) for h in range(2)]
        parts = [
            wide((offset[n, pl.ds(8 * h, 8), :].astype(F32) + phase[n, pl.ds(8 * h, 8), :]) * (1.0 / 32.0))
            for h in range(2)
        ]
        for out, (x0, x1), zero in ((level, halves, 0), (frac, parts, 0.0)):
            main, tail = spread(x0, x1, zero)
            out[pl.ds(pl.multiple_of((n + 1) * 16, 16), 8), :] = main
            out[pl.ds(pl.multiple_of((n + 1) * 16 + 8, 8), 8), :] = tail
        return 0

    lax.fori_loop(0, 2 * GROUPS - 1, one, 0)


def pick(x, where):
    return jnp.take_along_axis(x, where, axis=0, mode="promise_in_bounds")


def remap_kernel(part, data, level, frac, out):
    fields, depth = fields_of(part), depth_of(part)
    rest = depth - 8
    lane, row = lane_index(), row_index()

    def targets(tile):
        found = []
        for parity in range(2):
            for half in range(2):
                start = (parity + 16 * half) * 16 + tile
                s = level[pl.ds(start, 8, stride=32), :]
                f = frac[pl.ds(start, 8, stride=32), :]
                square = f * f * 0.5
                cubic = 3.0 * square - f * f * f
                found.append(((s >> 1) & 7, s >= 16, (s & 1) == 1, f, square, cubic))
        return found

    def columns(even, odd, found):
        back = [turn(x, 1, 0) for x in odd]
        before = [jnp.where(row == 0, even[0], back[0]), jnp.where(row == 0, back[0], back[1])]
        left = [0.5 * (before[i] + even[i]) for i in range(2)]
        ahead = [turn(x, -1, 0) for x in left]
        right = [jnp.where(row == 7, ahead[1], ahead[0]), jnp.where(row == 7, odd[1], ahead[1])]
        pair = [even[i] + odd[i] for i in range(2)]
        run = list(pair)
        for shift in (1, 2, 4):
            run = [x + jnp.where(row >= shift, turn(x, shift, 0), 0.0) for x in run]
        half_sum = jnp.broadcast_to(run[0][7:8], (8, LANES))
        total = half_sum + run[1][7:8]
        below = [run[0] - pair[0], (run[1] - pair[1]) + half_sum]
        edges = []
        for where, high, is_odd, f, square, cubic in found:
            le, ri, ev, od, be = (
                jnp.where(high, pick(x[1], where), pick(x[0], where)) for x in (left, right, even, odd, below)
            )
            middle = 0.5 * (ev + od)
            lo = jnp.where(is_odd, middle, le)
            hi = jnp.where(is_odd, ri, middle)
            m = jnp.where(is_odd, od, ev)
            base = be + jnp.where(is_odd, ev, 0.0)
            edges.append(base + lo * f + (hi - lo) * square + ((m + m) - (lo + hi)) * cubic)
        ev0, ev1, od0, od1 = edges
        next0, next1 = turn(ev0, -1, 0), turn(ev1, -1, 0)
        new_even = [od0 - ev0, od1 - ev1]
        new_odd = [jnp.where(row == 7, next1, next0) - od0, jnp.where(row == 7, total, next1) - od1]
        return new_even, new_odd

    def span(start, half):
        return pl.ds(start + half * 8 * depth, 8, stride=depth)

    def main(tile, _):
        found = targets(tile)
        for field in range(fields):
            at = [(field * LEVS + l) * 8 + tile for l in range(LEVS)]
            even, odd = ([data[span(at[l], half), :] for half in range(2)] for l in range(LEVS))
            new = columns(even, odd, found)
            for l in range(LEVS):
                for half in range(2):
                    out[span(at[l], half), :] = new[l][half]
        return 0

    lax.fori_loop(0, 8, main, 0)

    def tail(tile, _):
        found = targets(8 + tile)
        at = [rest + tile, rest + tile + 4]
        a, b = ([data[span(at[i], half), :] for half in range(2)] for i in range(2))
        even = [jnp.where(lane < 64, a[half], turn(b[half], 64, 1)) for half in range(2)]
        odd = [jnp.where(lane < 64, turn(a[half], 64, 1), b[half]) for half in range(2)]
        even, odd = columns(even, odd, found)
        for half in range(2):
            out[span(at[0], half), :] = jnp.where(lane < 64, even[half], turn(odd[half], 64, 1))
            out[span(at[1], half), :] = jnp.where(lane < 64, turn(even[half], 64, 1), odd[half])
        return 0

    lax.fori_loop(0, 4, tail, 0)


def collect_kernel(part, data, *refs):
    out, flat, sem = refs[-3:]
    fields, depth = fields_of(part), depth_of(part)
    rest = depth - 8
    lane = lane_index()

    def gather(field, _):
        for l in range(LEVS):
            slot = l * 4 + field
            pieces = []
            for g in range(GROUPS):
                _, o = span_of(g)
                main = data[g, pl.ds(pl.multiple_of((field * LEVS + l) * 8, 8), 8), :]
                tail = pltpu.roll(data[g, pl.ds(rest, 8), :], LANES - slot * 16, 1)
                mixed = jnp.where(lane < 16, tail, main)
                pieces.append((turn(main, o, 1), turn(mixed, o - CHUNK, 1)))
            for h in range(2):
                for c in range(TILES):
                    value = None
                    for g in range(GROUPS):
                        start = CHUNK * g - LANES * c
                        if start >= LANES or start + CHUNK <= 0:
                            continue
                        piece = pieces[g][h]
                        value = piece if value is None else jnp.where(lane >= start, piece, value)
                    at = field * (ROWS * STEP) + 8 * h * STEP + c * LEVS + l
                    flat[pl.ds(at, 8, stride=STEP), :] = value
        return 0

    lax.fori_loop(0, fields, gather, 0)
    view = flat.reshape(fields, ROWS, TILES, LEVS, LANES)
    first, count, with_air = part
    copies = []
    for c in range(TILES):
        cut = pl.ds(LANES * c, LANES)
        target = out.at[pl.ds(first, fields), :, :, cut]
        copies.append(pltpu.make_async_copy(view.at[:, :, c], target, sem.at[c]))
    for copy in copies:
        copy.start()
    for copy in copies:
        copy.wait()


ANYWHERE = pl.BlockSpec(memory_space=pl.ANY)
IN_VMEM = pl.BlockSpec(memory_space=pltpu.VMEM)
PARAMS = pltpu.CompilerParams(vmem_limit_bytes=VMEM_LIMIT)


def transport(part, lat, tracers, thickness, courant_x, courant_y, low, high):
    shape = (GROUPS, depth_of(part), LANES)
    factor = pltpu.VMEM((LEVS * TILES * ROWS, LANES), F32)
    return pl.pallas_call(
        functools.partial(transport_kernel, part),
        out_shape=jax.ShapeDtypeStruct(shape, F32),
        in_specs=[pl.BlockSpec(memory_space=pltpu.SMEM)] + [ANYWHERE] * 6,
        out_specs=IN_VMEM,
        scratch_shapes=[
            pltpu.VMEM(((part[1] + 3) * FIELD, LANES), F32),
            factor,
            factor,
            factor,
            factor,
            pltpu.VMEM((STEP * 24, LANES), F32),
            pltpu.SemaphoreType.DMA((8 * TILES,)),
        ],
        compiler_params=PARAMS,
    )(lat, tracers, thickness, courant_x, courant_y, low, high)


def remap(part, data, level, frac):
    depth = depth_of(part)
    return pl.pallas_call(
        functools.partial(remap_kernel, part),
        out_shape=jax.ShapeDtypeStruct((GROUPS * depth, LANES), F32),
        in_specs=[IN_VMEM] * 3,
        out_specs=IN_VMEM,
        compiler_params=PARAMS,
    )(data.reshape(GROUPS * depth, LANES), level, frac).reshape(GROUPS, depth, LANES)


def collect(part, data, result):
    shape = (NTR + 1, ROWS, LEVS, LANES * TILES)
    given = (data,) if result is None else (data, result)
    return pl.pallas_call(
        functools.partial(collect_kernel, part),
        out_shape=jax.ShapeDtypeStruct(shape, F32),
        in_specs=[IN_VMEM, ANYWHERE][: len(given)],
        out_specs=ANYWHERE,
        scratch_shapes=[
            pltpu.VMEM((fields_of(part) * ROWS * STEP, LANES), F32),
            pltpu.SemaphoreType.DMA((TILES,)),
        ],
        input_output_aliases={} if result is None else {1: 0},
        compiler_params=PARAMS,
    )(*given)


def exchange(data):
    return lax.all_to_all(data, "lev", split_axis=0, concat_axis=0, tiled=True)


def shards(tracers, thickness, courant_x, courant_y, level_index, level_offset, level_phase):
    rim = jax.ShapeDtypeStruct((NTR + 2, 2, LEVS, LANES * TILES), F32)
    south, north = pl.pallas_call(
        halo_kernel,
        out_shape=(rim, rim),
        in_specs=[ANYWHERE] * 3,
        out_specs=(ANYWHERE, ANYWHERE),
        scratch_shapes=[pltpu.SemaphoreType.DMA((2, 3))],
    )(tracers, thickness, courant_y)
    count = lax.axis_size("lat")
    low = lax.ppermute(north, "lat", [(i, i + 1) for i in range(count - 1)])
    high = lax.ppermute(south, "lat", [(i + 1, i) for i in range(count - 1)])
    table = (2 * GROUPS * 16, LANES)
    level, frac = pl.pallas_call(
        target_kernel,
        out_shape=(jax.ShapeDtypeStruct(table, jnp.int32), jax.ShapeDtypeStruct(table, F32)),
        in_specs=[IN_VMEM] * 3,
        out_specs=(IN_VMEM, IN_VMEM),
        compiler_params=PARAMS,
    )(level_index, level_offset, level_phase)
    lat = lax.axis_index("lat").astype(jnp.int32).reshape(1)
    result = None
    sent = [transport(part, lat, tracers, thickness, courant_x, courant_y, low, high) for part in PARTS]
    taken = [exchange(x) for x in sent]
    mapped = [remap(part, x, level, frac) for part, x in zip(PARTS, taken)]
    back = [exchange(x) for x in mapped]
    for part, x in zip(PARTS, back):
        result = collect(part, x, result)
    return result


def solution(mesh):
    in_specs = (
        P(None, "lat", "lev", None),
        P("lat", "lev", None),
        P("lat", "lev", None),
        P("lat", "lev", None),
        P(None, "lat", "lev"),
        P(None, "lat", "lev"),
        P(None, "lat", "lev"),
    )
    out_specs = P(None, "lat", "lev", None)
    return jax.shard_map(shards, mesh=mesh, in_specs=in_specs, out_specs=out_specs, check_vma=False)
```

```python
import functools

import jax
import jax.numpy as jnp
from jax import lax
from jax.experimental import pallas as pl
from jax.experimental.pallas import tpu as pltpu
from jax.sharding import PartitionSpec as P

F32 = jnp.float32
NTR = 9
FIELDS = NTR + 1
PAIRS = FIELDS // 2
ROWS = 16
LEVS = 2
LANES = 128
TILES = 9
LONS = LANES * TILES
CHUNK = 72
GROUPS = 16
STEP = TILES * LEVS
VMEM_LIMIT = 40 * 1024 * 1024

INNER, OUTER = 1, 2

REST = PAIRS * LEVS * 8
BLOCKS = (PAIRS + 3) // 4
DEPTH = REST + BLOCKS * 8

THICK, NORTH, EAST = NTR, NTR + 1, NTR + 2


def slots_of(part):
    return 8 + 4 * part


def lane_index():
    return lax.broadcasted_iota(jnp.int32, (8, LANES), 1)


def row_index():
    return lax.broadcasted_iota(jnp.int32, (8, LANES), 0)


def turn(x, shift, axis):
    shift = shift % x.shape[axis]
    return x if shift == 0 else pltpu.roll(x, shift, axis)


def west_of(tiles, lane):
    rolled = [turn(x, 1, 1) for x in tiles]
    return [jnp.where(lane == 0, rolled[c - 1], rolled[c]) for c in range(TILES)]


def east_of(tiles, lane):
    rolled = [turn(x, -1, 1) for x in tiles]
    return [jnp.where(lane == LANES - 1, rolled[(c + 1) % TILES], rolled[c]) for c in range(TILES)]


def span_of(group):
    return divmod(CHUNK * group, LANES)


def pick(x, where):
    return jnp.take_along_axis(x, where, axis=0, mode="promise_in_bounds")


def halo_kernel(tracers, thickness, courant_y, low, high, sem):
    copies = []
    for edge, (out, first) in enumerate(((low, 0), (high, ROWS - 2))):
        rows = pl.ds(first, 2)
        copies.append(pltpu.make_async_copy(tracers.at[:, rows], out.at[pl.ds(0, NTR)], sem.at[edge, 0]))
        copies.append(pltpu.make_async_copy(thickness.at[rows], out.at[THICK], sem.at[edge, 1]))
        copies.append(pltpu.make_async_copy(courant_y.at[rows], out.at[NORTH], sem.at[edge, 2]))
    for copy in copies:
        copy.start()
    for copy in copies:
        copy.wait()


def transport_kernel(part, *refs):
    if part == OUTER:
        lat, tracers, thickness, courant_x, courant_y, low, high, out, held, mx, ax, my, ay, fy, sem = refs
    else:
        tracers, thickness, courant_x, courant_y, out, held, mx, ax, my, ay, fy, sem = refs
    slots = slots_of(part)
    lane, row = lane_index(), row_index()
    view = held.reshape(NTR + 3, slots // part, part, TILES, LEVS, LANES)
    copies = []

    def bring(source, target):
        copies.append(pltpu.make_async_copy(source, target, sem.at[len(copies)]))

    for c in range(TILES):
        cut = pl.ds(LANES * c, LANES)
        runs = ((2, 12, 0, 0),) if part == INNER else ((0, 6, 2, 0), (10, 6, 0, 1))
        for first, size, at, run in runs:
            own, into = pl.ds(first, size), pl.ds(at, size)
            bring(tracers.at[:, own, :, cut], view.at[pl.ds(0, NTR), into, run, c])
            for array, source in ((THICK, thickness), (NORTH, courant_y), (EAST, courant_x)):
                bring(source.at[own, :, cut], view.at[array, into, run, c])
        if part == OUTER:
            bring(low.at[pl.ds(0, NTR + 1), :, :, cut], view.at[pl.ds(0, NTR + 1), pl.ds(0, 2), 0, c])
            bring(high.at[:, :, :, cut], view.at[pl.ds(0, NTR + 2), pl.ds(6, 2), 1, c])
    for copy in copies:
        copy.start()
    for g in range(GROUPS):
        out[g, pl.ds(REST, 8 * BLOCKS), :] = jnp.zeros((8 * BLOCKS, LANES), F32)
    for copy in copies:
        copy.wait()

    def rows_of(array, shift, c, l):
        start = (array * slots + (2 + shift) * part) * STEP + c * LEVS + l
        return held[pl.ds(start, 8, stride=STEP), :]

    def past(array, shift):
        return held[pl.ds((array * slots + 8 + (2 + shift) * part) * STEP, part * STEP), :]

    def place(l, c):
        return pl.ds((c * LEVS + l) * 8, 8)

    def faces(l, c, shift):
        return pl.ds((c * LEVS + l) * 16 + shift, 8)

    def keep_past(values):
        for run in range(part):
            fy[pl.ds(8 + run, STEP, stride=16), :] = values[run * STEP : (run + 1) * STEP]

    def factors(courant, before, after):
        mass = jnp.where(courant > 0, courant * before, courant * after)
        return mass, mass * jnp.where(courant > 0, 0.25 - 0.25 * courant, -0.25 - 0.25 * courant)

    for l in range(LEVS):
        thick = [rows_of(THICK, 0, c, l) for c in range(TILES)]
        west = west_of(thick, lane)
        for c in range(TILES):
            mx[place(l, c), :], ax[place(l, c), :] = factors(rows_of(EAST, 0, c, l), west[c], thick[c])
            courant = rows_of(NORTH, 0, c, l)
            if part == OUTER:
                courant = jnp.where((row > 0) | (lat[0] > 0), courant, 0.0)
            my[place(l, c), :], ay[place(l, c), :] = factors(courant, rows_of(THICK, -1, c, l), thick[c])
    past_mass, past_tilt = factors(past(NORTH, 0), past(THICK, -1), past(THICK, 0))

    def air():
        keep_past(past_mass)
        for l in range(LEVS):
            for c in range(TILES):
                fy[faces(l, c, 0), :] = my[place(l, c), :]
        tiles = []
        for l in range(LEVS):
            flux = [mx[place(l, c), :] for c in range(TILES)]
            flux_e = east_of(flux, lane)
            tiles.append(
                [
                    rows_of(THICK, 0, c, l) + (flux[c] - flux_e[c]) + (my[place(l, c), :] - fy[faces(l, c, part), :])
                    for c in range(TILES)
                ]
            )
        return tiles

    def tracer(array):
        past_q = [past(array, shift) for shift in (-2, -1, 0, 1)]
        up = past_mass > 0
        value = jnp.where(up, past_q[1], past_q[2])
        rise = jnp.where(up, past_q[2] - past_q[0], past_q[3] - past_q[1])
        keep_past(past_mass * value + past_tilt * rise)
        tiles = []
        for l in range(LEVS):
            q = [rows_of(array, 0, c, l) for c in range(TILES)]
            qw = west_of(q, lane)
            qe = east_of(q, lane)
            d = [qe[c] - qw[c] for c in range(TILES)]
            dw = west_of(d, lane)
            flux = []
            for c in range(TILES):
                mass = mx[place(l, c), :]
                up = mass > 0
                flux.append(mass * jnp.where(up, qw[c], q[c]) + ax[place(l, c), :] * jnp.where(up, dw[c], d[c]))
            flux_e = east_of(flux, lane)
            now = []
            for c in range(TILES):
                mass = my[place(l, c), :]
                up = mass > 0
                q2, q1, q3 = (rows_of(array, shift, c, l) for shift in (-2, -1, 1))
                value = jnp.where(up, q1, q[c])
                rise = jnp.where(up, q[c] - q2, q3 - q1)
                flux_y = mass * value + ay[place(l, c), :] * rise
                fy[faces(l, c, 0), :] = flux_y
                now.append(rows_of(THICK, 0, c, l) * q[c] + (flux[c] - flux_e[c]) + flux_y)
            tiles.append(now)
        return [[tiles[l][c] - fy[faces(l, c, part), :] for c in range(TILES)] for l in range(LEVS)]

    def two(pair, _):
        first = tracer(2 * pair)
        send_block(pair, first, tracer(2 * pair + 1))
        return 0

    def send_block(pair, first, second):
        block = REST
        for l in range(LEVS):
            slot = l * 4 + pair
            for g in range(GROUPS):
                pack(g, l, pl.multiple_of((pair * LEVS + l) * 8, 8), block, slot, first, second)

    def pack(g, l, at, block, slot, first, second):
        t, o = span_of(g)
        a = turn(first[l][t], -o, 1)
        b = turn(second[l][t], CHUNK - o, 1)
        if o + CHUNK > LANES:
            a = jnp.where(lane < LANES - o, a, turn(first[l][t + 1], -o, 1))
            lon = jnp.where(lane >= CHUNK, lane - CHUNK, lane + (LANES - CHUNK))
            b = jnp.where(lon < LANES - o, b, turn(second[l][t + 1], CHUNK - o, 1))
        out[g, pl.ds(at, 8), :] = jnp.where(lane < CHUNK, a, b)
        moved = pltpu.roll(b, slot * 16, 1)
        out[g, pl.ds(block, 8), :] = jnp.where((lane >> 4) == slot, moved, out[g, pl.ds(block, 8), :])

    lax.fori_loop(0, PAIRS - 1, two, 0)
    first, second = tracer(NTR - 1), air()
    for l in range(LEVS):
        for g in range(GROUPS):
            pack(g, l, ((PAIRS - 1) * LEVS + l) * 8, REST + 8, l * 4, first, second)


def target_kernel(index, offset, phase, *tables):
    lane, row = lane_index(), row_index()
    blank = jnp.zeros((8, LANES - CHUNK), F32)

    def rows_of(ref, n, part):
        if part == INNER:
            found = ref[n, pl.ds(4, 8), :]
            return jnp.concatenate([found, blank.astype(found.dtype)], 1)
        low, high = (jnp.concatenate([x, blank.astype(x.dtype)], 1) for x in (ref[n, pl.ds(0, 8), :], ref[n, pl.ds(8, 8), :]))
        return jnp.where((row & 1) == 0, pick(low, row >> 1), pick(high, 4 + (row >> 1)))

    for ref in tables:
        ref[pl.ds(0, 16), :] = jnp.zeros((16, LANES), ref.dtype)
    for n in range(2 * GROUPS - 1):
        for part in (INNER, OUTER):
            level, frac = tables[2 * part - 2 : 2 * part]
            s = rows_of(index, n, part)
            f = (rows_of(offset, n, part).astype(F32) + rows_of(phase, n, part)) * (1.0 / 32.0)
            for out, x in ((level, s), (frac, f)):
                moved = turn(x, CHUNK, 1)
                tail = jnp.where(lane < 16, moved, jnp.zeros_like(moved))
                tail = tail + turn(tail, 16, 1)
                tail = tail + turn(tail, 32, 1)
                other = turn(turn(tail, 64, 1), 4, 0)
                out[pl.ds((n + 1) * 16, 8), :] = jnp.where(lane < CHUNK, x, moved)
                out[pl.ds((n + 1) * 16 + 8, 8), :] = jnp.where(lane < 64, tail, other)


def remap_kernel(data, level, frac, out):
    lane, row = lane_index(), row_index()

    def targets(tile):
        found = []
        for parity in range(2):
            for half in range(2):
                start = (parity + 16 * half) * 16 + tile
                s = level[pl.ds(start, 8, stride=32), :]
                f = frac[pl.ds(start, 8, stride=32), :]
                square = f * f * 0.5
                cubic = 3.0 * square - f * f * f
                found.append(((s >> 1) & 7, s >= 16, (s & 1) == 1, f, square, cubic))
        return found

    def columns(even, odd, found):
        back = [turn(x, 1, 0) for x in odd]
        before = [jnp.where(row == 0, even[0], back[0]), jnp.where(row == 0, back[0], back[1])]
        left = [0.5 * (before[i] + even[i]) for i in range(2)]
        ahead = [turn(x, -1, 0) for x in left]
        right = [jnp.where(row == 7, ahead[1], ahead[0]), jnp.where(row == 7, odd[1], ahead[1])]
        pair = [even[i] + odd[i] for i in range(2)]
        run = list(pair)
        for shift in (1, 2, 4):
            run = [x + jnp.where(row >= shift, turn(x, shift, 0), 0.0) for x in run]
        half_sum = jnp.broadcast_to(run[0][7:8], (8, LANES))
        total = half_sum + run[1][7:8]
        below = [run[0] - pair[0], (run[1] - pair[1]) + half_sum]
        edges = []
        for where, high, is_odd, f, square, cubic in found:
            le, ri, ev, od, be = (
                jnp.where(high, pick(x[1], where), pick(x[0], where)) for x in (left, right, even, odd, below)
            )
            middle = 0.5 * (ev + od)
            lo = jnp.where(is_odd, middle, le)
            hi = jnp.where(is_odd, ri, middle)
            m = jnp.where(is_odd, od, ev)
            base = be + jnp.where(is_odd, ev, 0.0)
            edges.append(base + lo * f + (hi - lo) * square + ((m + m) - (lo + hi)) * cubic)
        ev0, ev1, od0, od1 = edges
        next0, next1 = turn(ev0, -1, 0), turn(ev1, -1, 0)
        new_even = [od0 - ev0, od1 - ev1]
        new_odd = [jnp.where(row == 7, next1, next0) - od0, jnp.where(row == 7, total, next1) - od1]
        return new_even, new_odd

    def span(start, half):
        return pl.ds(start + half * 8 * DEPTH, 8, stride=DEPTH)

    def main(tile, _):
        found = targets(tile)
        for pair in range(PAIRS):
            at = [(pair * LEVS + l) * 8 + tile for l in range(LEVS)]
            even, odd = ([data[span(at[l], half), :] for half in range(2)] for l in range(LEVS))
            new = columns(even, odd, found)
            for l in range(LEVS):
                for half in range(2):
                    out[span(at[l], half), :] = new[l][half]
        return 0

    lax.fori_loop(0, 8, main, 0)

    def tail(tile, _):
        found = targets(8 + tile)
        for block in range(BLOCKS):
            at = [REST + 8 * block + tile, REST + 8 * block + tile + 4]
            a, b = ([data[span(at[i], half), :] for half in range(2)] for i in range(2))
            even = [jnp.where(lane < 64, a[half], turn(b[half], 64, 1)) for half in range(2)]
            odd = [jnp.where(lane < 64, turn(a[half], 64, 1), b[half]) for half in range(2)]
            even, odd = columns(even, odd, found)
            for half in range(2):
                out[span(at[0], half), :] = jnp.where(lane < 64, even[half], turn(odd[half], 64, 1))
                out[span(at[1], half), :] = jnp.where(lane < 64, turn(even[half], 64, 1), odd[half])
        return 0

    lax.fori_loop(0, 4, tail, 0)


def collect_kernel(part, data, *refs):
    out, flat, sem = refs[-3:]
    lane = lane_index()

    def unpack(pair, at, block, slot):
        for l in range(LEVS):
            pieces = []
            for g in range(GROUPS):
                _, o = span_of(g)
                main = data[g, at(l), :]
                tail = pltpu.roll(data[g, pl.ds(block, 8), :], LANES - (l * 4 + slot) * 16, 1)
                mixed = jnp.where(lane < 16, tail, main)
                pieces.append((turn(main, o, 1), turn(mixed, o - CHUNK, 1)))
            for second in range(2):
                for c in range(TILES):
                    value = None
                    for g in range(GROUPS):
                        start = CHUNK * g - LANES * c
                        if start >= LANES or start + CHUNK <= 0:
                            continue
                        piece = pieces[g][second]
                        value = piece if value is None else jnp.where(lane >= start, piece, value)
                    flat[pl.ds((2 * pair + second) * 8 * STEP + c * LEVS + l, 8, stride=STEP), :] = value

    def one(pair, _):
        unpack(pair, lambda l: pl.ds(pl.multiple_of((pair * LEVS + l) * 8, 8), 8), REST, pair)
        return 0

    lax.fori_loop(0, PAIRS - 1, one, 0)
    unpack(PAIRS - 1, lambda l: pl.ds(((PAIRS - 1) * LEVS + l) * 8, 8), REST + 8, 0)
    view = flat.reshape(FIELDS, 8 // part, part, TILES, LEVS, LANES)
    copies = []
    for c in range(TILES):
        cut = pl.ds(LANES * c, LANES)
        for run, first in enumerate((4,) if part == INNER else (0, 12)):
            target = out.at[:, pl.ds(first, 8 // part), :, cut]
            copies.append(pltpu.make_async_copy(view.at[:, :, run, c], target, sem.at[len(copies)]))
    for copy in copies:
        copy.start()
    for copy in copies:
        copy.wait()


ANYWHERE = pl.BlockSpec(memory_space=pl.ANY)
IN_VMEM = pl.BlockSpec(memory_space=pltpu.VMEM)
PARAMS = pltpu.CompilerParams(vmem_limit_bytes=VMEM_LIMIT)


def transport(part, *given):
    factor = pltpu.VMEM((STEP * 8, LANES), F32)
    scalars = [pl.BlockSpec(memory_space=pltpu.SMEM)] if part == OUTER else []
    return pl.pallas_call(
        functools.partial(transport_kernel, part),
        out_shape=jax.ShapeDtypeStruct((GROUPS, DEPTH, LANES), F32),
        in_specs=scalars + [ANYWHERE] * (len(given) - len(scalars)),
        out_specs=IN_VMEM,
        scratch_shapes=[
            pltpu.VMEM(((NTR + 3) * slots_of(part) * STEP, LANES), F32),
            factor,
            factor,
            factor,
            factor,
            pltpu.VMEM((STEP * 16, LANES), F32),
            pltpu.SemaphoreType.DMA((10 * TILES,)),
        ],
        compiler_params=PARAMS,
    )(*given)


def remap(data, level, frac):
    return pl.pallas_call(
        remap_kernel,
        out_shape=jax.ShapeDtypeStruct((GROUPS * DEPTH, LANES), F32),
        in_specs=[IN_VMEM] * 3,
        out_specs=IN_VMEM,
        compiler_params=PARAMS,
    )(data.reshape(GROUPS * DEPTH, LANES), level, frac).reshape(GROUPS, DEPTH, LANES)


def collect(part, data, result):
    given = (data,) if result is None else (data, result)
    return pl.pallas_call(
        functools.partial(collect_kernel, part),
        out_shape=jax.ShapeDtypeStruct((FIELDS, ROWS, LEVS, LONS), F32),
        in_specs=[IN_VMEM, ANYWHERE][: len(given)],
        out_specs=ANYWHERE,
        scratch_shapes=[
            pltpu.VMEM((FIELDS * 8 * STEP, LANES), F32),
            pltpu.SemaphoreType.DMA((2 * TILES,)),
        ],
        input_output_aliases={} if result is None else {1: 0},
        compiler_params=PARAMS,
    )(*given)


def exchange(data):
    return lax.all_to_all(data, "lev", split_axis=0, concat_axis=0, tiled=True)


def shards(tracers, thickness, courant_x, courant_y, level_index, level_offset, level_phase):
    rim = jax.ShapeDtypeStruct((NTR + 2, 2, LEVS, LONS), F32)
    south, north = pl.pallas_call(
        halo_kernel,
        out_shape=(rim, rim),
        in_specs=[ANYWHERE] * 3,
        out_specs=(IN_VMEM, IN_VMEM),
        scratch_shapes=[pltpu.SemaphoreType.DMA((2, 3))],
    )(tracers, thickness, courant_y)
    count = lax.axis_size("lat")
    low = lax.ppermute(north, "lat", [(i, i + 1) for i in range(count - 1)])
    high = lax.ppermute(south, "lat", [(i + 1, i) for i in range(count - 1)])
    own = (tracers, thickness, courant_x, courant_y)
    inner = exchange(transport(INNER, *own))
    lat = lax.axis_index("lat").astype(jnp.int32).reshape(1)
    outer = exchange(transport(OUTER, lat, *own, low, high))
    table = (2 * GROUPS * 16, LANES)
    tables = (jax.ShapeDtypeStruct(table, jnp.int32), jax.ShapeDtypeStruct(table, F32))
    places = pl.pallas_call(
        target_kernel,
        out_shape=tables + tables,
        in_specs=[IN_VMEM] * 3,
        out_specs=(IN_VMEM,) * 4,
        compiler_params=PARAMS,
    )(level_index, level_offset, level_phase)
    inner = exchange(remap(inner, *places[:2]))
    outer = exchange(remap(outer, *places[2:]))
    return collect(OUTER, outer, collect(INNER, inner, None))


def solution(mesh):
    in_specs = (
        P(None, "lat", "lev", None),
        P("lat", "lev", None),
        P("lat", "lev", None),
        P("lat", "lev", None),
        P(None, "lat", "lev"),
        P(None, "lat", "lev"),
        P(None, "lat", "lev"),
    )
    out_specs = P(None, "lat", "lev", None)
    return jax.shard_map(shards, mesh=mesh, in_specs=in_specs, out_specs=out_specs, check_vma=False)
```

```python
import functools

import jax
import jax.numpy as jnp
from jax import lax
from jax.experimental import pallas as pl
from jax.experimental.pallas import tpu as pltpu
from jax.sharding import PartitionSpec as P

F32 = jnp.float32
NTR = 9
FIELDS = NTR + 1
PAIRS = FIELDS // 2
ROWS = 16
LEVS = 2
LANES = 128
TILES = 9
LONS = LANES * TILES
CHUNK = 72
GROUPS = 16
STEP = TILES * LEVS
VMEM_LIMIT = 40 * 1024 * 1024

INNER, OUTER = 1, 2

REST = PAIRS * LEVS * 8
BLOCKS = (PAIRS + 3) // 4
DEPTH = REST + BLOCKS * 8

THICK, NORTH, EAST = NTR, NTR + 1, NTR + 2


def slots_of(part):
    return 8 + 4 * part


def lane_index():
    return lax.broadcasted_iota(jnp.int32, (8, LANES), 1)


def row_index():
    return lax.broadcasted_iota(jnp.int32, (8, LANES), 0)


def turn(x, shift, axis):
    shift = shift % x.shape[axis]
    return x if shift == 0 else pltpu.roll(x, shift, axis)


def west_of(tiles, lane):
    rolled = [turn(x, 1, 1) for x in tiles]
    return [jnp.where(lane == 0, rolled[c - 1], rolled[c]) for c in range(TILES)]


def east_of(tiles, lane):
    rolled = [turn(x, -1, 1) for x in tiles]
    return [jnp.where(lane == LANES - 1, rolled[(c + 1) % TILES], rolled[c]) for c in range(TILES)]


def span_of(group):
    return divmod(CHUNK * group, LANES)


def pick(x, where):
    return jnp.take_along_axis(x, where, axis=0, mode="promise_in_bounds")


def halo_kernel(tracers, thickness, courant_y, low, high, sem):
    copies = []
    for edge, (out, first) in enumerate(((low, 0), (high, ROWS - 2))):
        rows = pl.ds(first, 2)
        copies.append(pltpu.make_async_copy(tracers.at[:, rows], out.at[pl.ds(0, NTR)], sem.at[edge, 0]))
        copies.append(pltpu.make_async_copy(thickness.at[rows], out.at[THICK], sem.at[edge, 1]))
        copies.append(pltpu.make_async_copy(courant_y.at[rows], out.at[NORTH], sem.at[edge, 2]))
    for copy in copies:
        copy.start()
    for copy in copies:
        copy.wait()


def transport_kernel(part, *refs):
    if part == OUTER:
        lat, tracers, thickness, courant_x, courant_y, low, high, out, held, mx, ax, my, ay, fy, sem = refs
    else:
        tracers, thickness, courant_x, courant_y, _, out, held, mx, ax, my, ay, fy, sem = refs
    slots = slots_of(part)
    lane, row = lane_index(), row_index()
    view = held.reshape(NTR + 3, slots // part, part, TILES, LEVS, LANES)
    copies = []

    def bring(source, target):
        copies.append(pltpu.make_async_copy(source, target, sem.at[len(copies)]))

    for c in range(TILES):
        cut = pl.ds(LANES * c, LANES)
        runs = ((2, 12, 0, 0),) if part == INNER else ((0, 6, 2, 0), (10, 6, 0, 1))
        for first, size, at, run in runs:
            own, into = pl.ds(first, size), pl.ds(at, size)
            bring(tracers.at[:, own, :, cut], view.at[pl.ds(0, NTR), into, run, c])
            for array, source in ((THICK, thickness), (NORTH, courant_y), (EAST, courant_x)):
                bring(source.at[own, :, cut], view.at[array, into, run, c])
        if part == OUTER:
            bring(low.at[pl.ds(0, NTR + 1), :, :, cut], view.at[pl.ds(0, NTR + 1), pl.ds(0, 2), 0, c])
            bring(high.at[:, :, :, cut], view.at[pl.ds(0, NTR + 2), pl.ds(6, 2), 1, c])
    for copy in copies:
        copy.start()
    for g in range(GROUPS):
        out[g, pl.ds(REST, 8 * BLOCKS), :] = jnp.zeros((8 * BLOCKS, LANES), F32)
    for copy in copies:
        copy.wait()

    def rows_of(array, shift, c, l):
        start = (array * slots + (2 + shift) * part) * STEP + c * LEVS + l
        return held[pl.ds(start, 8, stride=STEP), :]

    def past(array, shift):
        return held[pl.ds((array * slots + 8 + (2 + shift) * part) * STEP, part * STEP), :]

    def place(l, c):
        return pl.ds((c * LEVS + l) * 8, 8)

    def faces(l, c, shift):
        return pl.ds((c * LEVS + l) * 16 + shift, 8)

    def keep_past(values):
        for run in range(part):
            fy[pl.ds(8 + run, STEP, stride=16), :] = values[run * STEP : (run + 1) * STEP]

    def factors(courant, before, after):
        mass = jnp.where(courant > 0, courant * before, courant * after)
        return mass, mass * jnp.where(courant > 0, 0.25 - 0.25 * courant, -0.25 - 0.25 * courant)

    for l in range(LEVS):
        thick = [rows_of(THICK, 0, c, l) for c in range(TILES)]
        west = west_of(thick, lane)
        for c in range(TILES):
            mx[place(l, c), :], ax[place(l, c), :] = factors(rows_of(EAST, 0, c, l), west[c], thick[c])
            courant = rows_of(NORTH, 0, c, l)
            if part == OUTER:
                courant = jnp.where((row > 0) | (lat[0] > 0), courant, 0.0)
            my[place(l, c), :], ay[place(l, c), :] = factors(courant, rows_of(THICK, -1, c, l), thick[c])
    past_mass, past_tilt = factors(past(NORTH, 0), past(THICK, -1), past(THICK, 0))

    def air():
        keep_past(past_mass)
        for l in range(LEVS):
            for c in range(TILES):
                fy[faces(l, c, 0), :] = my[place(l, c), :]
        tiles = []
        for l in range(LEVS):
            flux = [mx[place(l, c), :] for c in range(TILES)]
            flux_e = east_of(flux, lane)
            tiles.append(
                [
                    rows_of(THICK, 0, c, l) + (flux[c] - flux_e[c]) + (my[place(l, c), :] - fy[faces(l, c, part), :])
                    for c in range(TILES)
                ]
            )
        return tiles

    def tracer(array):
        past_q = [past(array, shift) for shift in (-2, -1, 0, 1)]
        up = past_mass > 0
        value = jnp.where(up, past_q[1], past_q[2])
        rise = jnp.where(up, past_q[2] - past_q[0], past_q[3] - past_q[1])
        keep_past(past_mass * value + past_tilt * rise)
        tiles = []
        for l in range(LEVS):
            q = [rows_of(array, 0, c, l) for c in range(TILES)]
            qw = west_of(q, lane)
            qe = east_of(q, lane)
            d = [qe[c] - qw[c] for c in range(TILES)]
            dw = west_of(d, lane)
            flux = []
            for c in range(TILES):
                mass = mx[place(l, c), :]
                up = mass > 0
                flux.append(mass * jnp.where(up, qw[c], q[c]) + ax[place(l, c), :] * jnp.where(up, dw[c], d[c]))
            flux_e = east_of(flux, lane)
            now = []
            for c in range(TILES):
                mass = my[place(l, c), :]
                up = mass > 0
                q2, q1, q3 = (rows_of(array, shift, c, l) for shift in (-2, -1, 1))
                value = jnp.where(up, q1, q[c])
                rise = jnp.where(up, q[c] - q2, q3 - q1)
                flux_y = mass * value + ay[place(l, c), :] * rise
                fy[faces(l, c, 0), :] = flux_y
                now.append(rows_of(THICK, 0, c, l) * q[c] + (flux[c] - flux_e[c]) + flux_y)
            tiles.append(now)
        return [[tiles[l][c] - fy[faces(l, c, part), :] for c in range(TILES)] for l in range(LEVS)]

    def two(pair, _):
        first = tracer(2 * pair)
        send_block(pair, first, tracer(2 * pair + 1))
        return 0

    def send_block(pair, first, second):
        block = REST
        for l in range(LEVS):
            slot = l * 4 + pair
            for g in range(GROUPS):
                pack(g, l, pl.multiple_of((pair * LEVS + l) * 8, 8), block, slot, first, second)

    def pack(g, l, at, block, slot, first, second):
        t, o = span_of(g)
        a = turn(first[l][t], -o, 1)
        b = turn(second[l][t], CHUNK - o, 1)
        if o + CHUNK > LANES:
            a = jnp.where(lane < LANES - o, a, turn(first[l][t + 1], -o, 1))
            lon = jnp.where(lane >= CHUNK, lane - CHUNK, lane + (LANES - CHUNK))
            b = jnp.where(lon < LANES - o, b, turn(second[l][t + 1], CHUNK - o, 1))
        out[g, pl.ds(at, 8), :] = jnp.where(lane < CHUNK, a, b)
        moved = pltpu.roll(b, slot * 16, 1)
        out[g, pl.ds(block, 8), :] = jnp.where((lane >> 4) == slot, moved, out[g, pl.ds(block, 8), :])

    lax.fori_loop(0, PAIRS - 1, two, 0)
    first, second = tracer(NTR - 1), air()
    for l in range(LEVS):
        for g in range(GROUPS):
            pack(g, l, ((PAIRS - 1) * LEVS + l) * 8, REST + 8, l * 4, first, second)


def target_kernel(index, offset, phase, *tables):
    lane, row = lane_index(), row_index()
    blank = jnp.zeros((8, LANES - CHUNK), F32)

    def rows_of(ref, n, part):
        if part == INNER:
            found = ref[n, pl.ds(4, 8), :]
            return jnp.concatenate([found, blank.astype(found.dtype)], 1)
        low, high = (jnp.concatenate([x, blank.astype(x.dtype)], 1) for x in (ref[n, pl.ds(0, 8), :], ref[n, pl.ds(8, 8), :]))
        return jnp.where((row & 1) == 0, pick(low, row >> 1), pick(high, 4 + (row >> 1)))

    for ref in tables:
        ref[pl.ds(0, 16), :] = jnp.zeros((16, LANES), ref.dtype)
    for n in range(2 * GROUPS - 1):
        for part in (INNER, OUTER):
            level, frac = tables[2 * part - 2 : 2 * part]
            s = rows_of(index, n, part)
            f = (rows_of(offset, n, part).astype(F32) + rows_of(phase, n, part)) * (1.0 / 32.0)
            for out, x in ((level, s), (frac, f)):
                moved = turn(x, CHUNK, 1)
                tail = jnp.where(lane < 16, moved, jnp.zeros_like(moved))
                tail = tail + turn(tail, 16, 1)
                tail = tail + turn(tail, 32, 1)
                other = turn(turn(tail, 64, 1), 4, 0)
                out[pl.ds((n + 1) * 16, 8), :] = jnp.where(lane < CHUNK, x, moved)
                out[pl.ds((n + 1) * 16 + 8, 8), :] = jnp.where(lane < 64, tail, other)


def remap_kernel(data, level, frac, out):
    lane, row = lane_index(), row_index()

    def targets(tile):
        found = []
        for parity in range(2):
            for half in range(2):
                start = (parity + 16 * half) * 16 + tile
                s = level[pl.ds(start, 8, stride=32), :]
                f = frac[pl.ds(start, 8, stride=32), :]
                square = f * f * 0.5
                cubic = 3.0 * square - f * f * f
                found.append(((s >> 1) & 7, s >= 16, (s & 1) == 1, f, square, cubic))
        return found

    def columns(even, odd, found):
        back = [turn(x, 1, 0) for x in odd]
        before = [jnp.where(row == 0, even[0], back[0]), jnp.where(row == 0, back[0], back[1])]
        left = [0.5 * (before[i] + even[i]) for i in range(2)]
        ahead = [turn(x, -1, 0) for x in left]
        right = [jnp.where(row == 7, ahead[1], ahead[0]), jnp.where(row == 7, odd[1], ahead[1])]
        pair = [even[i] + odd[i] for i in range(2)]
        run = list(pair)
        for shift in (1, 2, 4):
            run = [x + jnp.where(row >= shift, turn(x, shift, 0), 0.0) for x in run]
        half_sum = jnp.broadcast_to(run[0][7:8], (8, LANES))
        total = half_sum + run[1][7:8]
        below = [run[0] - pair[0], (run[1] - pair[1]) + half_sum]
        edges = []
        for where, high, is_odd, f, square, cubic in found:
            le, ri, ev, od, be = (
                jnp.where(high, pick(x[1], where), pick(x[0], where)) for x in (left, right, even, odd, below)
            )
            middle = 0.5 * (ev + od)
            lo = jnp.where(is_odd, middle, le)
            hi = jnp.where(is_odd, ri, middle)
            m = jnp.where(is_odd, od, ev)
            base = be + jnp.where(is_odd, ev, 0.0)
            edges.append(base + lo * f + (hi - lo) * square + ((m + m) - (lo + hi)) * cubic)
        ev0, ev1, od0, od1 = edges
        next0, next1 = turn(ev0, -1, 0), turn(ev1, -1, 0)
        new_even = [od0 - ev0, od1 - ev1]
        new_odd = [jnp.where(row == 7, next1, next0) - od0, jnp.where(row == 7, total, next1) - od1]
        return new_even, new_odd

    def span(start, half):
        return pl.ds(start + half * 8 * DEPTH, 8, stride=DEPTH)

    def main(tile, _):
        found = targets(tile)
        for pair in range(PAIRS):
            at = [(pair * LEVS + l) * 8 + tile for l in range(LEVS)]
            even, odd = ([data[span(at[l], half), :] for half in range(2)] for l in range(LEVS))
            new = columns(even, odd, found)
            for l in range(LEVS):
                for half in range(2):
                    out[span(at[l], half), :] = new[l][half]
        return 0

    lax.fori_loop(0, 8, main, 0)

    def tail(tile, _):
        found = targets(8 + tile)
        for block in range(BLOCKS):
            at = [REST + 8 * block + tile, REST + 8 * block + tile + 4]
            a, b = ([data[span(at[i], half), :] for half in range(2)] for i in range(2))
            even = [jnp.where(lane < 64, a[half], turn(b[half], 64, 1)) for half in range(2)]
            odd = [jnp.where(lane < 64, turn(a[half], 64, 1), b[half]) for half in range(2)]
            even, odd = columns(even, odd, found)
            for half in range(2):
                out[span(at[0], half), :] = jnp.where(lane < 64, even[half], turn(odd[half], 64, 1))
                out[span(at[1], half), :] = jnp.where(lane < 64, turn(even[half], 64, 1), odd[half])
        return 0

    lax.fori_loop(0, 4, tail, 0)


def collect_kernel(part, data, *refs):
    out, flat, sem = refs[-3:]
    lane = lane_index()

    def unpack(pair, at, block, slot):
        for l in range(LEVS):
            pieces = []
            for g in range(GROUPS):
                _, o = span_of(g)
                main = data[g, at(l), :]
                tail = pltpu.roll(data[g, pl.ds(block, 8), :], LANES - (l * 4 + slot) * 16, 1)
                mixed = jnp.where(lane < 16, tail, main)
                pieces.append((turn(main, o, 1), turn(mixed, o - CHUNK, 1)))
            for second in range(2):
                for c in range(TILES):
                    value = None
                    for g in range(GROUPS):
                        start = CHUNK * g - LANES * c
                        if start >= LANES or start + CHUNK <= 0:
                            continue
                        piece = pieces[g][second]
                        value = piece if value is None else jnp.where(lane >= start, piece, value)
                    flat[pl.ds((2 * pair + second) * 8 * STEP + c * LEVS + l, 8, stride=STEP), :] = value

    def one(pair, _):
        unpack(pair, lambda l: pl.ds(pl.multiple_of((pair * LEVS + l) * 8, 8), 8), REST, pair)
        return 0

    lax.fori_loop(0, PAIRS - 1, one, 0)
    unpack(PAIRS - 1, lambda l: pl.ds(((PAIRS - 1) * LEVS + l) * 8, 8), REST + 8, 0)
    view = flat.reshape(FIELDS, 8 // part, part, TILES, LEVS, LANES)
    copies = []
    for c in range(TILES):
        cut = pl.ds(LANES * c, LANES)
        for run, first in enumerate((4,) if part == INNER else (0, 12)):
            target = out.at[:, pl.ds(first, 8 // part), :, cut]
            copies.append(pltpu.make_async_copy(view.at[:, :, run, c], target, sem.at[len(copies)]))
    for copy in copies:
        copy.start()
    for copy in copies:
        copy.wait()


ANYWHERE = pl.BlockSpec(memory_space=pl.ANY)
IN_HBM = pl.BlockSpec(memory_space=pltpu.HBM)
IN_VMEM = pl.BlockSpec(memory_space=pltpu.VMEM)
PARAMS = pltpu.CompilerParams(vmem_limit_bytes=VMEM_LIMIT)


def transport(part, *given):
    factor = pltpu.VMEM((STEP * 8, LANES), F32)
    scalars = [pl.BlockSpec(memory_space=pltpu.SMEM)] if part == OUTER else []
    others = [ANYWHERE] * (len(given) - len(scalars) - 4)
    return pl.pallas_call(
        functools.partial(transport_kernel, part),
        out_shape=jax.ShapeDtypeStruct((GROUPS, DEPTH, LANES), F32),
        in_specs=scalars + [IN_HBM] * 4 + others,
        out_specs=IN_VMEM,
        scratch_shapes=[
            pltpu.VMEM(((NTR + 3) * slots_of(part) * STEP, LANES), F32),
            factor,
            factor,
            factor,
            factor,
            pltpu.VMEM((STEP * 16, LANES), F32),
            pltpu.SemaphoreType.DMA((10 * TILES,)),
        ],
        compiler_params=PARAMS,
    )(*given)


def remap(data, level, frac):
    return pl.pallas_call(
        remap_kernel,
        out_shape=jax.ShapeDtypeStruct((GROUPS * DEPTH, LANES), F32),
        in_specs=[IN_VMEM] * 3,
        out_specs=IN_VMEM,
        compiler_params=PARAMS,
    )(data.reshape(GROUPS * DEPTH, LANES), level, frac).reshape(GROUPS, DEPTH, LANES)


def collect(part, data, result):
    given = (data,) if result is None else (data, result)
    return pl.pallas_call(
        functools.partial(collect_kernel, part),
        out_shape=jax.ShapeDtypeStruct((FIELDS, ROWS, LEVS, LONS), F32),
        in_specs=[IN_VMEM, ANYWHERE][: len(given)],
        out_specs=ANYWHERE,
        scratch_shapes=[
            pltpu.VMEM((FIELDS * 8 * STEP, LANES), F32),
            pltpu.SemaphoreType.DMA((2 * TILES,)),
        ],
        input_output_aliases={} if result is None else {1: 0},
        compiler_params=PARAMS,
    )(*given)


def exchange(data):
    return lax.all_to_all(data, "lev", split_axis=0, concat_axis=0, tiled=True)


def shards(tracers, thickness, courant_x, courant_y, level_index, level_offset, level_phase):
    own = [pltpu.with_memory_space_constraint(x, pltpu.HBM) for x in (tracers, thickness, courant_x, courant_y)]
    rim = jax.ShapeDtypeStruct((NTR + 2, 2, LEVS, LONS), F32)
    south, north = pl.pallas_call(
        halo_kernel,
        out_shape=(rim, rim),
        in_specs=[IN_HBM] * 3,
        out_specs=(IN_VMEM, IN_VMEM),
        scratch_shapes=[pltpu.SemaphoreType.DMA((2, 3))],
    )(own[0], own[1], own[3])
    count = lax.axis_size("lat")
    low = lax.ppermute(north, "lat", [(i, i + 1) for i in range(count - 1)])
    high = lax.ppermute(south, "lat", [(i + 1, i) for i in range(count - 1)])
    inner = exchange(transport(INNER, *own, south))
    lat = lax.axis_index("lat").astype(jnp.int32).reshape(1)
    outer = exchange(transport(OUTER, lat, *own, low, high))
    table = (2 * GROUPS * 16, LANES)
    tables = (jax.ShapeDtypeStruct(table, jnp.int32), jax.ShapeDtypeStruct(table, F32))
    places = pl.pallas_call(
        target_kernel,
        out_shape=tables + tables,
        in_specs=[IN_VMEM] * 3,
        out_specs=(IN_VMEM,) * 4,
        compiler_params=PARAMS,
    )(level_index, level_offset, level_phase)
    inner = exchange(remap(inner, *places[:2]))
    outer = exchange(remap(outer, *places[2:]))
    return collect(OUTER, outer, collect(INNER, inner, None))


def solution(mesh):
    in_specs = (
        P(None, "lat", "lev", None),
        P("lat", "lev", None),
        P("lat", "lev", None),
        P("lat", "lev", None),
        P(None, "lat", "lev"),
        P(None, "lat", "lev"),
        P(None, "lat", "lev"),
    )
    out_specs = P(None, "lat", "lev", None)
    return jax.shard_map(shards, mesh=mesh, in_specs=in_specs, out_specs=out_specs, check_vma=False)
```

```python
import functools

import jax
import jax.numpy as jnp
from jax import lax
from jax.experimental import pallas as pl
from jax.experimental.pallas import tpu as pltpu
from jax.sharding import PartitionSpec as P

F32 = jnp.float32
NTR = 9
FIELDS = NTR + 1
PAIRS = FIELDS // 2
ROWS = 16
LEVS = 2
LANES = 128
TILES = 9
LONS = LANES * TILES
CHUNK = 72
GROUPS = 16
STEP = TILES * LEVS
VMEM_LIMIT = 40 * 1024 * 1024

INNER, OUTER = 1, 2

REST = PAIRS * LEVS * 8
BLOCKS = (PAIRS + 3) // 4
DEPTH = REST + BLOCKS * 8

THICK, NORTH, EAST = NTR, NTR + 1, NTR + 2


def slots_of(part):
    return 8 + 4 * part


def lane_index():
    return lax.broadcasted_iota(jnp.int32, (8, LANES), 1)


def row_index():
    return lax.broadcasted_iota(jnp.int32, (8, LANES), 0)


def turn(x, shift, axis):
    shift = shift % x.shape[axis]
    return x if shift == 0 else pltpu.roll(x, shift, axis)


def west_of(tiles, lane):
    rolled = [turn(x, 1, 1) for x in tiles]
    return [jnp.where(lane == 0, rolled[c - 1], rolled[c]) for c in range(TILES)]


def east_of(tiles, lane):
    rolled = [turn(x, -1, 1) for x in tiles]
    return [jnp.where(lane == LANES - 1, rolled[(c + 1) % TILES], rolled[c]) for c in range(TILES)]


def span_of(group):
    return divmod(CHUNK * group, LANES)


def pick(x, where):
    return jnp.take_along_axis(x, where, axis=0, mode="promise_in_bounds")


def halo_kernel(tracers, thickness, courant_y, low, high, sem):
    copies = []
    for edge, (out, first) in enumerate(((low, 0), (high, ROWS - 2))):
        rows = pl.ds(first, 2)
        copies.append(pltpu.make_async_copy(tracers.at[:, rows], out.at[pl.ds(0, NTR)], sem.at[edge, 0]))
        copies.append(pltpu.make_async_copy(thickness.at[rows], out.at[THICK], sem.at[edge, 1]))
        copies.append(pltpu.make_async_copy(courant_y.at[rows], out.at[NORTH], sem.at[edge, 2]))
    for copy in copies:
        copy.start()
    for copy in copies:
        copy.wait()


def transport_kernel(part, *refs):
    if part == OUTER:
        where, tracers, thickness, courant_x, courant_y, low, high, _, out, held, mx, ax, my, ay, fy, sem = refs
    else:
        tracers, thickness, courant_x, courant_y, _, out, held, mx, ax, my, ay, fy, sem = refs
    chunk = list(range(GROUPS))
    if part == OUTER:
        y, z = where[1] >> 2, where[1] & 3
        chunk = [4 * ((g & 3) ^ z) + (((g >> 2) - y) & 3) for g in range(GROUPS)]
    slots = slots_of(part)
    lane, row = lane_index(), row_index()
    view = held.reshape(NTR + 3, slots // part, part, TILES, LEVS, LANES)
    copies = []

    def bring(source, target):
        copies.append(pltpu.make_async_copy(source, target, sem.at[len(copies)]))

    for c in range(TILES):
        cut = pl.ds(LANES * c, LANES)
        runs = ((2, 12, 0, 0),) if part == INNER else ((0, 6, 2, 0), (10, 6, 0, 1))
        for first, size, at, run in runs:
            own, into = pl.ds(first, size), pl.ds(at, size)
            bring(tracers.at[:, own, :, cut], view.at[pl.ds(0, NTR), into, run, c])
            for array, source in ((THICK, thickness), (NORTH, courant_y), (EAST, courant_x)):
                bring(source.at[own, :, cut], view.at[array, into, run, c])
        if part == OUTER:
            bring(low.at[pl.ds(0, NTR + 1), :, :, cut], view.at[pl.ds(0, NTR + 1), pl.ds(0, 2), 0, c])
            bring(high.at[:, :, :, cut], view.at[pl.ds(0, NTR + 2), pl.ds(6, 2), 1, c])
    for copy in copies:
        copy.start()
    for g in range(GROUPS):
        out[g, pl.ds(REST, 8 * BLOCKS), :] = jnp.zeros((8 * BLOCKS, LANES), F32)
    for copy in copies:
        copy.wait()

    def rows_of(array, shift, c, l):
        start = (array * slots + (2 + shift) * part) * STEP + c * LEVS + l
        return held[pl.ds(start, 8, stride=STEP), :]

    def past(array, shift):
        return held[pl.ds((array * slots + 8 + (2 + shift) * part) * STEP, part * STEP), :]

    def place(l, c):
        return pl.ds((c * LEVS + l) * 8, 8)

    def faces(l, c, shift):
        return pl.ds((c * LEVS + l) * 16 + shift, 8)

    def keep_past(values):
        for run in range(part):
            fy[pl.ds(8 + run, STEP, stride=16), :] = values[run * STEP : (run + 1) * STEP]

    def factors(courant, before, after):
        mass = jnp.where(courant > 0, courant * before, courant * after)
        return mass, mass * jnp.where(courant > 0, 0.25 - 0.25 * courant, -0.25 - 0.25 * courant)

    for l in range(LEVS):
        thick = [rows_of(THICK, 0, c, l) for c in range(TILES)]
        west = west_of(thick, lane)
        for c in range(TILES):
            mx[place(l, c), :], ax[place(l, c), :] = factors(rows_of(EAST, 0, c, l), west[c], thick[c])
            courant = rows_of(NORTH, 0, c, l)
            if part == OUTER:
                courant = jnp.where((row > 0) | (where[0] > 0), courant, 0.0)
            my[place(l, c), :], ay[place(l, c), :] = factors(courant, rows_of(THICK, -1, c, l), thick[c])
    past_mass, past_tilt = factors(past(NORTH, 0), past(THICK, -1), past(THICK, 0))

    def air():
        keep_past(past_mass)
        for l in range(LEVS):
            for c in range(TILES):
                fy[faces(l, c, 0), :] = my[place(l, c), :]
        tiles = []
        for l in range(LEVS):
            flux = [mx[place(l, c), :] for c in range(TILES)]
            flux_e = east_of(flux, lane)
            tiles.append(
                [
                    rows_of(THICK, 0, c, l) + (flux[c] - flux_e[c]) + (my[place(l, c), :] - fy[faces(l, c, part), :])
                    for c in range(TILES)
                ]
            )
        return tiles

    def tracer(array):
        past_q = [past(array, shift) for shift in (-2, -1, 0, 1)]
        up = past_mass > 0
        value = jnp.where(up, past_q[1], past_q[2])
        rise = jnp.where(up, past_q[2] - past_q[0], past_q[3] - past_q[1])
        keep_past(past_mass * value + past_tilt * rise)
        tiles = []
        for l in range(LEVS):
            q = [rows_of(array, 0, c, l) for c in range(TILES)]
            qw = west_of(q, lane)
            qe = east_of(q, lane)
            d = [qe[c] - qw[c] for c in range(TILES)]
            dw = west_of(d, lane)
            flux = []
            for c in range(TILES):
                mass = mx[place(l, c), :]
                up = mass > 0
                flux.append(mass * jnp.where(up, qw[c], q[c]) + ax[place(l, c), :] * jnp.where(up, dw[c], d[c]))
            flux_e = east_of(flux, lane)
            now = []
            for c in range(TILES):
                mass = my[place(l, c), :]
                up = mass > 0
                q2, q1, q3 = (rows_of(array, shift, c, l) for shift in (-2, -1, 1))
                value = jnp.where(up, q1, q[c])
                rise = jnp.where(up, q[c] - q2, q3 - q1)
                flux_y = mass * value + ay[place(l, c), :] * rise
                fy[faces(l, c, 0), :] = flux_y
                now.append(rows_of(THICK, 0, c, l) * q[c] + (flux[c] - flux_e[c]) + flux_y)
            tiles.append(now)
        return [[tiles[l][c] - fy[faces(l, c, part), :] for c in range(TILES)] for l in range(LEVS)]

    def two(pair, _):
        first = tracer(2 * pair)
        send_block(pair, first, tracer(2 * pair + 1))
        return 0

    def send_block(pair, first, second):
        block = REST
        for l in range(LEVS):
            slot = l * 4 + pair
            for g in range(GROUPS):
                pack(g, l, pl.multiple_of((pair * LEVS + l) * 8, 8), block, slot, first, second)

    def pack(g, l, at, block, slot, first, second):
        t, o = span_of(g)
        a = turn(first[l][t], -o, 1)
        b = turn(second[l][t], CHUNK - o, 1)
        if o + CHUNK > LANES:
            a = jnp.where(lane < LANES - o, a, turn(first[l][t + 1], -o, 1))
            lon = jnp.where(lane >= CHUNK, lane - CHUNK, lane + (LANES - CHUNK))
            b = jnp.where(lon < LANES - o, b, turn(second[l][t + 1], CHUNK - o, 1))
        out[chunk[g], pl.ds(at, 8), :] = jnp.where(lane < CHUNK, a, b)
        moved = pltpu.roll(b, slot * 16, 1)
        last = pl.ds(block, 8)
        out[chunk[g], last, :] = jnp.where((lane >> 4) == slot, moved, out[chunk[g], last, :])

    lax.fori_loop(0, PAIRS - 1, two, 0)
    first, second = tracer(NTR - 1), air()
    for l in range(LEVS):
        for g in range(GROUPS):
            pack(g, l, ((PAIRS - 1) * LEVS + l) * 8, REST + 8, l * 4, first, second)


def target_kernel(index, offset, phase, inner, outer):
    lane = lane_index()
    blank = jnp.zeros((8, LANES - CHUNK), F32)
    for ref in (inner, outer):
        ref[pl.ds(0, 16), :] = jnp.zeros((16, LANES), F32)
    for n in range(2 * GROUPS - 1):
        at = (n + 1) * 16
        main, tail = [], []
        for h in range(2):
            rows = pl.ds(8 * h, 8)
            part = (offset[n, rows, :].astype(F32) + phase[n, rows, :]) * (1.0 / 32.0)
            x = jnp.concatenate([index[n, rows, :].astype(F32) + part, blank], 1)
            moved = turn(x, CHUNK, 1)
            main.append(jnp.where(lane < CHUNK, x, moved))
            last = jnp.where(lane < 16, moved, 0.0)
            last = last + turn(last, 16, 1)
            tail.append(last + turn(last, 32, 1))
        other = [turn(x, 64, 1) for x in tail]
        inner[pl.ds(at, 4), :] = main[0][4:]
        inner[pl.ds(at + 4, 4), :] = main[1][:4]
        inner[pl.ds(at + 8, 8), :] = turn(tail[0], 4, 0) + other[1]
        outer[pl.ds(at, 4, stride=2), :] = main[0][:4]
        outer[pl.ds(at + 1, 4, stride=2), :] = main[1][4:]
        outer[pl.ds(at + 8, 2, stride=2), :] = (tail[0] + turn(other[0], -2, 0))[:2]
        outer[pl.ds(at + 9, 2, stride=2), :] = (tail[1] + turn(other[1], -2, 0))[4:6]


def remap_rows(data, table, out):
    lane, row = lane_index(), row_index()

    def targets(tile):
        found = []
        for parity in range(2):
            for half in range(2):
                start = (parity + 16 * half) * 16 + tile
                position = table[pl.ds(start, 8, stride=32), :]
                s = jnp.minimum(position.astype(jnp.int32), 2 * GROUPS - 1)
                f = position - s.astype(F32)
                square = f * f * 0.5
                cubic = 3.0 * square - f * f * f
                found.append(((s >> 1) & 7, s >= 16, (s & 1) == 1, f, square, cubic))
        return found

    def columns(even, odd, found):
        back = [turn(x, 1, 0) for x in odd]
        before = [jnp.where(row == 0, even[0], back[0]), jnp.where(row == 0, back[0], back[1])]
        left = [0.5 * (before[i] + even[i]) for i in range(2)]
        ahead = [turn(x, -1, 0) for x in left]
        right = [jnp.where(row == 7, ahead[1], ahead[0]), jnp.where(row == 7, odd[1], ahead[1])]
        pair = [even[i] + odd[i] for i in range(2)]
        run = list(pair)
        for shift in (1, 2, 4):
            run = [x + jnp.where(row >= shift, turn(x, shift, 0), 0.0) for x in run]
        half_sum = jnp.broadcast_to(run[0][7:8], (8, LANES))
        total = half_sum + run[1][7:8]
        below = [run[0] - pair[0], (run[1] - pair[1]) + half_sum]
        edges = []
        for where, high, is_odd, f, square, cubic in found:
            le, ri, ev, od, be = (
                jnp.where(high, pick(x[1], where), pick(x[0], where)) for x in (left, right, even, odd, below)
            )
            middle = 0.5 * (ev + od)
            lo = jnp.where(is_odd, middle, le)
            hi = jnp.where(is_odd, ri, middle)
            m = jnp.where(is_odd, od, ev)
            base = be + jnp.where(is_odd, ev, 0.0)
            edges.append(base + lo * f + (hi - lo) * square + ((m + m) - (lo + hi)) * cubic)
        ev0, ev1, od0, od1 = edges
        next0, next1 = turn(ev0, -1, 0), turn(ev1, -1, 0)
        new_even = [od0 - ev0, od1 - ev1]
        new_odd = [jnp.where(row == 7, next1, next0) - od0, jnp.where(row == 7, total, next1) - od1]
        return new_even, new_odd

    def span(start, half):
        return pl.ds(start + half * 8 * DEPTH, 8, stride=DEPTH)

    def main(tile, _):
        found = targets(tile)
        for pair in range(PAIRS):
            at = [(pair * LEVS + l) * 8 + tile for l in range(LEVS)]
            even, odd = ([data[span(at[l], half), :] for half in range(2)] for l in range(LEVS))
            new = columns(even, odd, found)
            for l in range(LEVS):
                for half in range(2):
                    out[span(at[l], half), :] = new[l][half]
        return 0

    lax.fori_loop(0, 8, main, 0)

    def tail(tile, _):
        found = targets(8 + tile)
        for block in range(BLOCKS):
            at = [REST + 8 * block + tile, REST + 8 * block + tile + 4]
            a, b = ([data[span(at[i], half), :] for half in range(2)] for i in range(2))
            even = [jnp.where(lane < 64, a[half], turn(b[half], 64, 1)) for half in range(2)]
            odd = [jnp.where(lane < 64, turn(a[half], 64, 1), b[half]) for half in range(2)]
            even, odd = columns(even, odd, found)
            for half in range(2):
                out[span(at[0], half), :] = jnp.where(lane < 64, even[half], turn(odd[half], 64, 1))
                out[span(at[1], half), :] = jnp.where(lane < 64, turn(even[half], 64, 1), odd[half])
        return 0

    lax.fori_loop(0, 4, tail, 0)


def places_of(where):
    y, z = where[1] >> 2, where[1] & 3
    return [[((y - j) & 3) * 4 + (z ^ k) for k in range(4)] for j in range(4)]


def gather_chunks(where, sources, target, sem):
    copies = []
    for j, found in enumerate(places_of(where)):
        for k, place in enumerate(found):
            copies.append(pltpu.make_async_copy(sources[j][k], target(place), sem.at[4 * j + k]))
    for copy in copies:
        copy.start()
    for copy in copies:
        copy.wait()


def remap_outer_kernel(where, *refs):
    given, (table, out, data, new, sem) = refs[:4], refs[4:]

    def rows(place):
        return pl.ds(pl.multiple_of(place * DEPTH, 8), DEPTH)

    gather_chunks(where, [[given[j].at[k] for k in range(4)] for j in range(4)], lambda p: data.at[rows(p)], sem)
    remap_rows(data, table, new)
    y, z = where[1] >> 2, where[1] & 3
    copies = []
    for j in range(4):
        for k in range(4):
            place = ((y + j) & 3) * 4 + (z ^ k)
            copies.append(pltpu.make_async_copy(new.at[rows(place)], out.at[4 * j + k], sem.at[4 * j + k]))
    for copy in copies:
        copy.start()
    for copy in copies:
        copy.wait()


def collect_kernel(part, *refs):
    if part == INNER:
        data, out, flat, sem = refs
    else:
        where, given, (_, out, data, flat, sem) = refs[0], refs[1:5], refs[5:]
        gather_chunks(where, [[given[k].at[j] for k in range(4)] for j in range(4)], lambda p: data.at[p], sem)
    lane = lane_index()

    def unpack(pair, at, block, slot):
        for l in range(LEVS):
            pieces = []
            for g in range(GROUPS):
                _, o = span_of(g)
                main = data[g, at(l), :]
                tail = pltpu.roll(data[g, pl.ds(block, 8), :], LANES - (l * 4 + slot) * 16, 1)
                mixed = jnp.where(lane < 16, tail, main)
                pieces.append((turn(main, o, 1), turn(mixed, o - CHUNK, 1)))
            for second in range(2):
                for c in range(TILES):
                    value = None
                    for g in range(GROUPS):
                        start = CHUNK * g - LANES * c
                        if start >= LANES or start + CHUNK <= 0:
                            continue
                        piece = pieces[g][second]
                        value = piece if value is None else jnp.where(lane >= start, piece, value)
                    flat[pl.ds((2 * pair + second) * 8 * STEP + c * LEVS + l, 8, stride=STEP), :] = value

    def one(pair, _):
        unpack(pair, lambda l: pl.ds(pl.multiple_of((pair * LEVS + l) * 8, 8), 8), REST, pair)
        return 0

    lax.fori_loop(0, PAIRS - 1, one, 0)
    unpack(PAIRS - 1, lambda l: pl.ds(((PAIRS - 1) * LEVS + l) * 8, 8), REST + 8, 0)
    view = flat.reshape(FIELDS, 8 // part, part, TILES, LEVS, LANES)
    copies = []
    for c in range(TILES):
        cut = pl.ds(LANES * c, LANES)
        for run, first in enumerate((4,) if part == INNER else (0, 12)):
            target = out.at[:, pl.ds(first, 8 // part), :, cut]
            copies.append(pltpu.make_async_copy(view.at[:, :, run, c], target, sem.at[len(copies)]))
    for copy in copies:
        copy.start()
    for copy in copies:
        copy.wait()


ANYWHERE = pl.BlockSpec(memory_space=pl.ANY)
IN_SMEM = pl.BlockSpec(memory_space=pltpu.SMEM)
IN_HBM = pl.BlockSpec(memory_space=pltpu.HBM)
IN_VMEM = pl.BlockSpec(memory_space=pltpu.VMEM)
PARAMS = pltpu.CompilerParams(vmem_limit_bytes=VMEM_LIMIT)


def transport(part, *given):
    factor = pltpu.VMEM((STEP * 8, LANES), F32)
    scalars = [IN_SMEM] if part == OUTER else []
    others = [ANYWHERE] * (len(given) - len(scalars) - 4)
    return pl.pallas_call(
        functools.partial(transport_kernel, part),
        out_shape=jax.ShapeDtypeStruct((GROUPS, DEPTH, LANES), F32),
        in_specs=scalars + [IN_HBM] * 4 + others,
        out_specs=IN_VMEM,
        scratch_shapes=[
            pltpu.VMEM(((NTR + 3) * slots_of(part) * STEP, LANES), F32),
            factor,
            factor,
            factor,
            factor,
            pltpu.VMEM((STEP * 16, LANES), F32),
            pltpu.SemaphoreType.DMA((10 * TILES,)),
        ],
        compiler_params=PARAMS,
    )(*given)


def remap_inner(data, table):
    return pl.pallas_call(
        remap_rows,
        out_shape=jax.ShapeDtypeStruct((GROUPS * DEPTH, LANES), F32),
        in_specs=[IN_VMEM] * 2,
        out_specs=IN_VMEM,
        compiler_params=PARAMS,
    )(data.reshape(GROUPS * DEPTH, LANES), table).reshape(GROUPS, DEPTH, LANES)


def remap_outer(where, given, table):
    held = pltpu.VMEM((GROUPS * DEPTH, LANES), F32)
    return pl.pallas_call(
        remap_outer_kernel,
        out_shape=jax.ShapeDtypeStruct((GROUPS, DEPTH, LANES), F32),
        in_specs=[IN_SMEM] + [ANYWHERE] * 4 + [IN_VMEM],
        out_specs=ANYWHERE,
        scratch_shapes=[held, held, pltpu.SemaphoreType.DMA((GROUPS,))],
        compiler_params=PARAMS,
    )(where, *given, table)


def collect(part, *given):
    scratch = [pltpu.VMEM((FIELDS * 8 * STEP, LANES), F32), pltpu.SemaphoreType.DMA((2 * TILES,))]
    if part == OUTER:
        scratch = [pltpu.VMEM((GROUPS, DEPTH, LANES), F32)] + scratch
    return pl.pallas_call(
        functools.partial(collect_kernel, part),
        out_shape=jax.ShapeDtypeStruct((FIELDS, ROWS, LEVS, LONS), F32),
        in_specs=[IN_VMEM] if part == INNER else [IN_SMEM] + [ANYWHERE] * 5,
        out_specs=ANYWHERE,
        scratch_shapes=scratch,
        input_output_aliases={} if part == INNER else {5: 0},
        compiler_params=PARAMS,
    )(*given)


def exchange(data):
    return lax.all_to_all(data, "lev", split_axis=0, concat_axis=0, tiled=True)


def over_z(data, k):
    return lax.ppermute(data, "lev", [(i, i ^ k) for i in range(GROUPS)])


def over_y(data, j):
    return lax.ppermute(data, "lev", [(i, (i + 4 * j) % GROUPS) for i in range(GROUPS)])


def exchange_out(data):
    part = [data[4 * k : 4 * k + 4] for k in range(4)]
    for k in (2, 3, 1):
        part[k] = over_z(part[k], k)
    turned = [jnp.stack([part[k][j] for k in range(4)]) for j in range(4)]
    return [turned[0]] + [over_y(turned[j], j) for j in range(1, 4)]


def exchange_back(data):
    part = [data[4 * j : 4 * j + 4] for j in range(4)]
    for j in range(1, 4):
        part[j] = over_y(part[j], j)
    turned = [jnp.stack([part[j][k] for j in range(4)]) for k in range(4)]
    for k in (2, 3, 1):
        turned[k] = over_z(turned[k], k)
    return turned


def shards(tracers, thickness, courant_x, courant_y, level_index, level_offset, level_phase):
    own = [pltpu.with_memory_space_constraint(x, pltpu.HBM) for x in (tracers, thickness, courant_x, courant_y)]
    where = jnp.stack([lax.axis_index("lat"), lax.axis_index("lev")]).astype(jnp.int32)
    rim = jax.ShapeDtypeStruct((NTR + 2, 2, LEVS, LONS), F32)
    south, north = pl.pallas_call(
        halo_kernel,
        out_shape=(rim, rim),
        in_specs=[IN_HBM] * 3,
        out_specs=(IN_VMEM, IN_VMEM),
        scratch_shapes=[pltpu.SemaphoreType.DMA((2, 3))],
    )(own[0], own[1], own[3])
    count = lax.axis_size("lat")
    low = lax.ppermute(north, "lat", [(i, i + 1) for i in range(count - 1)])
    high = lax.ppermute(south, "lat", [(i + 1, i) for i in range(count - 1)])
    inner = exchange(transport(INNER, *own, south))
    table = jax.ShapeDtypeStruct((2 * GROUPS * 16, LANES), F32)
    inner_table, outer_table = pl.pallas_call(
        target_kernel,
        out_shape=(table, table),
        in_specs=[IN_VMEM] * 3,
        out_specs=(IN_VMEM, IN_VMEM),
        compiler_params=PARAMS,
    )(level_index, level_offset, level_phase)
    outer = exchange_out(transport(OUTER, where, *own, low, high, outer_table))
    inner = exchange(remap_inner(inner, inner_table))
    outer = exchange_back(remap_outer(where, outer, outer_table))
    return collect(OUTER, where, *outer, collect(INNER, inner))


def solution(mesh):
    in_specs = (
        P(None, "lat", "lev", None),
        P("lat", "lev", None),
        P("lat", "lev", None),
        P("lat", "lev", None),
        P(None, "lat", "lev"),
        P(None, "lat", "lev"),
        P(None, "lat", "lev"),
    )
    out_specs = P(None, "lat", "lev", None)
    return jax.shard_map(shards, mesh=mesh, in_specs=in_specs, out_specs=out_specs, check_vma=False)
```

```python
import functools

import jax
import jax.numpy as jnp
from jax import lax
from jax.experimental import pallas as pl
from jax.experimental.pallas import tpu as pltpu
from jax.sharding import PartitionSpec as P

F32 = jnp.float32
NTR = 9
FIELDS = NTR + 1
PAIRS = FIELDS // 2
ROWS = 16
LEVS = 2
LANES = 128
TILES = 9
LONS = LANES * TILES
CHUNK = 72
GROUPS = 16
STEP = TILES * LEVS
VMEM_LIMIT = 40 * 1024 * 1024

INNER, OUTER = 1, 2

REST = PAIRS * LEVS * 8
BLOCKS = (PAIRS + 3) // 4
DEPTH = REST + BLOCKS * 8

THICK, NORTH, EAST = NTR, NTR + 1, NTR + 2


def slots_of(part):
    return 8 + 4 * part


def lane_index():
    return lax.broadcasted_iota(jnp.int32, (8, LANES), 1)


def row_index():
    return lax.broadcasted_iota(jnp.int32, (8, LANES), 0)


def turn(x, shift, axis):
    shift = shift % x.shape[axis]
    return x if shift == 0 else pltpu.roll(x, shift, axis)


def west_of(tiles, lane):
    rolled = [turn(x, 1, 1) for x in tiles]
    return [jnp.where(lane == 0, rolled[c - 1], rolled[c]) for c in range(TILES)]


def east_of(tiles, lane):
    rolled = [turn(x, -1, 1) for x in tiles]
    return [jnp.where(lane == LANES - 1, rolled[(c + 1) % TILES], rolled[c]) for c in range(TILES)]


def span_of(group):
    return divmod(CHUNK * group, LANES)


def pick(x, where):
    return jnp.take_along_axis(x, where, axis=0, mode="promise_in_bounds")


def halo_kernel(tracers, thickness, courant_y, low, high, sem):
    copies = []
    for edge, (out, first) in enumerate(((low, 0), (high, ROWS - 2))):
        rows = pl.ds(first, 2)
        copies.append(pltpu.make_async_copy(tracers.at[:, rows], out.at[pl.ds(0, NTR)], sem.at[edge, 0]))
        copies.append(pltpu.make_async_copy(thickness.at[rows], out.at[THICK], sem.at[edge, 1]))
        copies.append(pltpu.make_async_copy(courant_y.at[rows], out.at[NORTH], sem.at[edge, 2]))
    for copy in copies:
        copy.start()
    for copy in copies:
        copy.wait()


def transport_kernel(part, *refs):
    if part == OUTER:
        tracers, thickness, courant_x, courant_y, low, high, _, out, held, mx, ax, my, ay, fy, sem = refs
    else:
        tracers, thickness, courant_x, courant_y, _, out, held, mx, ax, my, ay, fy, sem = refs
    chunk = slots_to()
    slots = slots_of(part)
    lane, row = lane_index(), row_index()
    view = held.reshape(NTR + 3, slots // part, part, TILES, LEVS, LANES)
    copies = []

    def bring(source, target):
        copies.append(pltpu.make_async_copy(source, target, sem.at[len(copies)]))

    for c in range(TILES):
        cut = pl.ds(LANES * c, LANES)
        runs = ((2, 12, 0, 0),) if part == INNER else ((0, 6, 2, 0), (10, 6, 0, 1))
        for first, size, at, run in runs:
            own, into = pl.ds(first, size), pl.ds(at, size)
            bring(tracers.at[:, own, :, cut], view.at[pl.ds(0, NTR), into, run, c])
            for array, source in ((THICK, thickness), (NORTH, courant_y), (EAST, courant_x)):
                bring(source.at[own, :, cut], view.at[array, into, run, c])
        if part == OUTER:
            bring(low.at[pl.ds(0, NTR + 1), :, :, cut], view.at[pl.ds(0, NTR + 1), pl.ds(0, 2), 0, c])
            bring(high.at[:, :, :, cut], view.at[pl.ds(0, NTR + 2), pl.ds(6, 2), 1, c])
    for copy in copies:
        copy.start()
    for g in range(GROUPS):
        out[g, pl.ds(REST, 8 * BLOCKS), :] = jnp.zeros((8 * BLOCKS, LANES), F32)
    for copy in copies:
        copy.wait()

    def rows_of(array, shift, c, l):
        start = (array * slots + (2 + shift) * part) * STEP + c * LEVS + l
        return held[pl.ds(start, 8, stride=STEP), :]

    def past(array, shift):
        return held[pl.ds((array * slots + 8 + (2 + shift) * part) * STEP, part * STEP), :]

    def place(l, c):
        return pl.ds((c * LEVS + l) * 8, 8)

    def faces(l, c, shift):
        return pl.ds((c * LEVS + l) * 16 + shift, 8)

    def keep_past(values):
        for run in range(part):
            fy[pl.ds(8 + run, STEP, stride=16), :] = values[run * STEP : (run + 1) * STEP]

    def factors(courant, before, after):
        mass = jnp.where(courant > 0, courant * before, courant * after)
        return mass, mass * jnp.where(courant > 0, 0.25 - 0.25 * courant, -0.25 - 0.25 * courant)

    for l in range(LEVS):
        thick = [rows_of(THICK, 0, c, l) for c in range(TILES)]
        west = west_of(thick, lane)
        for c in range(TILES):
            mx[place(l, c), :], ax[place(l, c), :] = factors(rows_of(EAST, 0, c, l), west[c], thick[c])
            courant = rows_of(NORTH, 0, c, l)
            if part == OUTER:
                courant = jnp.where((row > 0) | (lax.axis_index("lat") > 0), courant, 0.0)
            my[place(l, c), :], ay[place(l, c), :] = factors(courant, rows_of(THICK, -1, c, l), thick[c])
    past_mass, past_tilt = factors(past(NORTH, 0), past(THICK, -1), past(THICK, 0))

    def air():
        keep_past(past_mass)
        for l in range(LEVS):
            for c in range(TILES):
                fy[faces(l, c, 0), :] = my[place(l, c), :]
        tiles = []
        for l in range(LEVS):
            flux = [mx[place(l, c), :] for c in range(TILES)]
            flux_e = east_of(flux, lane)
            tiles.append(
                [
                    rows_of(THICK, 0, c, l) + (flux[c] - flux_e[c]) + (my[place(l, c), :] - fy[faces(l, c, part), :])
                    for c in range(TILES)
                ]
            )
        return tiles

    def tracer(array):
        past_q = [past(array, shift) for shift in (-2, -1, 0, 1)]
        up = past_mass > 0
        value = jnp.where(up, past_q[1], past_q[2])
        rise = jnp.where(up, past_q[2] - past_q[0], past_q[3] - past_q[1])
        keep_past(past_mass * value + past_tilt * rise)
        tiles = []
        for l in range(LEVS):
            q = [rows_of(array, 0, c, l) for c in range(TILES)]
            qw = west_of(q, lane)
            qe = east_of(q, lane)
            d = [qe[c] - qw[c] for c in range(TILES)]
            dw = west_of(d, lane)
            flux = []
            for c in range(TILES):
                mass = mx[place(l, c), :]
                up = mass > 0
                flux.append(mass * jnp.where(up, qw[c], q[c]) + ax[place(l, c), :] * jnp.where(up, dw[c], d[c]))
            flux_e = east_of(flux, lane)
            now = []
            for c in range(TILES):
                mass = my[place(l, c), :]
                up = mass > 0
                q2, q1, q3 = (rows_of(array, shift, c, l) for shift in (-2, -1, 1))
                value = jnp.where(up, q1, q[c])
                rise = jnp.where(up, q[c] - q2, q3 - q1)
                flux_y = mass * value + ay[place(l, c), :] * rise
                fy[faces(l, c, 0), :] = flux_y
                now.append(rows_of(THICK, 0, c, l) * q[c] + (flux[c] - flux_e[c]) + flux_y)
            tiles.append(now)
        return [[tiles[l][c] - fy[faces(l, c, part), :] for c in range(TILES)] for l in range(LEVS)]

    def two(pair, _):
        first = tracer(2 * pair)
        send_block(pair, first, tracer(2 * pair + 1))
        return 0

    def send_block(pair, first, second):
        block = REST
        for l in range(LEVS):
            slot = l * 4 + pair
            for g in range(GROUPS):
                pack(g, l, pl.multiple_of((pair * LEVS + l) * 8, 8), block, slot, first, second)

    def pack(g, l, at, block, slot, first, second):
        t, o = span_of(g)
        a = turn(first[l][t], -o, 1)
        b = turn(second[l][t], CHUNK - o, 1)
        if o + CHUNK > LANES:
            a = jnp.where(lane < LANES - o, a, turn(first[l][t + 1], -o, 1))
            lon = jnp.where(lane >= CHUNK, lane - CHUNK, lane + (LANES - CHUNK))
            b = jnp.where(lon < LANES - o, b, turn(second[l][t + 1], CHUNK - o, 1))
        out[chunk[g], pl.ds(at, 8), :] = jnp.where(lane < CHUNK, a, b)
        moved = pltpu.roll(b, slot * 16, 1)
        last = pl.ds(block, 8)
        out[chunk[g], last, :] = jnp.where((lane >> 4) == slot, moved, out[chunk[g], last, :])

    lax.fori_loop(0, PAIRS - 1, two, 0)
    first, second = tracer(NTR - 1), air()
    for l in range(LEVS):
        for g in range(GROUPS):
            pack(g, l, ((PAIRS - 1) * LEVS + l) * 8, REST + 8, l * 4, first, second)


def target_kernel(index, offset, phase, inner, outer):
    lane = lane_index()
    blank = jnp.zeros((8, LANES - CHUNK), F32)
    for ref in (inner, outer):
        ref[pl.ds(0, 16), :] = jnp.zeros((16, LANES), F32)
    for n in range(2 * GROUPS - 1):
        at = (n + 1) * 16
        main, tail = [], []
        for h in range(2):
            rows = pl.ds(8 * h, 8)
            part = (offset[n, rows, :].astype(F32) + phase[n, rows, :]) * (1.0 / 32.0)
            x = jnp.concatenate([index[n, rows, :].astype(F32) + part, blank], 1)
            moved = turn(x, CHUNK, 1)
            main.append(jnp.where(lane < CHUNK, x, moved))
            last = jnp.where(lane < 16, moved, 0.0)
            last = last + turn(last, 16, 1)
            tail.append(last + turn(last, 32, 1))
        other = [turn(x, 64, 1) for x in tail]
        inner[pl.ds(at, 4), :] = main[0][4:]
        inner[pl.ds(at + 4, 4), :] = main[1][:4]
        inner[pl.ds(at + 8, 8), :] = turn(tail[0], 4, 0) + other[1]
        outer[pl.ds(at, 4, stride=2), :] = main[0][:4]
        outer[pl.ds(at + 1, 4, stride=2), :] = main[1][4:]
        outer[pl.ds(at + 8, 2, stride=2), :] = (tail[0] + turn(other[0], -2, 0))[:2]
        outer[pl.ds(at + 9, 2, stride=2), :] = (tail[1] + turn(other[1], -2, 0))[4:6]


def remap_rows(data, table, out):
    lane, row = lane_index(), row_index()

    def targets(tile):
        found = []
        for parity in range(2):
            for half in range(2):
                start = (parity + 16 * half) * 16 + tile
                position = table[pl.ds(start, 8, stride=32), :]
                s = jnp.minimum(position.astype(jnp.int32), 2 * GROUPS - 1)
                f = position - s.astype(F32)
                square = f * f * 0.5
                cubic = 3.0 * square - f * f * f
                found.append(((s >> 1) & 7, s >= 16, (s & 1) == 1, f, square, cubic))
        return found

    def columns(even, odd, found):
        back = [turn(x, 1, 0) for x in odd]
        before = [jnp.where(row == 0, even[0], back[0]), jnp.where(row == 0, back[0], back[1])]
        left = [0.5 * (before[i] + even[i]) for i in range(2)]
        ahead = [turn(x, -1, 0) for x in left]
        right = [jnp.where(row == 7, ahead[1], ahead[0]), jnp.where(row == 7, odd[1], ahead[1])]
        pair = [even[i] + odd[i] for i in range(2)]
        run = list(pair)
        for shift in (1, 2, 4):
            run = [x + jnp.where(row >= shift, turn(x, shift, 0), 0.0) for x in run]
        half_sum = jnp.broadcast_to(run[0][7:8], (8, LANES))
        total = half_sum + run[1][7:8]
        below = [run[0] - pair[0], (run[1] - pair[1]) + half_sum]
        edges = []
        for where, high, is_odd, f, square, cubic in found:
            le, ri, ev, od, be = (
                jnp.where(high, pick(x[1], where), pick(x[0], where)) for x in (left, right, even, odd, below)
            )
            middle = 0.5 * (ev + od)
            lo = jnp.where(is_odd, middle, le)
            hi = jnp.where(is_odd, ri, middle)
            m = jnp.where(is_odd, od, ev)
            base = be + jnp.where(is_odd, ev, 0.0)
            edges.append(base + lo * f + (hi - lo) * square + ((m + m) - (lo + hi)) * cubic)
        ev0, ev1, od0, od1 = edges
        next0, next1 = turn(ev0, -1, 0), turn(ev1, -1, 0)
        new_even = [od0 - ev0, od1 - ev1]
        new_odd = [jnp.where(row == 7, next1, next0) - od0, jnp.where(row == 7, total, next1) - od1]
        return new_even, new_odd

    def span(start, half):
        return pl.ds(start + half * 8 * DEPTH, 8, stride=DEPTH)

    def main(tile, _):
        found = targets(tile)
        for pair in range(PAIRS):
            at = [(pair * LEVS + l) * 8 + tile for l in range(LEVS)]
            even, odd = ([data[span(at[l], half), :] for half in range(2)] for l in range(LEVS))
            new = columns(even, odd, found)
            for l in range(LEVS):
                for half in range(2):
                    out[span(at[l], half), :] = new[l][half]
        return 0

    lax.fori_loop(0, 8, main, 0)

    def tail(tile, _):
        found = targets(8 + tile)
        for block in range(BLOCKS):
            at = [REST + 8 * block + tile, REST + 8 * block + tile + 4]
            a, b = ([data[span(at[i], half), :] for half in range(2)] for i in range(2))
            even = [jnp.where(lane < 64, a[half], turn(b[half], 64, 1)) for half in range(2)]
            odd = [jnp.where(lane < 64, turn(a[half], 64, 1), b[half]) for half in range(2)]
            even, odd = columns(even, odd, found)
            for half in range(2):
                out[span(at[0], half), :] = jnp.where(lane < 64, even[half], turn(odd[half], 64, 1))
                out[span(at[1], half), :] = jnp.where(lane < 64, turn(even[half], 64, 1), odd[half])
        return 0

    lax.fori_loop(0, 4, tail, 0)


def place_of():
    lev = lax.axis_index("lev")
    return lev >> 2, lev & 3, (lax.axis_index("lat") & 1) == 1


def slots_to():
    y, z, odd = place_of()
    slots = []
    for g in range(GROUPS):
        j, k = ((g >> 2) - y) & 3, (g & 3) ^ z
        slots.append(jnp.where(odd, 4 * j + k, 4 * k + j))
    return slots


def gather_chunks(given, target, sem):
    y, z, odd = place_of()
    copies = []
    for a in range(4):
        for b in range(4):
            j, k = jnp.where(odd, a, b), jnp.where(odd, b, a)
            place = ((y - j) & 3) * 4 + (z ^ k)
            copies.append(pltpu.make_async_copy(given[b].at[a], target(place), sem.at[4 * a + b]))
    for copy in copies:
        copy.start()
    for copy in copies:
        copy.wait()


def remap_kernel(*refs):
    given, (table, out, data, new, sem) = refs[:4], refs[4:]

    def rows(place):
        return pl.ds(pl.multiple_of(place * DEPTH, 8), DEPTH)

    gather_chunks(given, lambda place: data.at[rows(place)], sem)
    remap_rows(data, table, new)
    copies = []
    for g, slot in enumerate(slots_to()):
        copies.append(pltpu.make_async_copy(new.at[rows(g)], out.at[slot], sem.at[g]))
    for copy in copies:
        copy.start()
    for copy in copies:
        copy.wait()


def collect_kernel(part, *refs):
    given, (out, data, flat, sem) = refs[:4], refs[-4:]
    gather_chunks(given, lambda place: data.at[place], sem)
    lane = lane_index()

    def unpack(pair, at, block, slot):
        for l in range(LEVS):
            pieces = []
            for g in range(GROUPS):
                _, o = span_of(g)
                main = data[g, at(l), :]
                tail = pltpu.roll(data[g, pl.ds(block, 8), :], LANES - (l * 4 + slot) * 16, 1)
                mixed = jnp.where(lane < 16, tail, main)
                pieces.append((turn(main, o, 1), turn(mixed, o - CHUNK, 1)))
            for second in range(2):
                for c in range(TILES):
                    value = None
                    for g in range(GROUPS):
                        start = CHUNK * g - LANES * c
                        if start >= LANES or start + CHUNK <= 0:
                            continue
                        piece = pieces[g][second]
                        value = piece if value is None else jnp.where(lane >= start, piece, value)
                    flat[pl.ds((2 * pair + second) * 8 * STEP + c * LEVS + l, 8, stride=STEP), :] = value

    def one(pair, _):
        unpack(pair, lambda l: pl.ds(pl.multiple_of((pair * LEVS + l) * 8, 8), 8), REST, pair)
        return 0

    lax.fori_loop(0, PAIRS - 1, one, 0)
    unpack(PAIRS - 1, lambda l: pl.ds(((PAIRS - 1) * LEVS + l) * 8, 8), REST + 8, 0)
    view = flat.reshape(FIELDS, 8 // part, part, TILES, LEVS, LANES)
    copies = []
    for c in range(TILES):
        cut = pl.ds(LANES * c, LANES)
        for run, first in enumerate((4,) if part == INNER else (0, 12)):
            target = out.at[:, pl.ds(first, 8 // part), :, cut]
            copies.append(pltpu.make_async_copy(view.at[:, :, run, c], target, sem.at[len(copies)]))
    for copy in copies:
        copy.start()
    for copy in copies:
        copy.wait()


ANYWHERE = pl.BlockSpec(memory_space=pl.ANY)
IN_HBM = pl.BlockSpec(memory_space=pltpu.HBM)
IN_VMEM = pl.BlockSpec(memory_space=pltpu.VMEM)
PARAMS = pltpu.CompilerParams(vmem_limit_bytes=VMEM_LIMIT)


def transport(part, *given):
    factor = pltpu.VMEM((STEP * 8, LANES), F32)
    return pl.pallas_call(
        functools.partial(transport_kernel, part),
        out_shape=jax.ShapeDtypeStruct((GROUPS, DEPTH, LANES), F32),
        in_specs=[IN_HBM] * 4 + [ANYWHERE] * (len(given) - 4),
        out_specs=IN_VMEM,
        scratch_shapes=[
            pltpu.VMEM(((NTR + 3) * slots_of(part) * STEP, LANES), F32),
            factor,
            factor,
            factor,
            factor,
            pltpu.VMEM((STEP * 16, LANES), F32),
            pltpu.SemaphoreType.DMA((10 * TILES,)),
        ],
        compiler_params=PARAMS,
    )(*given)


def remap(given, table):
    held = pltpu.VMEM((GROUPS * DEPTH, LANES), F32)
    return pl.pallas_call(
        remap_kernel,
        out_shape=jax.ShapeDtypeStruct((GROUPS, DEPTH, LANES), F32),
        in_specs=[ANYWHERE] * 4 + [IN_VMEM],
        out_specs=ANYWHERE,
        scratch_shapes=[held, held, pltpu.SemaphoreType.DMA((GROUPS,))],
        compiler_params=PARAMS,
    )(*given, table)


def collect(part, given, *result):
    return pl.pallas_call(
        functools.partial(collect_kernel, part),
        out_shape=jax.ShapeDtypeStruct((FIELDS, ROWS, LEVS, LONS), F32),
        in_specs=[ANYWHERE] * (4 + len(result)),
        out_specs=ANYWHERE,
        scratch_shapes=[
            pltpu.VMEM((GROUPS, DEPTH, LANES), F32),
            pltpu.VMEM((FIELDS * 8 * STEP, LANES), F32),
            pltpu.SemaphoreType.DMA((2 * TILES,)),
        ],
        input_output_aliases={4: 0} if result else {},
        compiler_params=PARAMS,
    )(*given, *result)


def hop(blocks, first):
    lats = lax.axis_size("lat")
    moved = {}
    for a in (2, 3, 1):
        pairs = []
        for lat in range(lats):
            along_z = (lat % 2 == 0) == first
            for lev in range(GROUPS):
                target = lev ^ a if along_z else (lev + 4 * a) % GROUPS
                pairs.append((lat * GROUPS + lev, lat * GROUPS + target))
        moved[a] = lax.ppermute(blocks[a], ("lat", "lev"), pairs)
    return [blocks[0]] + [moved[a] for a in range(1, 4)]


def first_hop(data):
    return hop([data[4 * a : 4 * a + 4] for a in range(4)], True)


def second_hop(rows):
    return hop([jnp.stack([rows[a][b] for a in range(4)]) for b in range(4)], False)


def after(values, *others):
    return lax.optimization_barrier((values, others))[0]


def shards(tracers, thickness, courant_x, courant_y, level_index, level_offset, level_phase):
    own = [pltpu.with_memory_space_constraint(x, pltpu.HBM) for x in (tracers, thickness, courant_x, courant_y)]
    rim = jax.ShapeDtypeStruct((NTR + 2, 2, LEVS, LONS), F32)
    south, north = pl.pallas_call(
        halo_kernel,
        out_shape=(rim, rim),
        in_specs=[IN_HBM] * 3,
        out_specs=(IN_VMEM, IN_VMEM),
        scratch_shapes=[pltpu.SemaphoreType.DMA((2, 3))],
    )(own[0], own[1], own[3])
    count = lax.axis_size("lat")
    low = lax.ppermute(north, "lat", [(i, i + 1) for i in range(count - 1)])
    high = lax.ppermute(south, "lat", [(i + 1, i) for i in range(count - 1)])
    inner = transport(INNER, *own, south)
    table = jax.ShapeDtypeStruct((2 * GROUPS * 16, LANES), F32)
    inner_table, outer_table = pl.pallas_call(
        target_kernel,
        out_shape=(table, table),
        in_specs=[IN_VMEM] * 3,
        out_specs=(IN_VMEM, IN_VMEM),
        compiler_params=PARAMS,
    )(level_index, level_offset, level_phase)
    outer = transport(OUTER, *own, low, high, outer_table)
    inner = first_hop(inner)
    inner, outer = second_hop(after(inner, outer)), first_hop(outer)
    outer = second_hop(outer)
    inner = remap(inner, inner_table)
    outer = remap(after(outer, inner), outer_table)
    inner = first_hop(inner)
    inner, outer = second_hop(after(inner, outer)), first_hop(outer)
    outer = second_hop(outer)
    return collect(OUTER, outer, collect(INNER, inner))


def solution(mesh):
    in_specs = (
        P(None, "lat", "lev", None),
        P("lat", "lev", None),
        P("lat", "lev", None),
        P("lat", "lev", None),
        P(None, "lat", "lev"),
        P(None, "lat", "lev"),
        P(None, "lat", "lev"),
    )
    out_specs = P(None, "lat", "lev", None)
    return jax.shard_map(shards, mesh=mesh, in_specs=in_specs, out_specs=out_specs, check_vma=False)
```

```python
import functools

import jax
import jax.numpy as jnp
from jax import lax
from jax.experimental import pallas as pl
from jax.experimental.pallas import tpu as pltpu
from jax.sharding import PartitionSpec as P

F32 = jnp.float32
NTR = 9
FIELDS = NTR + 1
PAIRS = FIELDS // 2
ROWS = 16
LEVS = 2
LANES = 128
TILES = 9
LONS = LANES * TILES
CHUNK = 72
GROUPS = 16
STEP = TILES * LEVS
VMEM_LIMIT = 40 * 1024 * 1024

INNER, OUTER = 1, 2

REST = PAIRS * LEVS * 8
BLOCKS = (PAIRS + 3) // 4
DEPTH = REST + BLOCKS * 8

THICK, NORTH, EAST = NTR, NTR + 1, NTR + 2


def slots_of(part):
    return 8 + 4 * part


def lane_index():
    return lax.broadcasted_iota(jnp.int32, (8, LANES), 1)


def row_index():
    return lax.broadcasted_iota(jnp.int32, (8, LANES), 0)


def turn(x, shift, axis):
    shift = shift % x.shape[axis]
    return x if shift == 0 else pltpu.roll(x, shift, axis)


def west_of(tiles, lane):
    rolled = [turn(x, 1, 1) for x in tiles]
    return [jnp.where(lane == 0, rolled[c - 1], rolled[c]) for c in range(TILES)]


def east_of(tiles, lane):
    rolled = [turn(x, -1, 1) for x in tiles]
    return [jnp.where(lane == LANES - 1, rolled[(c + 1) % TILES], rolled[c]) for c in range(TILES)]


def span_of(group):
    return divmod(CHUNK * group, LANES)


def pick(x, where):
    return jnp.take_along_axis(x, where, axis=0, mode="promise_in_bounds")


def on_odd_row():
    return (lax.axis_index("lat") & 1) == 1


def halo_kernel(tracers, thickness, courant_y, inside, across, sem):
    odd = on_odd_row()
    copies = []
    for edge, (out, first) in enumerate(((inside, jnp.where(odd, 0, ROWS - 2)), (across, jnp.where(odd, ROWS - 2, 0)))):
        rows = pl.ds(first, 2)
        copies.append(pltpu.make_async_copy(tracers.at[:, rows], out.at[pl.ds(0, NTR)], sem.at[edge, 0]))
        copies.append(pltpu.make_async_copy(thickness.at[rows], out.at[THICK], sem.at[edge, 1]))
        copies.append(pltpu.make_async_copy(courant_y.at[rows], out.at[NORTH], sem.at[edge, 2]))
    for copy in copies:
        copy.start()
    for copy in copies:
        copy.wait()


def transport_kernel(part, *refs):
    if part == OUTER:
        tracers, thickness, courant_x, courant_y, inside, across, _, out, held, mx, ax, my, ay, fy, sem = refs
    else:
        tracers, thickness, courant_x, courant_y, _, out, held, mx, ax, my, ay, fy, sem = refs
    chunk = slots_to()
    slots = slots_of(part)
    lane, row = lane_index(), row_index()
    view = held.reshape(NTR + 3, slots // part, part, TILES, LEVS, LANES)
    copies = []

    def bring(source, target):
        copies.append(pltpu.make_async_copy(source, target, sem.at[len(copies)]))

    for c in range(TILES):
        cut = pl.ds(LANES * c, LANES)
        runs = ((2, 12, 0, 0),) if part == INNER else ((0, 6, 2, 0), (10, 6, 0, 1))
        for first, size, at, run in runs:
            own, into = pl.ds(first, size), pl.ds(at, size)
            bring(tracers.at[:, own, :, cut], view.at[pl.ds(0, NTR), into, run, c])
            for array, source in ((THICK, thickness), (NORTH, courant_y), (EAST, courant_x)):
                bring(source.at[own, :, cut], view.at[array, into, run, c])
    for copy in copies:
        copy.start()
    if part == OUTER:

        def bring_halos(low, high):
            for c in range(TILES):
                cut = pl.ds(LANES * c, LANES)
                bring(low.at[pl.ds(0, NTR + 1), :, :, cut], view.at[pl.ds(0, NTR + 1), pl.ds(0, 2), 0, c])
                bring(high.at[:, :, :, cut], view.at[pl.ds(0, NTR + 2), pl.ds(6, 2), 1, c])
            return copies[-2 * TILES :]

        odd = on_odd_row()

        @pl.when(odd)
        def _():
            for copy in bring_halos(inside, across):
                copy.start()

        del copies[-2 * TILES :]
        halos = bring_halos(across, inside)

        @pl.when(jnp.logical_not(odd))
        def _():
            for copy in halos:
                copy.start()

    for g in range(GROUPS):
        out[g, pl.ds(REST, 8 * BLOCKS), :] = jnp.zeros((8 * BLOCKS, LANES), F32)
    for copy in copies:
        copy.wait()

    def rows_of(array, shift, c, l):
        start = (array * slots + (2 + shift) * part) * STEP + c * LEVS + l
        return held[pl.ds(start, 8, stride=STEP), :]

    def past(array, shift):
        return held[pl.ds((array * slots + 8 + (2 + shift) * part) * STEP, part * STEP), :]

    def place(l, c):
        return pl.ds((c * LEVS + l) * 8, 8)

    def faces(l, c, shift):
        return pl.ds((c * LEVS + l) * 16 + shift, 8)

    def keep_past(values):
        for run in range(part):
            fy[pl.ds(8 + run, STEP, stride=16), :] = values[run * STEP : (run + 1) * STEP]

    def factors(courant, before, after):
        mass = jnp.where(courant > 0, courant * before, courant * after)
        return mass, mass * jnp.where(courant > 0, 0.25 - 0.25 * courant, -0.25 - 0.25 * courant)

    for l in range(LEVS):
        thick = [rows_of(THICK, 0, c, l) for c in range(TILES)]
        west = west_of(thick, lane)
        for c in range(TILES):
            mx[place(l, c), :], ax[place(l, c), :] = factors(rows_of(EAST, 0, c, l), west[c], thick[c])
            courant = rows_of(NORTH, 0, c, l)
            if part == OUTER:
                courant = jnp.where((row > 0) | (lax.axis_index("lat") > 0), courant, 0.0)
            my[place(l, c), :], ay[place(l, c), :] = factors(courant, rows_of(THICK, -1, c, l), thick[c])
    past_mass, past_tilt = factors(past(NORTH, 0), past(THICK, -1), past(THICK, 0))

    def air():
        keep_past(past_mass)
        for l in range(LEVS):
            for c in range(TILES):
                fy[faces(l, c, 0), :] = my[place(l, c), :]
        tiles = []
        for l in range(LEVS):
            flux = [mx[place(l, c), :] for c in range(TILES)]
            flux_e = east_of(flux, lane)
            tiles.append(
                [
                    rows_of(THICK, 0, c, l) + (flux[c] - flux_e[c]) + (my[place(l, c), :] - fy[faces(l, c, part), :])
                    for c in range(TILES)
                ]
            )
        return tiles

    def tracer(array):
        past_q = [past(array, shift) for shift in (-2, -1, 0, 1)]
        up = past_mass > 0
        value = jnp.where(up, past_q[1], past_q[2])
        rise = jnp.where(up, past_q[2] - past_q[0], past_q[3] - past_q[1])
        keep_past(past_mass * value + past_tilt * rise)
        tiles = []
        for l in range(LEVS):
            q = [rows_of(array, 0, c, l) for c in range(TILES)]
            qw = west_of(q, lane)
            qe = east_of(q, lane)
            d = [qe[c] - qw[c] for c in range(TILES)]
            dw = west_of(d, lane)
            flux = []
            for c in range(TILES):
                mass = mx[place(l, c), :]
                up = mass > 0
                flux.append(mass * jnp.where(up, qw[c], q[c]) + ax[place(l, c), :] * jnp.where(up, dw[c], d[c]))
            flux_e = east_of(flux, lane)
            now = []
            for c in range(TILES):
                mass = my[place(l, c), :]
                up = mass > 0
                q2, q1, q3 = (rows_of(array, shift, c, l) for shift in (-2, -1, 1))
                value = jnp.where(up, q1, q[c])
                rise = jnp.where(up, q[c] - q2, q3 - q1)
                flux_y = mass * value + ay[place(l, c), :] * rise
                fy[faces(l, c, 0), :] = flux_y
                now.append(rows_of(THICK, 0, c, l) * q[c] + (flux[c] - flux_e[c]) + flux_y)
            tiles.append(now)
        return [[tiles[l][c] - fy[faces(l, c, part), :] for c in range(TILES)] for l in range(LEVS)]

    def two(pair, _):
        first = tracer(2 * pair)
        send_block(pair, first, tracer(2 * pair + 1))
        return 0

    def send_block(pair, first, second):
        block = REST
        for l in range(LEVS):
            slot = l * 4 + pair
            for g in range(GROUPS):
                pack(g, l, pl.multiple_of((pair * LEVS + l) * 8, 8), block, slot, first, second)

    def pack(g, l, at, block, slot, first, second):
        t, o = span_of(g)
        a = turn(first[l][t], -o, 1)
        b = turn(second[l][t], CHUNK - o, 1)
        if o + CHUNK > LANES:
            a = jnp.where(lane < LANES - o, a, turn(first[l][t + 1], -o, 1))
            lon = jnp.where(lane >= CHUNK, lane - CHUNK, lane + (LANES - CHUNK))
            b = jnp.where(lon < LANES - o, b, turn(second[l][t + 1], CHUNK - o, 1))
        out[chunk[g], pl.ds(at, 8), :] = jnp.where(lane < CHUNK, a, b)
        moved = pltpu.roll(b, slot * 16, 1)
        last = pl.ds(block, 8)
        out[chunk[g], last, :] = jnp.where((lane >> 4) == slot, moved, out[chunk[g], last, :])

    lax.fori_loop(0, PAIRS - 1, two, 0)
    first, second = tracer(NTR - 1), air()
    for l in range(LEVS):
        for g in range(GROUPS):
            pack(g, l, ((PAIRS - 1) * LEVS + l) * 8, REST + 8, l * 4, first, second)


def target_kernel(index, offset, phase, inner, outer):
    lane = lane_index()
    blank = jnp.zeros((8, LANES - CHUNK), F32)
    for ref in (inner, outer):
        ref[pl.ds(0, 16), :] = jnp.zeros((16, LANES), F32)
    for n in range(2 * GROUPS - 1):
        at = (n + 1) * 16
        main, tail = [], []
        for h in range(2):
            rows = pl.ds(8 * h, 8)
            part = (offset[n, rows, :].astype(F32) + phase[n, rows, :]) * (1.0 / 32.0)
            x = jnp.concatenate([index[n, rows, :].astype(F32) + part, blank], 1)
            moved = turn(x, CHUNK, 1)
            main.append(jnp.where(lane < CHUNK, x, moved))
            last = jnp.where(lane < 16, moved, 0.0)
            last = last + turn(last, 16, 1)
            tail.append(last + turn(last, 32, 1))
        other = [turn(x, 64, 1) for x in tail]
        inner[pl.ds(at, 4), :] = main[0][4:]
        inner[pl.ds(at + 4, 4), :] = main[1][:4]
        inner[pl.ds(at + 8, 8), :] = turn(tail[0], 4, 0) + other[1]
        outer[pl.ds(at, 4, stride=2), :] = main[0][:4]
        outer[pl.ds(at + 1, 4, stride=2), :] = main[1][4:]
        outer[pl.ds(at + 8, 2, stride=2), :] = (tail[0] + turn(other[0], -2, 0))[:2]
        outer[pl.ds(at + 9, 2, stride=2), :] = (tail[1] + turn(other[1], -2, 0))[4:6]


def remap_rows(data, table, out):
    lane, row = lane_index(), row_index()

    def targets(tile):
        found = []
        for parity in range(2):
            for half in range(2):
                start = (parity + 16 * half) * 16 + tile
                position = table[pl.ds(start, 8, stride=32), :]
                s = jnp.minimum(position.astype(jnp.int32), 2 * GROUPS - 1)
                f = position - s.astype(F32)
                square = f * f * 0.5
                cubic = 3.0 * square - f * f * f
                found.append(((s >> 1) & 7, s >= 16, (s & 1) == 1, f, square, cubic))
        return found

    def columns(even, odd, found):
        back = [turn(x, 1, 0) for x in odd]
        before = [jnp.where(row == 0, even[0], back[0]), jnp.where(row == 0, back[0], back[1])]
        left = [0.5 * (before[i] + even[i]) for i in range(2)]
        ahead = [turn(x, -1, 0) for x in left]
        right = [jnp.where(row == 7, ahead[1], ahead[0]), jnp.where(row == 7, odd[1], ahead[1])]
        pair = [even[i] + odd[i] for i in range(2)]
        run = list(pair)
        for shift in (1, 2, 4):
            run = [x + jnp.where(row >= shift, turn(x, shift, 0), 0.0) for x in run]
        half_sum = jnp.broadcast_to(run[0][7:8], (8, LANES))
        total = half_sum + run[1][7:8]
        below = [run[0] - pair[0], (run[1] - pair[1]) + half_sum]
        edges = []
        for where, high, is_odd, f, square, cubic in found:
            le, ri, ev, od, be = (
                jnp.where(high, pick(x[1], where), pick(x[0], where)) for x in (left, right, even, odd, below)
            )
            middle = 0.5 * (ev + od)
            lo = jnp.where(is_odd, middle, le)
            hi = jnp.where(is_odd, ri, middle)
            m = jnp.where(is_odd, od, ev)
            base = be + jnp.where(is_odd, ev, 0.0)
            edges.append(base + lo * f + (hi - lo) * square + ((m + m) - (lo + hi)) * cubic)
        ev0, ev1, od0, od1 = edges
        next0, next1 = turn(ev0, -1, 0), turn(ev1, -1, 0)
        new_even = [od0 - ev0, od1 - ev1]
        new_odd = [jnp.where(row == 7, next1, next0) - od0, jnp.where(row == 7, total, next1) - od1]
        return new_even, new_odd

    def span(start, half):
        return pl.ds(start + half * 8 * DEPTH, 8, stride=DEPTH)

    def main(tile, _):
        found = targets(tile)
        for pair in range(PAIRS):
            at = [(pair * LEVS + l) * 8 + tile for l in range(LEVS)]
            even, odd = ([data[span(at[l], half), :] for half in range(2)] for l in range(LEVS))
            new = columns(even, odd, found)
            for l in range(LEVS):
                for half in range(2):
                    out[span(at[l], half), :] = new[l][half]
        return 0

    lax.fori_loop(0, 8, main, 0)

    def tail(tile, _):
        found = targets(8 + tile)
        for block in range(BLOCKS):
            at = [REST + 8 * block + tile, REST + 8 * block + tile + 4]
            a, b = ([data[span(at[i], half), :] for half in range(2)] for i in range(2))
            even = [jnp.where(lane < 64, a[half], turn(b[half], 64, 1)) for half in range(2)]
            odd = [jnp.where(lane < 64, turn(a[half], 64, 1), b[half]) for half in range(2)]
            even, odd = columns(even, odd, found)
            for half in range(2):
                out[span(at[0], half), :] = jnp.where(lane < 64, even[half], turn(odd[half], 64, 1))
                out[span(at[1], half), :] = jnp.where(lane < 64, turn(even[half], 64, 1), odd[half])
        return 0

    lax.fori_loop(0, 4, tail, 0)


def place_of():
    lev = lax.axis_index("lev")
    return lev >> 2, lev & 3, on_odd_row()


def slots_to():
    y, z, odd = place_of()
    slots = []
    for g in range(GROUPS):
        j, k = ((g >> 2) - y) & 3, (g & 3) ^ z
        slots.append(jnp.where(odd, 4 * j + k, 4 * k + j))
    return slots


def gather_chunks(given, target, sem):
    y, z, odd = place_of()
    copies = []
    for a in range(4):
        for b in range(4):
            j, k = jnp.where(odd, a, b), jnp.where(odd, b, a)
            place = ((y - j) & 3) * 4 + (z ^ k)
            copies.append(pltpu.make_async_copy(given[b].at[a], target(place), sem.at[4 * a + b]))
    for copy in copies:
        copy.start()
    for copy in copies:
        copy.wait()


def remap_kernel(*refs):
    given, (table, out, data, new, sem) = refs[:4], refs[4:]

    def rows(place):
        return pl.ds(pl.multiple_of(place * DEPTH, 8), DEPTH)

    gather_chunks(given, lambda place: data.at[rows(place)], sem)
    remap_rows(data, table, new)
    copies = []
    for g, slot in enumerate(slots_to()):
        copies.append(pltpu.make_async_copy(new.at[rows(g)], out.at[slot], sem.at[g]))
    for copy in copies:
        copy.start()
    for copy in copies:
        copy.wait()


def collect_kernel(part, *refs):
    given, (out, data, flat, sem) = refs[:4], refs[-4:]
    gather_chunks(given, lambda place: data.at[place], sem)
    lane = lane_index()

    def unpack(pair, at, block, slot):
        for l in range(LEVS):
            pieces = []
            for g in range(GROUPS):
                _, o = span_of(g)
                main = data[g, at(l), :]
                tail = pltpu.roll(data[g, pl.ds(block, 8), :], LANES - (l * 4 + slot) * 16, 1)
                mixed = jnp.where(lane < 16, tail, main)
                pieces.append((turn(main, o, 1), turn(mixed, o - CHUNK, 1)))
            for second in range(2):
                for c in range(TILES):
                    value = None
                    for g in range(GROUPS):
                        start = CHUNK * g - LANES * c
                        if start >= LANES or start + CHUNK <= 0:
                            continue
                        piece = pieces[g][second]
                        value = piece if value is None else jnp.where(lane >= start, piece, value)
                    flat[pl.ds((2 * pair + second) * 8 * STEP + c * LEVS + l, 8, stride=STEP), :] = value

    def one(pair, _):
        unpack(pair, lambda l: pl.ds(pl.multiple_of((pair * LEVS + l) * 8, 8), 8), REST, pair)
        return 0

    lax.fori_loop(0, PAIRS - 1, one, 0)
    unpack(PAIRS - 1, lambda l: pl.ds(((PAIRS - 1) * LEVS + l) * 8, 8), REST + 8, 0)
    view = flat.reshape(FIELDS, 8 // part, part, TILES, LEVS, LANES)
    copies = []
    for c in range(TILES):
        cut = pl.ds(LANES * c, LANES)
        for run, first in enumerate((4,) if part == INNER else (0, 12)):
            target = out.at[:, pl.ds(first, 8 // part), :, cut]
            copies.append(pltpu.make_async_copy(view.at[:, :, run, c], target, sem.at[len(copies)]))
    for copy in copies:
        copy.start()
    for copy in copies:
        copy.wait()


ANYWHERE = pl.BlockSpec(memory_space=pl.ANY)
IN_HBM = pl.BlockSpec(memory_space=pltpu.HBM)
IN_VMEM = pl.BlockSpec(memory_space=pltpu.VMEM)
PARAMS = pltpu.CompilerParams(vmem_limit_bytes=VMEM_LIMIT)


def transport(part, *given):
    factor = pltpu.VMEM((STEP * 8, LANES), F32)
    return pl.pallas_call(
        functools.partial(transport_kernel, part),
        out_shape=jax.ShapeDtypeStruct((GROUPS, DEPTH, LANES), F32),
        in_specs=[IN_HBM] * 4 + [IN_HBM if part == INNER else ANYWHERE] * (len(given) - 4),
        out_specs=IN_VMEM,
        scratch_shapes=[
            pltpu.VMEM(((NTR + 3) * slots_of(part) * STEP, LANES), F32),
            factor,
            factor,
            factor,
            factor,
            pltpu.VMEM((STEP * 16, LANES), F32),
            pltpu.SemaphoreType.DMA((10 * TILES,)),
        ],
        compiler_params=PARAMS,
    )(*given)


def remap(given, table):
    held = pltpu.VMEM((GROUPS * DEPTH, LANES), F32)
    return pl.pallas_call(
        remap_kernel,
        out_shape=jax.ShapeDtypeStruct((GROUPS, DEPTH, LANES), F32),
        in_specs=[ANYWHERE] * 4 + [IN_VMEM],
        out_specs=ANYWHERE,
        scratch_shapes=[held, held, pltpu.SemaphoreType.DMA((GROUPS,))],
        compiler_params=PARAMS,
    )(*given, table)


def collect(part, given, *result):
    return pl.pallas_call(
        functools.partial(collect_kernel, part),
        out_shape=jax.ShapeDtypeStruct((FIELDS, ROWS, LEVS, LONS), F32),
        in_specs=[ANYWHERE] * (4 + len(result)),
        out_specs=ANYWHERE,
        scratch_shapes=[
            pltpu.VMEM((GROUPS, DEPTH, LANES), F32),
            pltpu.VMEM((FIELDS * 8 * STEP, LANES), F32),
            pltpu.SemaphoreType.DMA((2 * TILES,)),
        ],
        input_output_aliases={4: 0} if result else {},
        compiler_params=PARAMS,
    )(*given, *result)


def hop(blocks, first):
    lats = lax.axis_size("lat")
    moved = {}
    for a in (2, 3, 1):
        pairs = []
        for lat in range(lats):
            along_z = (lat % 2 == 0) == first
            for lev in range(GROUPS):
                target = lev ^ a if along_z else (lev + 4 * a) % GROUPS
                pairs.append((lat * GROUPS + lev, lat * GROUPS + target))
        moved[a] = lax.ppermute(blocks[a], ("lat", "lev"), pairs)
    return [blocks[0]] + [moved[a] for a in range(1, 4)]


def first_hop(data):
    return hop([data[4 * a : 4 * a + 4] for a in range(4)], True)


def second_hop(rows):
    return hop([jnp.stack([rows[a][b] for a in range(4)]) for b in range(4)], False)


def after(values, *others):
    return lax.optimization_barrier((values, others))[0]


def shards(tracers, thickness, courant_x, courant_y, level_index, level_offset, level_phase):
    own = [pltpu.with_memory_space_constraint(x, pltpu.HBM) for x in (tracers, thickness, courant_x, courant_y)]
    rim = pltpu.HBM((NTR + 2, 2, LEVS, LONS), F32)
    inside, across = pl.pallas_call(
        halo_kernel,
        out_shape=(rim, rim),
        in_specs=[IN_HBM] * 3,
        out_specs=(IN_VMEM, IN_VMEM),
        scratch_shapes=[pltpu.SemaphoreType.DMA((2, 3))],
    )(own[0], own[1], own[3])
    lats = lax.axis_size("lat")
    to_core = [(i, i ^ 1) for i in range(lats)]
    to_chip = [(i, i + 1) for i in range(1, lats - 1, 2)] + [(i + 1, i) for i in range(1, lats - 1, 2)]
    first = pltpu.with_memory_space_constraint(inside, pltpu.HBM)
    inside, across = lax.ppermute(inside, "lat", to_core), lax.ppermute(across, "lat", to_chip)
    inner = transport(INNER, *own, first)
    table = jax.ShapeDtypeStruct((2 * GROUPS * 16, LANES), F32)
    inner_table, outer_table = pl.pallas_call(
        target_kernel,
        out_shape=(table, table),
        in_specs=[IN_VMEM] * 3,
        out_specs=(IN_VMEM, IN_VMEM),
        compiler_params=PARAMS,
    )(level_index, level_offset, level_phase)
    outer = transport(OUTER, *own, inside, across, outer_table)
    inner = first_hop(inner)
    inner, outer = second_hop(after(inner, outer)), first_hop(outer)
    inner = remap(inner, inner_table)
    outer = second_hop(after(outer, inner))
    inner = first_hop(inner)
    outer = remap(outer, outer_table)
    inner, outer = second_hop(after(inner, outer)), first_hop(outer)
    outer = second_hop(outer)
    return collect(OUTER, outer, collect(INNER, inner))


def solution(mesh):
    in_specs = (
        P(None, "lat", "lev", None),
        P("lat", "lev", None),
        P("lat", "lev", None),
        P("lat", "lev", None),
        P(None, "lat", "lev"),
        P(None, "lat", "lev"),
        P(None, "lat", "lev"),
    )
    out_specs = P(None, "lat", "lev", None)
    return jax.shard_map(shards, mesh=mesh, in_specs=in_specs, out_specs=out_specs, check_vma=False)
```

```python
import functools

import jax
import jax.numpy as jnp
from jax import lax
from jax.experimental import pallas as pl
from jax.experimental.pallas import tpu as pltpu
from jax.sharding import PartitionSpec as P

F32 = jnp.float32
NTR = 9
FIELDS = NTR + 1
PAIRS = FIELDS // 2
ROWS = 16
LEVS = 2
LANES = 128
TILES = 9
LONS = LANES * TILES
CHUNK = 72
GROUPS = 16
STEP = TILES * LEVS
VMEM_LIMIT = 40 * 1024 * 1024

INNER, OUTER = 1, 2

REST = PAIRS * LEVS * 8
BLOCKS = (PAIRS + 3) // 4
DEPTH = REST + BLOCKS * 8

THICK, NORTH, EAST = NTR, NTR + 1, NTR + 2


def slots_of(part):
    return 8 + 4 * part


def lane_index():
    return lax.broadcasted_iota(jnp.int32, (8, LANES), 1)


def row_index():
    return lax.broadcasted_iota(jnp.int32, (8, LANES), 0)


def turn(x, shift, axis):
    shift = shift % x.shape[axis]
    return x if shift == 0 else pltpu.roll(x, shift, axis)


def west_of(tiles, lane):
    rolled = [turn(x, 1, 1) for x in tiles]
    return [jnp.where(lane == 0, rolled[c - 1], rolled[c]) for c in range(TILES)]


def east_of(tiles, lane):
    rolled = [turn(x, -1, 1) for x in tiles]
    return [jnp.where(lane == LANES - 1, rolled[(c + 1) % TILES], rolled[c]) for c in range(TILES)]


def span_of(group):
    return divmod(CHUNK * group, LANES)


def pick(x, where):
    return jnp.take_along_axis(x, where, axis=0, mode="promise_in_bounds")


def on_odd_row():
    return (lax.axis_index("lat") & 1) == 1


def halo_kernel(tracers, thickness, courant_y, inside, across, sem):
    odd = on_odd_row()
    copies = []
    for edge, (out, first) in enumerate(((inside, jnp.where(odd, 0, ROWS - 2)), (across, jnp.where(odd, ROWS - 2, 0)))):
        rows = pl.ds(first, 2)
        copies.append(pltpu.make_async_copy(tracers.at[:, rows], out.at[pl.ds(0, NTR)], sem.at[edge, 0]))
        copies.append(pltpu.make_async_copy(thickness.at[rows], out.at[THICK], sem.at[edge, 1]))
        copies.append(pltpu.make_async_copy(courant_y.at[rows], out.at[NORTH], sem.at[edge, 2]))
    for copy in copies:
        copy.start()
    for copy in copies:
        copy.wait()


def transport_kernel(part, *refs):
    if part == OUTER:
        tracers, thickness, courant_x, courant_y, inside, across, _, out, held, mx, ax, my, ay, fy, sem = refs
    else:
        tracers, thickness, courant_x, courant_y, _, out, held, mx, ax, my, ay, fy, sem = refs
    chunk = slots_to(False) if part == INNER else list(range(GROUPS))
    slots = slots_of(part)
    lane, row = lane_index(), row_index()
    view = held.reshape(NTR + 3, slots // part, part, TILES, LEVS, LANES)
    copies = []

    def bring(source, target):
        copies.append(pltpu.make_async_copy(source, target, sem.at[len(copies)]))

    for c in range(TILES):
        cut = pl.ds(LANES * c, LANES)
        runs = ((2, 12, 0, 0),) if part == INNER else ((0, 6, 2, 0), (10, 6, 0, 1))
        for first, size, at, run in runs:
            own, into = pl.ds(first, size), pl.ds(at, size)
            bring(tracers.at[:, own, :, cut], view.at[pl.ds(0, NTR), into, run, c])
            for array, source in ((THICK, thickness), (NORTH, courant_y), (EAST, courant_x)):
                bring(source.at[own, :, cut], view.at[array, into, run, c])
    for copy in copies:
        copy.start()
    if part == OUTER:

        def bring_halos(low, high):
            for c in range(TILES):
                cut = pl.ds(LANES * c, LANES)
                bring(low.at[pl.ds(0, NTR + 1), :, :, cut], view.at[pl.ds(0, NTR + 1), pl.ds(0, 2), 0, c])
                bring(high.at[:, :, :, cut], view.at[pl.ds(0, NTR + 2), pl.ds(6, 2), 1, c])
            return copies[-2 * TILES :]

        odd = on_odd_row()

        @pl.when(odd)
        def _():
            for copy in bring_halos(inside, across):
                copy.start()

        del copies[-2 * TILES :]
        halos = bring_halos(across, inside)

        @pl.when(jnp.logical_not(odd))
        def _():
            for copy in halos:
                copy.start()

    for g in range(GROUPS):
        out[g, pl.ds(REST, 8 * BLOCKS), :] = jnp.zeros((8 * BLOCKS, LANES), F32)
    for copy in copies:
        copy.wait()

    def rows_of(array, shift, c, l):
        start = (array * slots + (2 + shift) * part) * STEP + c * LEVS + l
        return held[pl.ds(start, 8, stride=STEP), :]

    def past(array, shift):
        return held[pl.ds((array * slots + 8 + (2 + shift) * part) * STEP, part * STEP), :]

    def place(l, c):
        return pl.ds((c * LEVS + l) * 8, 8)

    def faces(l, c, shift):
        return pl.ds((c * LEVS + l) * 16 + shift, 8)

    def keep_past(values):
        for run in range(part):
            fy[pl.ds(8 + run, STEP, stride=16), :] = values[run * STEP : (run + 1) * STEP]

    def factors(courant, before, after):
        mass = jnp.where(courant > 0, courant * before, courant * after)
        return mass, mass * jnp.where(courant > 0, 0.25 - 0.25 * courant, -0.25 - 0.25 * courant)

    for l in range(LEVS):
        thick = [rows_of(THICK, 0, c, l) for c in range(TILES)]
        west = west_of(thick, lane)
        for c in range(TILES):
            mx[place(l, c), :], ax[place(l, c), :] = factors(rows_of(EAST, 0, c, l), west[c], thick[c])
            courant = rows_of(NORTH, 0, c, l)
            if part == OUTER:
                courant = jnp.where((row > 0) | (lax.axis_index("lat") > 0), courant, 0.0)
            my[place(l, c), :], ay[place(l, c), :] = factors(courant, rows_of(THICK, -1, c, l), thick[c])
    past_mass, past_tilt = factors(past(NORTH, 0), past(THICK, -1), past(THICK, 0))

    def air():
        keep_past(past_mass)
        for l in range(LEVS):
            for c in range(TILES):
                fy[faces(l, c, 0), :] = my[place(l, c), :]
        tiles = []
        for l in range(LEVS):
            flux = [mx[place(l, c), :] for c in range(TILES)]
            flux_e = east_of(flux, lane)
            tiles.append(
                [
                    rows_of(THICK, 0, c, l) + (flux[c] - flux_e[c]) + (my[place(l, c), :] - fy[faces(l, c, part), :])
                    for c in range(TILES)
                ]
            )
        return tiles

    def tracer(array):
        past_q = [past(array, shift) for shift in (-2, -1, 0, 1)]
        up = past_mass > 0
        value = jnp.where(up, past_q[1], past_q[2])
        rise = jnp.where(up, past_q[2] - past_q[0], past_q[3] - past_q[1])
        keep_past(past_mass * value + past_tilt * rise)
        tiles = []
        for l in range(LEVS):
            q = [rows_of(array, 0, c, l) for c in range(TILES)]
            qw = west_of(q, lane)
            qe = east_of(q, lane)
            d = [qe[c] - qw[c] for c in range(TILES)]
            dw = west_of(d, lane)
            flux = []
            for c in range(TILES):
                mass = mx[place(l, c), :]
                up = mass > 0
                flux.append(mass * jnp.where(up, qw[c], q[c]) + ax[place(l, c), :] * jnp.where(up, dw[c], d[c]))
            flux_e = east_of(flux, lane)
            now = []
            for c in range(TILES):
                mass = my[place(l, c), :]
                up = mass > 0
                q2, q1, q3 = (rows_of(array, shift, c, l) for shift in (-2, -1, 1))
                value = jnp.where(up, q1, q[c])
                rise = jnp.where(up, q[c] - q2, q3 - q1)
                flux_y = mass * value + ay[place(l, c), :] * rise
                fy[faces(l, c, 0), :] = flux_y
                now.append(rows_of(THICK, 0, c, l) * q[c] + (flux[c] - flux_e[c]) + flux_y)
            tiles.append(now)
        return [[tiles[l][c] - fy[faces(l, c, part), :] for c in range(TILES)] for l in range(LEVS)]

    def two(pair, _):
        first = tracer(2 * pair)
        send_block(pair, first, tracer(2 * pair + 1))
        return 0

    def send_block(pair, first, second):
        block = REST
        for l in range(LEVS):
            slot = l * 4 + pair
            for g in range(GROUPS):
                pack(g, l, pl.multiple_of((pair * LEVS + l) * 8, 8), block, slot, first, second)

    def pack(g, l, at, block, slot, first, second):
        t, o = span_of(g)
        a = turn(first[l][t], -o, 1)
        b = turn(second[l][t], CHUNK - o, 1)
        if o + CHUNK > LANES:
            a = jnp.where(lane < LANES - o, a, turn(first[l][t + 1], -o, 1))
            lon = jnp.where(lane >= CHUNK, lane - CHUNK, lane + (LANES - CHUNK))
            b = jnp.where(lon < LANES - o, b, turn(second[l][t + 1], CHUNK - o, 1))
        out[chunk[g], pl.ds(at, 8), :] = jnp.where(lane < CHUNK, a, b)
        moved = pltpu.roll(b, slot * 16, 1)
        last = pl.ds(block, 8)
        out[chunk[g], last, :] = jnp.where((lane >> 4) == slot, moved, out[chunk[g], last, :])

    lax.fori_loop(0, PAIRS - 1, two, 0)
    first, second = tracer(NTR - 1), air()
    for l in range(LEVS):
        for g in range(GROUPS):
            pack(g, l, ((PAIRS - 1) * LEVS + l) * 8, REST + 8, l * 4, first, second)


def target_kernel(index, offset, phase, inner, outer):
    lane = lane_index()
    blank = jnp.zeros((8, LANES - CHUNK), F32)
    for ref in (inner, outer):
        ref[pl.ds(0, 16), :] = jnp.zeros((16, LANES), F32)
    for n in range(2 * GROUPS - 1):
        at = (n + 1) * 16
        main, tail = [], []
        for h in range(2):
            rows = pl.ds(8 * h, 8)
            part = (offset[n, rows, :].astype(F32) + phase[n, rows, :]) * (1.0 / 32.0)
            x = jnp.concatenate([index[n, rows, :].astype(F32) + part, blank], 1)
            moved = turn(x, CHUNK, 1)
            main.append(jnp.where(lane < CHUNK, x, moved))
            last = jnp.where(lane < 16, moved, 0.0)
            last = last + turn(last, 16, 1)
            tail.append(last + turn(last, 32, 1))
        other = [turn(x, 64, 1) for x in tail]
        inner[pl.ds(at, 4), :] = main[0][4:]
        inner[pl.ds(at + 4, 4), :] = main[1][:4]
        inner[pl.ds(at + 8, 8), :] = turn(tail[0], 4, 0) + other[1]
        outer[pl.ds(at, 4, stride=2), :] = main[0][:4]
        outer[pl.ds(at + 1, 4, stride=2), :] = main[1][4:]
        outer[pl.ds(at + 8, 2, stride=2), :] = (tail[0] + turn(other[0], -2, 0))[:2]
        outer[pl.ds(at + 9, 2, stride=2), :] = (tail[1] + turn(other[1], -2, 0))[4:6]


def remap_rows(data, table, out):
    lane, row = lane_index(), row_index()

    def targets(tile):
        found = []
        for parity in range(2):
            for half in range(2):
                start = (parity + 16 * half) * 16 + tile
                position = table[pl.ds(start, 8, stride=32), :]
                s = jnp.minimum(position.astype(jnp.int32), 2 * GROUPS - 1)
                f = position - s.astype(F32)
                square = f * f * 0.5
                cubic = 3.0 * square - f * f * f
                found.append(((s >> 1) & 7, s >= 16, (s & 1) == 1, f, square, cubic))
        return found

    def columns(even, odd, found):
        back = [turn(x, 1, 0) for x in odd]
        before = [jnp.where(row == 0, even[0], back[0]), jnp.where(row == 0, back[0], back[1])]
        left = [0.5 * (before[i] + even[i]) for i in range(2)]
        ahead = [turn(x, -1, 0) for x in left]
        right = [jnp.where(row == 7, ahead[1], ahead[0]), jnp.where(row == 7, odd[1], ahead[1])]
        pair = [even[i] + odd[i] for i in range(2)]
        run = list(pair)
        for shift in (1, 2, 4):
            run = [x + jnp.where(row >= shift, turn(x, shift, 0), 0.0) for x in run]
        half_sum = jnp.broadcast_to(run[0][7:8], (8, LANES))
        total = half_sum + run[1][7:8]
        below = [run[0] - pair[0], (run[1] - pair[1]) + half_sum]
        edges = []
        for where, high, is_odd, f, square, cubic in found:
            le, ri, ev, od, be = (
                jnp.where(high, pick(x[1], where), pick(x[0], where)) for x in (left, right, even, odd, below)
            )
            middle = 0.5 * (ev + od)
            lo = jnp.where(is_odd, middle, le)
            hi = jnp.where(is_odd, ri, middle)
            m = jnp.where(is_odd, od, ev)
            base = be + jnp.where(is_odd, ev, 0.0)
            edges.append(base + lo * f + (hi - lo) * square + ((m + m) - (lo + hi)) * cubic)
        ev0, ev1, od0, od1 = edges
        next0, next1 = turn(ev0, -1, 0), turn(ev1, -1, 0)
        new_even = [od0 - ev0, od1 - ev1]
        new_odd = [jnp.where(row == 7, next1, next0) - od0, jnp.where(row == 7, total, next1) - od1]
        return new_even, new_odd

    def span(start, half):
        return pl.ds(start + half * 8 * DEPTH, 8, stride=DEPTH)

    def main(tile, _):
        found = targets(tile)
        for pair in range(PAIRS):
            at = [(pair * LEVS + l) * 8 + tile for l in range(LEVS)]
            even, odd = ([data[span(at[l], half), :] for half in range(2)] for l in range(LEVS))
            new = columns(even, odd, found)
            for l in range(LEVS):
                for half in range(2):
                    out[span(at[l], half), :] = new[l][half]
        return 0

    lax.fori_loop(0, 8, main, 0)

    def tail(tile, _):
        found = targets(8 + tile)
        for block in range(BLOCKS):
            at = [REST + 8 * block + tile, REST + 8 * block + tile + 4]
            a, b = ([data[span(at[i], half), :] for half in range(2)] for i in range(2))
            even = [jnp.where(lane < 64, a[half], turn(b[half], 64, 1)) for half in range(2)]
            odd = [jnp.where(lane < 64, turn(a[half], 64, 1), b[half]) for half in range(2)]
            even, odd = columns(even, odd, found)
            for half in range(2):
                out[span(at[0], half), :] = jnp.where(lane < 64, even[half], turn(odd[half], 64, 1))
                out[span(at[1], half), :] = jnp.where(lane < 64, turn(even[half], 64, 1), odd[half])
        return 0

    lax.fori_loop(0, 4, tail, 0)


def place_of(back):
    lev = lax.axis_index("lev")
    return lev >> 2, lev & 3, on_odd_row() != back


def slots_to(back):
    y, z, y_first = place_of(back)
    slots = []
    for g in range(GROUPS):
        j, k = ((g >> 2) - y) & 3, (g & 3) ^ z
        slots.append(jnp.where(y_first, 4 * j + k, 4 * k + j))
    return slots


def gather_chunks(back, given, target, sem):
    y, z, y_first = place_of(back)
    copies = []
    for a in range(4):
        for b in range(4):
            j, k = jnp.where(y_first, a, b), jnp.where(y_first, b, a)
            place = ((y - j) & 3) * 4 + (z ^ k)
            copies.append(pltpu.make_async_copy(given[b].at[a], target(place), sem.at[4 * a + b]))
    for copy in copies:
        copy.start()
    for copy in copies:
        copy.wait()


def remap_kernel(*refs):
    given, (table, out, data, new, sem) = refs[:4], refs[4:]

    def rows(place):
        return pl.ds(pl.multiple_of(place * DEPTH, 8), DEPTH)

    gather_chunks(False, given, lambda place: data.at[rows(place)], sem)
    remap_rows(data, table, new)
    copies = []
    for g, slot in enumerate(slots_to(True)):
        copies.append(pltpu.make_async_copy(new.at[rows(g)], out.at[slot], sem.at[g]))
    for copy in copies:
        copy.start()
    for copy in copies:
        copy.wait()


def collect_kernel(part, *refs):
    if part == OUTER:
        data, _, out, flat, sem = refs
    else:
        given, (out, data, flat, sem) = refs[:4], refs[-4:]
        gather_chunks(True, given, lambda place: data.at[place], sem)
    lane = lane_index()

    def unpack(pair, at, block, slot):
        for l in range(LEVS):
            pieces = []
            for g in range(GROUPS):
                _, o = span_of(g)
                main = data[g, at(l), :]
                tail = pltpu.roll(data[g, pl.ds(block, 8), :], LANES - (l * 4 + slot) * 16, 1)
                mixed = jnp.where(lane < 16, tail, main)
                pieces.append((turn(main, o, 1), turn(mixed, o - CHUNK, 1)))
            for second in range(2):
                for c in range(TILES):
                    value = None
                    for g in range(GROUPS):
                        start = CHUNK * g - LANES * c
                        if start >= LANES or start + CHUNK <= 0:
                            continue
                        piece = pieces[g][second]
                        value = piece if value is None else jnp.where(lane >= start, piece, value)
                    flat[pl.ds((2 * pair + second) * 8 * STEP + c * LEVS + l, 8, stride=STEP), :] = value

    def one(pair, _):
        unpack(pair, lambda l: pl.ds(pl.multiple_of((pair * LEVS + l) * 8, 8), 8), REST, pair)
        return 0

    lax.fori_loop(0, PAIRS - 1, one, 0)
    unpack(PAIRS - 1, lambda l: pl.ds(((PAIRS - 1) * LEVS + l) * 8, 8), REST + 8, 0)
    view = flat.reshape(FIELDS, 8 // part, part, TILES, LEVS, LANES)
    copies = []
    for c in range(TILES):
        cut = pl.ds(LANES * c, LANES)
        for run, first in enumerate((4,) if part == INNER else (0, 12)):
            target = out.at[:, pl.ds(first, 8 // part), :, cut]
            copies.append(pltpu.make_async_copy(view.at[:, :, run, c], target, sem.at[len(copies)]))
    for copy in copies:
        copy.start()
    for copy in copies:
        copy.wait()


ANYWHERE = pl.BlockSpec(memory_space=pl.ANY)
IN_HBM = pl.BlockSpec(memory_space=pltpu.HBM)
IN_VMEM = pl.BlockSpec(memory_space=pltpu.VMEM)
PARAMS = pltpu.CompilerParams(vmem_limit_bytes=VMEM_LIMIT)


def transport(part, *given):
    factor = pltpu.VMEM((STEP * 8, LANES), F32)
    return pl.pallas_call(
        functools.partial(transport_kernel, part),
        out_shape=jax.ShapeDtypeStruct((GROUPS, DEPTH, LANES), F32),
        in_specs=[IN_HBM] * 4 + [IN_HBM if part == INNER else ANYWHERE] * (len(given) - 4),
        out_specs=IN_VMEM,
        scratch_shapes=[
            pltpu.VMEM(((NTR + 3) * slots_of(part) * STEP, LANES), F32),
            factor,
            factor,
            factor,
            factor,
            pltpu.VMEM((STEP * 16, LANES), F32),
            pltpu.SemaphoreType.DMA((10 * TILES,)),
        ],
        compiler_params=PARAMS,
    )(*given)


def remap_outer(data, table):
    return pl.pallas_call(
        remap_rows,
        out_shape=jax.ShapeDtypeStruct((GROUPS * DEPTH, LANES), F32),
        in_specs=[IN_VMEM] * 2,
        out_specs=IN_VMEM,
        compiler_params=PARAMS,
    )(data.reshape(GROUPS * DEPTH, LANES), table).reshape(GROUPS, DEPTH, LANES)


def remap_inner(given, table):
    held = pltpu.VMEM((GROUPS * DEPTH, LANES), F32)
    return pl.pallas_call(
        remap_kernel,
        out_shape=jax.ShapeDtypeStruct((GROUPS, DEPTH, LANES), F32),
        in_specs=[ANYWHERE] * 4 + [IN_VMEM],
        out_specs=ANYWHERE,
        scratch_shapes=[held, held, pltpu.SemaphoreType.DMA((GROUPS,))],
        compiler_params=PARAMS,
    )(*given, table)


def collect(part, given, *result):
    scratch = [pltpu.VMEM((FIELDS * 8 * STEP, LANES), F32), pltpu.SemaphoreType.DMA((2 * TILES,))]
    if part == INNER:
        scratch = [pltpu.VMEM((GROUPS, DEPTH, LANES), F32)] + scratch
    return pl.pallas_call(
        functools.partial(collect_kernel, part),
        out_shape=jax.ShapeDtypeStruct((FIELDS, ROWS, LEVS, LONS), F32),
        in_specs=[ANYWHERE] * 4 if part == INNER else [IN_VMEM, ANYWHERE],
        out_specs=ANYWHERE,
        scratch_shapes=scratch,
        input_output_aliases={} if part == INNER else {1: 0},
        compiler_params=PARAMS,
    )(*given, *result)


def exchange(data):
    return lax.all_to_all(data, "lev", split_axis=0, concat_axis=0, tiled=True)


def hop(blocks, evens_along_z):
    lats = lax.axis_size("lat")
    moved = {}
    for a in (2, 3, 1):
        pairs = []
        for lat in range(lats):
            along_z = (lat % 2 == 0) == evens_along_z
            for lev in range(GROUPS):
                target = lev ^ a if along_z else (lev + 4 * a) % GROUPS
                pairs.append((lat * GROUPS + lev, lat * GROUPS + target))
        moved[a] = lax.ppermute(blocks[a], ("lat", "lev"), pairs)
    return [blocks[0]] + [moved[a] for a in range(1, 4)]


def first_hop(data, back=False):
    return hop([data[4 * a : 4 * a + 4] for a in range(4)], not back)


def second_hop(rows, back=False):
    return hop([jnp.stack([rows[a][b] for a in range(4)]) for b in range(4)], back)


def after(values, *others):
    return lax.optimization_barrier((values, others))[0]


def shards(tracers, thickness, courant_x, courant_y, level_index, level_offset, level_phase):
    own = [pltpu.with_memory_space_constraint(x, pltpu.HBM) for x in (tracers, thickness, courant_x, courant_y)]
    rim = pltpu.HBM((NTR + 2, 2, LEVS, LONS), F32)
    inside, across = pl.pallas_call(
        halo_kernel,
        out_shape=(rim, rim),
        in_specs=[IN_HBM] * 3,
        out_specs=(IN_VMEM, IN_VMEM),
        scratch_shapes=[pltpu.SemaphoreType.DMA((2, 3))],
    )(own[0], own[1], own[3])
    lats = lax.axis_size("lat")
    to_core = [(i, i ^ 1) for i in range(lats)]
    to_chip = [(i, i + 1) for i in range(1, lats - 1, 2)] + [(i + 1, i) for i in range(1, lats - 1, 2)]
    first = pltpu.with_memory_space_constraint(inside, pltpu.HBM)
    inside, across = lax.ppermute(inside, "lat", to_core), lax.ppermute(across, "lat", to_chip)
    inner = transport(INNER, *own, first)
    table = jax.ShapeDtypeStruct((2 * GROUPS * 16, LANES), F32)
    inner_table, outer_table = pl.pallas_call(
        target_kernel,
        out_shape=(table, table),
        in_specs=[IN_VMEM] * 3,
        out_specs=(IN_VMEM, IN_VMEM),
        compiler_params=PARAMS,
    )(level_index, level_offset, level_phase)
    outer = transport(OUTER, *own, inside, across, outer_table)
    inner = first_hop(inner)
    inner = second_hop(after(inner, outer))
    outer = exchange(after(outer, inner[2]))
    inner = remap_inner(inner, inner_table)
    inner = first_hop(inner, True)
    outer = remap_outer(after(outer, inner), outer_table)
    inner = second_hop(inner, True)
    outer = exchange(after(outer, inner[2]))
    return collect(OUTER, [outer], collect(INNER, inner))


def solution(mesh):
    in_specs = (
        P(None, "lat", "lev", None),
        P("lat", "lev", None),
        P("lat", "lev", None),
        P("lat", "lev", None),
        P(None, "lat", "lev"),
        P(None, "lat", "lev"),
        P(None, "lat", "lev"),
    )
    out_specs = P(None, "lat", "lev", None)
    return jax.shard_map(shards, mesh=mesh, in_specs=in_specs, out_specs=out_specs, check_vma=False)
```

```python
import functools

import jax
import jax.numpy as jnp
from jax import lax
from jax.experimental import pallas as pl
from jax.experimental.pallas import tpu as pltpu
from jax.sharding import PartitionSpec as P

F32 = jnp.float32
NTR = 9
FIELDS = NTR + 1
PAIRS = FIELDS // 2
ROWS = 16
LEVS = 2
LANES = 128
TILES = 9
LONS = LANES * TILES
CHUNK = 72
GROUPS = 16
STEP = TILES * LEVS
VMEM_LIMIT = 40 * 1024 * 1024

INNER, OUTER = 1, 2

REST = PAIRS * LEVS * 8
BLOCKS = (PAIRS + 3) // 4
DEPTH = REST + BLOCKS * 8

THICK, NORTH, EAST = NTR, NTR + 1, NTR + 2


def slots_of(part):
    return 8 + 4 * part


def lane_index():
    return lax.broadcasted_iota(jnp.int32, (8, LANES), 1)


def row_index():
    return lax.broadcasted_iota(jnp.int32, (8, LANES), 0)


def turn(x, shift, axis):
    shift = shift % x.shape[axis]
    return x if shift == 0 else pltpu.roll(x, shift, axis)


def west_of(tiles, lane):
    rolled = [turn(x, 1, 1) for x in tiles]
    return [jnp.where(lane == 0, rolled[c - 1], rolled[c]) for c in range(TILES)]


def east_of(tiles, lane):
    rolled = [turn(x, -1, 1) for x in tiles]
    return [jnp.where(lane == LANES - 1, rolled[(c + 1) % TILES], rolled[c]) for c in range(TILES)]


def span_of(group):
    return divmod(CHUNK * group, LANES)


def pick(x, where):
    return jnp.take_along_axis(x, where, axis=0, mode="promise_in_bounds")


def on_odd_row():
    return (lax.axis_index("lat") & 1) == 1


def halo_kernel(tracers, thickness, courant_y, inside, across, sem):
    odd = on_odd_row()
    copies = []
    for edge, (out, first) in enumerate(((inside, jnp.where(odd, 0, ROWS - 2)), (across, jnp.where(odd, ROWS - 2, 0)))):
        rows = pl.ds(first, 2)
        copies.append(pltpu.make_async_copy(tracers.at[:, rows], out.at[pl.ds(0, NTR)], sem.at[edge, 0]))
        copies.append(pltpu.make_async_copy(thickness.at[rows], out.at[THICK], sem.at[edge, 1]))
        copies.append(pltpu.make_async_copy(courant_y.at[rows], out.at[NORTH], sem.at[edge, 2]))
    for copy in copies:
        copy.start()
    for copy in copies:
        copy.wait()


def transport_kernel(part, *refs):
    if part == OUTER:
        tracers, thickness, courant_x, courant_y, inside, across, _, out, held, mx, ax, my, ay, fy, sem = refs
    else:
        tracers, thickness, courant_x, courant_y, _, out, held, mx, ax, my, ay, fy, sem = refs
    chunk = slots_to(False) if part == INNER else list(range(GROUPS))
    slots = slots_of(part)
    lane, row = lane_index(), row_index()
    view = held.reshape(NTR + 3, slots // part, part, TILES, LEVS, LANES)
    copies = []

    def bring(source, target):
        copies.append(pltpu.make_async_copy(source, target, sem.at[len(copies)]))

    for c in range(TILES):
        cut = pl.ds(LANES * c, LANES)
        runs = ((2, 12, 0, 0),) if part == INNER else ((0, 6, 2, 0), (10, 6, 0, 1))
        for first, size, at, run in runs:
            own, into = pl.ds(first, size), pl.ds(at, size)
            bring(tracers.at[:, own, :, cut], view.at[pl.ds(0, NTR), into, run, c])
            for array, source in ((THICK, thickness), (NORTH, courant_y), (EAST, courant_x)):
                bring(source.at[own, :, cut], view.at[array, into, run, c])
    for copy in copies:
        copy.start()
    if part == OUTER:

        def bring_halos(low, high):
            for c in range(TILES):
                cut = pl.ds(LANES * c, LANES)
                bring(low.at[pl.ds(0, NTR + 1), :, :, cut], view.at[pl.ds(0, NTR + 1), pl.ds(0, 2), 0, c])
                bring(high.at[:, :, :, cut], view.at[pl.ds(0, NTR + 2), pl.ds(6, 2), 1, c])
            return copies[-2 * TILES :]

        odd = on_odd_row()

        @pl.when(odd)
        def _():
            for copy in bring_halos(inside, across):
                copy.start()

        del copies[-2 * TILES :]
        halos = bring_halos(across, inside)

        @pl.when(jnp.logical_not(odd))
        def _():
            for copy in halos:
                copy.start()

    for g in range(GROUPS):
        out[g, pl.ds(REST, 8 * BLOCKS), :] = jnp.zeros((8 * BLOCKS, LANES), F32)
    for copy in copies:
        copy.wait()

    def rows_of(array, shift, c, l):
        start = (array * slots + (2 + shift) * part) * STEP + c * LEVS + l
        return held[pl.ds(start, 8, stride=STEP), :]

    def past(array, shift):
        return held[pl.ds((array * slots + 8 + (2 + shift) * part) * STEP, part * STEP), :]

    def place(l, c):
        return pl.ds((c * LEVS + l) * 8, 8)

    def faces(l, c, shift):
        return pl.ds((c * LEVS + l) * 16 + shift, 8)

    def keep_past(values):
        for run in range(part):
            fy[pl.ds(8 + run, STEP, stride=16), :] = values[run * STEP : (run + 1) * STEP]

    def factors(courant, before, after):
        mass = jnp.where(courant > 0, courant * before, courant * after)
        return mass, mass * jnp.where(courant > 0, 0.25 - 0.25 * courant, -0.25 - 0.25 * courant)

    for l in range(LEVS):
        thick = [rows_of(THICK, 0, c, l) for c in range(TILES)]
        west = west_of(thick, lane)
        for c in range(TILES):
            mx[place(l, c), :], ax[place(l, c), :] = factors(rows_of(EAST, 0, c, l), west[c], thick[c])
            courant = rows_of(NORTH, 0, c, l)
            if part == OUTER:
                courant = jnp.where((row > 0) | (lax.axis_index("lat") > 0), courant, 0.0)
            my[place(l, c), :], ay[place(l, c), :] = factors(courant, rows_of(THICK, -1, c, l), thick[c])
    past_mass, past_tilt = factors(past(NORTH, 0), past(THICK, -1), past(THICK, 0))

    def air():
        keep_past(past_mass)
        for l in range(LEVS):
            for c in range(TILES):
                fy[faces(l, c, 0), :] = my[place(l, c), :]
        tiles = []
        for l in range(LEVS):
            flux = [mx[place(l, c), :] for c in range(TILES)]
            flux_e = east_of(flux, lane)
            tiles.append(
                [
                    rows_of(THICK, 0, c, l) + (flux[c] - flux_e[c]) + (my[place(l, c), :] - fy[faces(l, c, part), :])
                    for c in range(TILES)
                ]
            )
        return tiles

    def tracer(array):
        past_q = [past(array, shift) for shift in (-2, -1, 0, 1)]
        up = past_mass > 0
        value = jnp.where(up, past_q[1], past_q[2])
        rise = jnp.where(up, past_q[2] - past_q[0], past_q[3] - past_q[1])
        keep_past(past_mass * value + past_tilt * rise)
        tiles = []
        for l in range(LEVS):
            q = [rows_of(array, 0, c, l) for c in range(TILES)]
            qw = west_of(q, lane)
            qe = east_of(q, lane)
            d = [qe[c] - qw[c] for c in range(TILES)]
            dw = west_of(d, lane)
            flux = []
            for c in range(TILES):
                mass = mx[place(l, c), :]
                up = mass > 0
                flux.append(mass * jnp.where(up, qw[c], q[c]) + ax[place(l, c), :] * jnp.where(up, dw[c], d[c]))
            flux_e = east_of(flux, lane)
            now = []
            for c in range(TILES):
                mass = my[place(l, c), :]
                up = mass > 0
                q2, q1, q3 = (rows_of(array, shift, c, l) for shift in (-2, -1, 1))
                value = jnp.where(up, q1, q[c])
                rise = jnp.where(up, q[c] - q2, q3 - q1)
                flux_y = mass * value + ay[place(l, c), :] * rise
                fy[faces(l, c, 0), :] = flux_y
                now.append(rows_of(THICK, 0, c, l) * q[c] + (flux[c] - flux_e[c]) + flux_y)
            tiles.append(now)
        return [[tiles[l][c] - fy[faces(l, c, part), :] for c in range(TILES)] for l in range(LEVS)]

    def two(pair, _):
        first = tracer(2 * pair)
        send_block(pair, first, tracer(2 * pair + 1))
        return 0

    def send_block(pair, first, second):
        block = REST
        for l in range(LEVS):
            slot = l * 4 + pair
            for g in range(GROUPS):
                pack(g, l, pl.multiple_of((pair * LEVS + l) * 8, 8), block, slot, first, second)

    def pack(g, l, at, block, slot, first, second):
        t, o = span_of(g)
        a = turn(first[l][t], -o, 1)
        b = turn(second[l][t], CHUNK - o, 1)
        if o + CHUNK > LANES:
            a = jnp.where(lane < LANES - o, a, turn(first[l][t + 1], -o, 1))
            lon = jnp.where(lane >= CHUNK, lane - CHUNK, lane + (LANES - CHUNK))
            b = jnp.where(lon < LANES - o, b, turn(second[l][t + 1], CHUNK - o, 1))
        out[chunk[g], pl.ds(at, 8), :] = jnp.where(lane < CHUNK, a, b)
        moved = pltpu.roll(b, slot * 16, 1)
        last = pl.ds(block, 8)
        out[chunk[g], last, :] = jnp.where((lane >> 4) == slot, moved, out[chunk[g], last, :])

    lax.fori_loop(0, PAIRS - 1, two, 0)
    first, second = tracer(NTR - 1), air()
    for l in range(LEVS):
        for g in range(GROUPS):
            pack(g, l, ((PAIRS - 1) * LEVS + l) * 8, REST + 8, l * 4, first, second)


def target_kernel(index, offset, phase, inner, outer):
    lane = lane_index()
    blank = jnp.zeros((8, LANES - CHUNK), F32)
    for ref in (inner, outer):
        ref[pl.ds(0, 16), :] = jnp.zeros((16, LANES), F32)
    for n in range(2 * GROUPS - 1):
        at = (n + 1) * 16
        main, tail = [], []
        for h in range(2):
            rows = pl.ds(8 * h, 8)
            part = (offset[n, rows, :].astype(F32) + phase[n, rows, :]) * (1.0 / 32.0)
            x = jnp.concatenate([index[n, rows, :].astype(F32) + part, blank], 1)
            moved = turn(x, CHUNK, 1)
            main.append(jnp.where(lane < CHUNK, x, moved))
            last = jnp.where(lane < 16, moved, 0.0)
            last = last + turn(last, 16, 1)
            tail.append(last + turn(last, 32, 1))
        other = [turn(x, 64, 1) for x in tail]
        inner[pl.ds(at, 4), :] = main[0][4:]
        inner[pl.ds(at + 4, 4), :] = main[1][:4]
        inner[pl.ds(at + 8, 8), :] = turn(tail[0], 4, 0) + other[1]
        outer[pl.ds(at, 4, stride=2), :] = main[0][:4]
        outer[pl.ds(at + 1, 4, stride=2), :] = main[1][4:]
        outer[pl.ds(at + 8, 2, stride=2), :] = (tail[0] + turn(other[0], -2, 0))[:2]
        outer[pl.ds(at + 9, 2, stride=2), :] = (tail[1] + turn(other[1], -2, 0))[4:6]


def remap_rows(data, table, out):
    lane, row = lane_index(), row_index()

    def targets(tile):
        found = []
        for parity in range(2):
            for half in range(2):
                start = (parity + 16 * half) * 16 + tile
                position = table[pl.ds(start, 8, stride=32), :]
                s = jnp.minimum(position.astype(jnp.int32), 2 * GROUPS - 1)
                f = position - s.astype(F32)
                square = f * f * 0.5
                cubic = 3.0 * square - f * f * f
                found.append(((s >> 1) & 7, s >= 16, (s & 1) == 1, f, square, cubic))
        return found

    def columns(even, odd, found):
        back = [turn(x, 1, 0) for x in odd]
        before = [jnp.where(row == 0, even[0], back[0]), jnp.where(row == 0, back[0], back[1])]
        left = [0.5 * (before[i] + even[i]) for i in range(2)]
        ahead = [turn(x, -1, 0) for x in left]
        right = [jnp.where(row == 7, ahead[1], ahead[0]), jnp.where(row == 7, odd[1], ahead[1])]
        pair = [even[i] + odd[i] for i in range(2)]
        run = list(pair)
        for shift in (1, 2, 4):
            run = [x + jnp.where(row >= shift, turn(x, shift, 0), 0.0) for x in run]
        half_sum = jnp.broadcast_to(run[0][7:8], (8, LANES))
        total = half_sum + run[1][7:8]
        below = [run[0] - pair[0], (run[1] - pair[1]) + half_sum]
        edges = []
        for where, high, is_odd, f, square, cubic in found:
            le, ri, ev, od, be = (
                jnp.where(high, pick(x[1], where), pick(x[0], where)) for x in (left, right, even, odd, below)
            )
            middle = 0.5 * (ev + od)
            lo = jnp.where(is_odd, middle, le)
            hi = jnp.where(is_odd, ri, middle)
            m = jnp.where(is_odd, od, ev)
            base = be + jnp.where(is_odd, ev, 0.0)
            edges.append(base + lo * f + (hi - lo) * square + ((m + m) - (lo + hi)) * cubic)
        ev0, ev1, od0, od1 = edges
        next0, next1 = turn(ev0, -1, 0), turn(ev1, -1, 0)
        new_even = [od0 - ev0, od1 - ev1]
        new_odd = [jnp.where(row == 7, next1, next0) - od0, jnp.where(row == 7, total, next1) - od1]
        return new_even, new_odd

    def span(start, half):
        return pl.ds(start + half * 8 * DEPTH, 8, stride=DEPTH)

    def main(tile, _):
        found = targets(tile)
        for pair in range(PAIRS):
            at = [(pair * LEVS + l) * 8 + tile for l in range(LEVS)]
            even, odd = ([data[span(at[l], half), :] for half in range(2)] for l in range(LEVS))
            new = columns(even, odd, found)
            for l in range(LEVS):
                for half in range(2):
                    out[span(at[l], half), :] = new[l][half]
        return 0

    lax.fori_loop(0, 8, main, 0)

    def tail(tile, _):
        found = targets(8 + tile)
        for block in range(BLOCKS):
            at = [REST + 8 * block + tile, REST + 8 * block + tile + 4]
            a, b = ([data[span(at[i], half), :] for half in range(2)] for i in range(2))
            even = [jnp.where(lane < 64, a[half], turn(b[half], 64, 1)) for half in range(2)]
            odd = [jnp.where(lane < 64, turn(a[half], 64, 1), b[half]) for half in range(2)]
            even, odd = columns(even, odd, found)
            for half in range(2):
                out[span(at[0], half), :] = jnp.where(lane < 64, even[half], turn(odd[half], 64, 1))
                out[span(at[1], half), :] = jnp.where(lane < 64, turn(even[half], 64, 1), odd[half])
        return 0

    lax.fori_loop(0, 4, tail, 0)


def place_of(back):
    lev = lax.axis_index("lev")
    return lev >> 2, lev & 3, on_odd_row() != back


def slots_to(back):
    y, z, y_first = place_of(back)
    slots = []
    for g in range(GROUPS):
        j, k = ((g >> 2) - y) & 3, (g & 3) ^ z
        slots.append(jnp.where(y_first, 4 * j + k, 4 * k + j))
    return slots


def gather_chunks(back, given, target, sem):
    y, z, y_first = place_of(back)
    copies = []
    for a in range(4):
        for b in range(4):
            j, k = jnp.where(y_first, a, b), jnp.where(y_first, b, a)
            place = ((y - j) & 3) * 4 + (z ^ k)
            copies.append(pltpu.make_async_copy(given[b].at[a], target(place), sem.at[4 * a + b]))
    for copy in copies:
        copy.start()
    for copy in copies:
        copy.wait()


def remap_kernel(*refs):
    given, (table, out, data, new, sem) = refs[:4], refs[4:]

    def rows(place):
        return pl.ds(pl.multiple_of(place * DEPTH, 8), DEPTH)

    gather_chunks(False, given, lambda place: data.at[rows(place)], sem)
    remap_rows(data, table, new)
    copies = []
    for g, slot in enumerate(slots_to(True)):
        copies.append(pltpu.make_async_copy(new.at[rows(g)], out.at[slot], sem.at[g]))
    for copy in copies:
        copy.start()
    for copy in copies:
        copy.wait()


def collect_kernel(part, *refs):
    if part == OUTER:
        data, _, out, flat, sem = refs
    else:
        given, (out, data, flat, sem) = refs[:4], refs[-4:]
        gather_chunks(True, given, lambda place: data.at[place], sem)
    lane = lane_index()

    def unpack(pair, at, block, slot):
        for l in range(LEVS):
            pieces = []
            for g in range(GROUPS):
                _, o = span_of(g)
                main = data[g, at(l), :]
                tail = pltpu.roll(data[g, pl.ds(block, 8), :], LANES - (l * 4 + slot) * 16, 1)
                mixed = jnp.where(lane < 16, tail, main)
                pieces.append((turn(main, o, 1), turn(mixed, o - CHUNK, 1)))
            for second in range(2):
                for c in range(TILES):
                    value = None
                    for g in range(GROUPS):
                        start = CHUNK * g - LANES * c
                        if start >= LANES or start + CHUNK <= 0:
                            continue
                        piece = pieces[g][second]
                        value = piece if value is None else jnp.where(lane >= start, piece, value)
                    flat[pl.ds((2 * pair + second) * 8 * STEP + c * LEVS + l, 8, stride=STEP), :] = value

    def one(pair, _):
        unpack(pair, lambda l: pl.ds(pl.multiple_of((pair * LEVS + l) * 8, 8), 8), REST, pair)
        return 0

    lax.fori_loop(0, PAIRS - 1, one, 0)
    unpack(PAIRS - 1, lambda l: pl.ds(((PAIRS - 1) * LEVS + l) * 8, 8), REST + 8, 0)
    view = flat.reshape(FIELDS, 8 // part, part, TILES, LEVS, LANES)
    copies = []
    for c in range(TILES):
        cut = pl.ds(LANES * c, LANES)
        for run, first in enumerate((4,) if part == INNER else (0, 12)):
            target = out.at[:, pl.ds(first, 8 // part), :, cut]
            copies.append(pltpu.make_async_copy(view.at[:, :, run, c], target, sem.at[len(copies)]))
    for copy in copies:
        copy.start()
    for copy in copies:
        copy.wait()


ANYWHERE = pl.BlockSpec(memory_space=pl.ANY)
IN_HBM = pl.BlockSpec(memory_space=pltpu.HBM)
IN_VMEM = pl.BlockSpec(memory_space=pltpu.VMEM)
PARAMS = pltpu.CompilerParams(vmem_limit_bytes=VMEM_LIMIT)


def transport(part, *given):
    factor = pltpu.VMEM((STEP * 8, LANES), F32)
    return pl.pallas_call(
        functools.partial(transport_kernel, part),
        out_shape=jax.ShapeDtypeStruct((GROUPS, DEPTH, LANES), F32),
        in_specs=[IN_HBM] * 4 + [IN_HBM if part == INNER else ANYWHERE] * (len(given) - 4),
        out_specs=IN_VMEM,
        scratch_shapes=[
            pltpu.VMEM(((NTR + 3) * slots_of(part) * STEP, LANES), F32),
            factor,
            factor,
            factor,
            factor,
            pltpu.VMEM((STEP * 16, LANES), F32),
            pltpu.SemaphoreType.DMA((10 * TILES,)),
        ],
        compiler_params=PARAMS,
    )(*given)


def remap_outer(data, table):
    return pl.pallas_call(
        remap_rows,
        out_shape=jax.ShapeDtypeStruct((GROUPS * DEPTH, LANES), F32),
        in_specs=[IN_VMEM] * 2,
        out_specs=IN_VMEM,
        compiler_params=PARAMS,
    )(data.reshape(GROUPS * DEPTH, LANES), table).reshape(GROUPS, DEPTH, LANES)


def remap_inner(given, table):
    held = pltpu.VMEM((GROUPS * DEPTH, LANES), F32)
    return pl.pallas_call(
        remap_kernel,
        out_shape=jax.ShapeDtypeStruct((GROUPS, DEPTH, LANES), F32),
        in_specs=[ANYWHERE] * 4 + [IN_VMEM],
        out_specs=ANYWHERE,
        scratch_shapes=[held, held, pltpu.SemaphoreType.DMA((GROUPS,))],
        compiler_params=PARAMS,
    )(*given, table)


def collect(part, given, *result):
    scratch = [pltpu.VMEM((FIELDS * 8 * STEP, LANES), F32), pltpu.SemaphoreType.DMA((2 * TILES,))]
    if part == INNER:
        scratch = [pltpu.VMEM((GROUPS, DEPTH, LANES), F32)] + scratch
    return pl.pallas_call(
        functools.partial(collect_kernel, part),
        out_shape=jax.ShapeDtypeStruct((FIELDS, ROWS, LEVS, LONS), F32),
        in_specs=[ANYWHERE] * 4 if part == INNER else [IN_VMEM, ANYWHERE],
        out_specs=ANYWHERE,
        scratch_shapes=scratch,
        input_output_aliases={} if part == INNER else {1: 0},
        compiler_params=PARAMS,
    )(*given, *result)


def exchange(data):
    return lax.all_to_all(data, "lev", split_axis=0, concat_axis=0, tiled=True)


def hop(blocks, evens_along_z):
    lats = lax.axis_size("lat")
    moved = {}
    for a in (2, 3, 1):
        pairs = []
        for lat in range(lats):
            along_z = (lat % 2 == 0) == evens_along_z
            for lev in range(GROUPS):
                target = lev ^ a if along_z else (lev + 4 * a) % GROUPS
                pairs.append((lat * GROUPS + lev, lat * GROUPS + target))
        moved[a] = lax.ppermute(blocks[a], ("lat", "lev"), pairs)
    return [blocks[0]] + [moved[a] for a in range(1, 4)]


def first_hop(data, back=False):
    return hop([data[4 * a : 4 * a + 4] for a in range(4)], not back)


def second_hop(rows, back=False):
    return hop([jnp.stack([rows[a][b] for a in range(4)]) for b in range(4)], back)


def after(values, *others):
    return lax.optimization_barrier((values, others))[0]


def shards(tracers, thickness, courant_x, courant_y, level_index, level_offset, level_phase):
    own = [pltpu.with_memory_space_constraint(x, pltpu.HBM) for x in (tracers, thickness, courant_x, courant_y)]
    rim = pltpu.HBM((NTR + 2, 2, LEVS, LONS), F32)
    inside, across = pl.pallas_call(
        halo_kernel,
        out_shape=(rim, rim),
        in_specs=[IN_HBM] * 3,
        out_specs=(IN_VMEM, IN_VMEM),
        scratch_shapes=[pltpu.SemaphoreType.DMA((2, 3))],
    )(own[0], own[1], own[3])
    lats = lax.axis_size("lat")
    to_core = [(i, i ^ 1) for i in range(lats)]
    to_chip = [(i, i + 1) for i in range(1, lats - 1, 2)] + [(i + 1, i) for i in range(1, lats - 1, 2)]
    first = pltpu.with_memory_space_constraint(inside, pltpu.HBM)
    inside, across = lax.ppermute(inside, "lat", to_core), lax.ppermute(across, "lat", to_chip)
    inner = transport(INNER, *own, first)
    table = jax.ShapeDtypeStruct((2 * GROUPS * 16, LANES), F32)
    inner_table, outer_table = pl.pallas_call(
        target_kernel,
        out_shape=(table, table),
        in_specs=[IN_VMEM] * 3,
        out_specs=(IN_VMEM, IN_VMEM),
        compiler_params=PARAMS,
    )(level_index, level_offset, level_phase)
    outer = transport(OUTER, *own, inside, across, outer_table)
    inner = first_hop(inner)
    inner, outer = second_hop(after(inner, outer)), exchange(outer)
    inner = remap_inner(inner, inner_table)
    outer = remap_outer(after(outer, inner), outer_table)
    inner = first_hop(inner, True)
    inner, outer = second_hop(after(inner, outer), True), exchange(outer)
    return collect(OUTER, [outer], collect(INNER, inner))


def solution(mesh):
    in_specs = (
        P(None, "lat", "lev", None),
        P("lat", "lev", None),
        P("lat", "lev", None),
        P("lat", "lev", None),
        P(None, "lat", "lev"),
        P(None, "lat", "lev"),
        P(None, "lat", "lev"),
    )
    out_specs = P(None, "lat", "lev", None)
    return jax.shard_map(shards, mesh=mesh, in_specs=in_specs, out_specs=out_specs, check_vma=False)
```

```python
import functools

import jax
import jax.numpy as jnp
from jax import lax
from jax.experimental import pallas as pl
from jax.experimental.pallas import tpu as pltpu
from jax.sharding import PartitionSpec as P

F32 = jnp.float32
NTR = 9
FIELDS = NTR + 1
PAIRS = FIELDS // 2
ROWS = 16
LEVS = 2
LANES = 128
TILES = 9
LONS = LANES * TILES
CHUNK = 72
GROUPS = 16
STEP = TILES * LEVS
VMEM_LIMIT = 40 * 1024 * 1024

INNER, OUTER = 1, 2

REST = PAIRS * LEVS * 8
BLOCKS = (PAIRS + 3) // 4
DEPTH = REST + BLOCKS * 8

THICK, NORTH, EAST = NTR, NTR + 1, NTR + 2


def slots_of(part):
    return 8 + 4 * part


def lane_index():
    return lax.broadcasted_iota(jnp.int32, (8, LANES), 1)


def row_index():
    return lax.broadcasted_iota(jnp.int32, (8, LANES), 0)


def turn(x, shift, axis):
    shift = shift % x.shape[axis]
    return x if shift == 0 else pltpu.roll(x, shift, axis)


def west_of(tiles, lane):
    rolled = [turn(x, 1, 1) for x in tiles]
    return [jnp.where(lane == 0, rolled[c - 1], rolled[c]) for c in range(TILES)]


def east_of(tiles, lane):
    rolled = [turn(x, -1, 1) for x in tiles]
    return [jnp.where(lane == LANES - 1, rolled[(c + 1) % TILES], rolled[c]) for c in range(TILES)]


def span_of(group):
    return divmod(CHUNK * group, LANES)


def pick(x, where):
    return jnp.take_along_axis(x, where, axis=0, mode="promise_in_bounds")


def on_odd_row():
    return (lax.axis_index("lat") & 1) == 1


def halo_kernel(tracers, thickness, courant_y, inside, across, sem):
    odd = on_odd_row()
    copies = []
    for edge, (out, first) in enumerate(((inside, jnp.where(odd, 0, ROWS - 2)), (across, jnp.where(odd, ROWS - 2, 0)))):
        rows = pl.ds(first, 2)
        copies.append(pltpu.make_async_copy(tracers.at[:, rows], out.at[pl.ds(0, NTR)], sem.at[edge, 0]))
        row = jnp.where(first == 0, 0, ROWS - 1)
        copies.append(pltpu.make_async_copy(thickness.at[row], out.at[NTR, 0], sem.at[edge, 1]))
        copies.append(pltpu.make_async_copy(courant_y.at[row], out.at[NTR, 1], sem.at[edge, 2]))
    for copy in copies:
        copy.start()
    for copy in copies:
        copy.wait()


def transport_kernel(part, *refs):
    if part == OUTER:
        tracers, thickness, courant_x, courant_y, inside, across, _, out, held, mx, ax, my, ay, fy, sem = refs
    else:
        tracers, thickness, courant_x, courant_y, _, out, held, mx, ax, my, ay, fy, sem = refs
    chunk = slots_to(False) if part == INNER else list(range(GROUPS))
    slots = slots_of(part)
    lane, row = lane_index(), row_index()
    view = held.reshape(NTR + 3, slots // part, part, TILES, LEVS, LANES)
    copies = []

    def bring(source, target):
        copies.append(pltpu.make_async_copy(source, target, sem.at[len(copies)]))

    for c in range(TILES):
        cut = pl.ds(LANES * c, LANES)
        runs = ((2, 12, 0, 0),) if part == INNER else ((0, 6, 2, 0), (10, 6, 0, 1))
        for first, size, at, run in runs:
            own, into = pl.ds(first, size), pl.ds(at, size)
            bring(tracers.at[:, own, :, cut], view.at[pl.ds(0, NTR), into, run, c])
            for array, source in ((THICK, thickness), (NORTH, courant_y), (EAST, courant_x)):
                bring(source.at[own, :, cut], view.at[array, into, run, c])
    for copy in copies:
        copy.start()
    if part == OUTER:

        def bring_halos(low, high):
            for c in range(TILES):
                cut = pl.ds(LANES * c, LANES)
                bring(low.at[pl.ds(0, NTR), :, :, cut], view.at[pl.ds(0, NTR), pl.ds(0, 2), 0, c])
                bring(low.at[NTR, 0, :, cut], view.at[THICK, 1, 0, c])
                bring(high.at[pl.ds(0, NTR), :, :, cut], view.at[pl.ds(0, NTR), pl.ds(6, 2), 1, c])
                bring(high.at[NTR, :, :, cut], view.at[pl.ds(THICK, 2), 6, 1, c])
            return copies[-4 * TILES :]

        odd = on_odd_row()

        @pl.when(odd)
        def _():
            for copy in bring_halos(inside, across):
                copy.start()

        del copies[-4 * TILES :]
        halos = bring_halos(across, inside)

        @pl.when(jnp.logical_not(odd))
        def _():
            for copy in halos:
                copy.start()

    for g in range(GROUPS):
        out[g, pl.ds(REST, 8 * BLOCKS), :] = jnp.zeros((8 * BLOCKS, LANES), F32)
    for copy in copies:
        copy.wait()

    def rows_of(array, shift, c, l):
        start = (array * slots + (2 + shift) * part) * STEP + c * LEVS + l
        return held[pl.ds(start, 8, stride=STEP), :]

    def past(array, shift):
        return held[pl.ds((array * slots + 8 + (2 + shift) * part) * STEP, part * STEP), :]

    def place(l, c):
        return pl.ds((c * LEVS + l) * 8, 8)

    def faces(l, c, shift):
        return pl.ds((c * LEVS + l) * 16 + shift, 8)

    def keep_past(values):
        for run in range(part):
            fy[pl.ds(8 + run, STEP, stride=16), :] = values[run * STEP : (run + 1) * STEP]

    def factors(courant, before, after):
        mass = jnp.where(courant > 0, courant * before, courant * after)
        return mass, mass * jnp.where(courant > 0, 0.25 - 0.25 * courant, -0.25 - 0.25 * courant)

    for l in range(LEVS):
        thick = [rows_of(THICK, 0, c, l) for c in range(TILES)]
        west = west_of(thick, lane)
        for c in range(TILES):
            mx[place(l, c), :], ax[place(l, c), :] = factors(rows_of(EAST, 0, c, l), west[c], thick[c])
            courant = rows_of(NORTH, 0, c, l)
            if part == OUTER:
                courant = jnp.where((row > 0) | (lax.axis_index("lat") > 0), courant, 0.0)
            my[place(l, c), :], ay[place(l, c), :] = factors(courant, rows_of(THICK, -1, c, l), thick[c])
    past_mass, past_tilt = factors(past(NORTH, 0), past(THICK, -1), past(THICK, 0))

    def air():
        keep_past(past_mass)
        for l in range(LEVS):
            for c in range(TILES):
                fy[faces(l, c, 0), :] = my[place(l, c), :]
        tiles = []
        for l in range(LEVS):
            flux = [mx[place(l, c), :] for c in range(TILES)]
            flux_e = east_of(flux, lane)
            tiles.append(
                [
                    rows_of(THICK, 0, c, l) + (flux[c] - flux_e[c]) + (my[place(l, c), :] - fy[faces(l, c, part), :])
                    for c in range(TILES)
                ]
            )
        return tiles

    def tracer(array):
        past_q = [past(array, shift) for shift in (-2, -1, 0, 1)]
        up = past_mass > 0
        value = jnp.where(up, past_q[1], past_q[2])
        rise = jnp.where(up, past_q[2] - past_q[0], past_q[3] - past_q[1])
        keep_past(past_mass * value + past_tilt * rise)
        tiles = []
        for l in range(LEVS):
            q = [rows_of(array, 0, c, l) for c in range(TILES)]
            qw = west_of(q, lane)
            qe = east_of(q, lane)
            d = [qe[c] - qw[c] for c in range(TILES)]
            dw = west_of(d, lane)
            flux = []
            for c in range(TILES):
                mass = mx[place(l, c), :]
                up = mass > 0
                flux.append(mass * jnp.where(up, qw[c], q[c]) + ax[place(l, c), :] * jnp.where(up, dw[c], d[c]))
            flux_e = east_of(flux, lane)
            now = []
            for c in range(TILES):
                mass = my[place(l, c), :]
                up = mass > 0
                q2, q1, q3 = (rows_of(array, shift, c, l) for shift in (-2, -1, 1))
                value = jnp.where(up, q1, q[c])
                rise = jnp.where(up, q[c] - q2, q3 - q1)
                flux_y = mass * value + ay[place(l, c), :] * rise
                fy[faces(l, c, 0), :] = flux_y
                now.append(rows_of(THICK, 0, c, l) * q[c] + (flux[c] - flux_e[c]) + flux_y)
            tiles.append(now)
        return [[tiles[l][c] - fy[faces(l, c, part), :] for c in range(TILES)] for l in range(LEVS)]

    def two(pair, _):
        first = tracer(2 * pair)
        send_block(pair, first, tracer(2 * pair + 1))
        return 0

    def send_block(pair, first, second):
        block = REST
        for l in range(LEVS):
            slot = l * 4 + pair
            for g in range(GROUPS):
                pack(g, l, pl.multiple_of((pair * LEVS + l) * 8, 8), block, slot, first, second)

    def pack(g, l, at, block, slot, first, second):
        t, o = span_of(g)
        a = turn(first[l][t], -o, 1)
        b = turn(second[l][t], CHUNK - o, 1)
        if o + CHUNK > LANES:
            a = jnp.where(lane < LANES - o, a, turn(first[l][t + 1], -o, 1))
            lon = jnp.where(lane >= CHUNK, lane - CHUNK, lane + (LANES - CHUNK))
            b = jnp.where(lon < LANES - o, b, turn(second[l][t + 1], CHUNK - o, 1))
        out[chunk[g], pl.ds(at, 8), :] = jnp.where(lane < CHUNK, a, b)
        moved = pltpu.roll(b, slot * 16, 1)
        last = pl.ds(block, 8)
        out[chunk[g], last, :] = jnp.where((lane >> 4) == slot, moved, out[chunk[g], last, :])

    lax.fori_loop(0, PAIRS - 1, two, 0)
    first, second = tracer(NTR - 1), air()
    for l in range(LEVS):
        for g in range(GROUPS):
            pack(g, l, ((PAIRS - 1) * LEVS + l) * 8, REST + 8, l * 4, first, second)


def target_kernel(index, offset, phase, inner, outer):
    lane = lane_index()
    blank = jnp.zeros((8, LANES - CHUNK), F32)
    for ref in (inner, outer):
        ref[pl.ds(0, 16), :] = jnp.zeros((16, LANES), F32)
    for n in range(2 * GROUPS - 1):
        at = (n + 1) * 16
        main, tail = [], []
        for h in range(2):
            rows = pl.ds(8 * h, 8)
            part = (offset[n, rows, :].astype(F32) + phase[n, rows, :]) * (1.0 / 32.0)
            x = jnp.concatenate([index[n, rows, :].astype(F32) + part, blank], 1)
            moved = turn(x, CHUNK, 1)
            main.append(jnp.where(lane < CHUNK, x, moved))
            last = jnp.where(lane < 16, moved, 0.0)
            last = last + turn(last, 16, 1)
            tail.append(last + turn(last, 32, 1))
        other = [turn(x, 64, 1) for x in tail]
        inner[pl.ds(at, 4), :] = main[0][4:]
        inner[pl.ds(at + 4, 4), :] = main[1][:4]
        inner[pl.ds(at + 8, 8), :] = turn(tail[0], 4, 0) + other[1]
        outer[pl.ds(at, 4, stride=2), :] = main[0][:4]
        outer[pl.ds(at + 1, 4, stride=2), :] = main[1][4:]
        outer[pl.ds(at + 8, 2, stride=2), :] = (tail[0] + turn(other[0], -2, 0))[:2]
        outer[pl.ds(at + 9, 2, stride=2), :] = (tail[1] + turn(other[1], -2, 0))[4:6]


def remap_rows(data, table, out):
    lane, row = lane_index(), row_index()

    def targets(tile):
        found = []
        for parity in range(2):
            for half in range(2):
                start = (parity + 16 * half) * 16 + tile
                position = table[pl.ds(start, 8, stride=32), :]
                s = jnp.minimum(position.astype(jnp.int32), 2 * GROUPS - 1)
                f = position - s.astype(F32)
                square = f * f * 0.5
                cubic = 3.0 * square - f * f * f
                found.append(((s >> 1) & 7, s >= 16, (s & 1) == 1, f, square, cubic))
        return found

    def columns(even, odd, found):
        back = [turn(x, 1, 0) for x in odd]
        before = [jnp.where(row == 0, even[0], back[0]), jnp.where(row == 0, back[0], back[1])]
        left = [0.5 * (before[i] + even[i]) for i in range(2)]
        ahead = [turn(x, -1, 0) for x in left]
        right = [jnp.where(row == 7, ahead[1], ahead[0]), jnp.where(row == 7, odd[1], ahead[1])]
        pair = [even[i] + odd[i] for i in range(2)]
        run = list(pair)
        for shift in (1, 2, 4):
            run = [x + jnp.where(row >= shift, turn(x, shift, 0), 0.0) for x in run]
        half_sum = jnp.broadcast_to(run[0][7:8], (8, LANES))
        total = half_sum + run[1][7:8]
        below = [run[0] - pair[0], (run[1] - pair[1]) + half_sum]
        edges = []
        for where, high, is_odd, f, square, cubic in found:
            le, ri, ev, od, be = (
                jnp.where(high, pick(x[1], where), pick(x[0], where)) for x in (left, right, even, odd, below)
            )
            middle = 0.5 * (ev + od)
            lo = jnp.where(is_odd, middle, le)
            hi = jnp.where(is_odd, ri, middle)
            m = jnp.where(is_odd, od, ev)
            base = be + jnp.where(is_odd, ev, 0.0)
            edges.append(base + lo * f + (hi - lo) * square + ((m + m) - (lo + hi)) * cubic)
        ev0, ev1, od0, od1 = edges
        next0, next1 = turn(ev0, -1, 0), turn(ev1, -1, 0)
        new_even = [od0 - ev0, od1 - ev1]
        new_odd = [jnp.where(row == 7, next1, next0) - od0, jnp.where(row == 7, total, next1) - od1]
        return new_even, new_odd

    def span(start, half):
        return pl.ds(start + half * 8 * DEPTH, 8, stride=DEPTH)

    def main(tile, _):
        found = targets(tile)
        for pair in range(PAIRS):
            at = [(pair * LEVS + l) * 8 + tile for l in range(LEVS)]
            even, odd = ([data[span(at[l], half), :] for half in range(2)] for l in range(LEVS))
            new = columns(even, odd, found)
            for l in range(LEVS):
                for half in range(2):
                    out[span(at[l], half), :] = new[l][half]
        return 0

    lax.fori_loop(0, 8, main, 0)

    def tail(tile, _):
        found = targets(8 + tile)
        for block in range(BLOCKS):
            at = [REST + 8 * block + tile, REST + 8 * block + tile + 4]
            a, b = ([data[span(at[i], half), :] for half in range(2)] for i in range(2))
            even = [jnp.where(lane < 64, a[half], turn(b[half], 64, 1)) for half in range(2)]
            odd = [jnp.where(lane < 64, turn(a[half], 64, 1), b[half]) for half in range(2)]
            even, odd = columns(even, odd, found)
            for half in range(2):
                out[span(at[0], half), :] = jnp.where(lane < 64, even[half], turn(odd[half], 64, 1))
                out[span(at[1], half), :] = jnp.where(lane < 64, turn(even[half], 64, 1), odd[half])
        return 0

    lax.fori_loop(0, 4, tail, 0)


def place_of(back):
    lev = lax.axis_index("lev")
    return lev >> 2, lev & 3, on_odd_row() != back


def slots_to(back):
    y, z, y_first = place_of(back)
    slots = []
    for g in range(GROUPS):
        j, k = ((g >> 2) - y) & 3, (g & 3) ^ z
        slots.append(jnp.where(y_first, 4 * j + k, 4 * k + j))
    return slots


def gather_chunks(back, given, target, sem):
    y, z, y_first = place_of(back)
    copies = []
    for a in range(4):
        for b in range(4):
            j, k = jnp.where(y_first, a, b), jnp.where(y_first, b, a)
            place = ((y - j) & 3) * 4 + (z ^ k)
            copies.append(pltpu.make_async_copy(given[b].at[a], target(place), sem.at[4 * a + b]))
    for copy in copies:
        copy.start()
    for copy in copies:
        copy.wait()


def remap_kernel(*refs):
    given, (table, out, data, new, sem) = refs[:4], refs[4:]

    def rows(place):
        return pl.ds(pl.multiple_of(place * DEPTH, 8), DEPTH)

    gather_chunks(False, given, lambda place: data.at[rows(place)], sem)
    remap_rows(data, table, new)
    copies = []
    for g, slot in enumerate(slots_to(True)):
        copies.append(pltpu.make_async_copy(new.at[rows(g)], out.at[slot], sem.at[g]))
    for copy in copies:
        copy.start()
    for copy in copies:
        copy.wait()


def collect_kernel(part, *refs):
    if part == OUTER:
        data, _, out, flat, sem = refs
    else:
        given, (out, data, flat, sem) = refs[:4], refs[-4:]
        gather_chunks(True, given, lambda place: data.at[place], sem)
    lane = lane_index()

    def unpack(pair, at, block, slot):
        for l in range(LEVS):
            pieces = []
            for g in range(GROUPS):
                _, o = span_of(g)
                main = data[g, at(l), :]
                tail = pltpu.roll(data[g, pl.ds(block, 8), :], LANES - (l * 4 + slot) * 16, 1)
                mixed = jnp.where(lane < 16, tail, main)
                pieces.append((turn(main, o, 1), turn(mixed, o - CHUNK, 1)))
            for second in range(2):
                for c in range(TILES):
                    value = None
                    for g in range(GROUPS):
                        start = CHUNK * g - LANES * c
                        if start >= LANES or start + CHUNK <= 0:
                            continue
                        piece = pieces[g][second]
                        value = piece if value is None else jnp.where(lane >= start, piece, value)
                    flat[pl.ds((2 * pair + second) * 8 * STEP + c * LEVS + l, 8, stride=STEP), :] = value

    def one(pair, _):
        unpack(pair, lambda l: pl.ds(pl.multiple_of((pair * LEVS + l) * 8, 8), 8), REST, pair)
        return 0

    lax.fori_loop(0, PAIRS - 1, one, 0)
    unpack(PAIRS - 1, lambda l: pl.ds(((PAIRS - 1) * LEVS + l) * 8, 8), REST + 8, 0)
    view = flat.reshape(FIELDS, 8 // part, part, TILES, LEVS, LANES)
    copies = []
    for c in range(TILES):
        cut = pl.ds(LANES * c, LANES)
        for run, first in enumerate((4,) if part == INNER else (0, 12)):
            target = out.at[:, pl.ds(first, 8 // part), :, cut]
            copies.append(pltpu.make_async_copy(view.at[:, :, run, c], target, sem.at[len(copies)]))
    for copy in copies:
        copy.start()
    for copy in copies:
        copy.wait()


ANYWHERE = pl.BlockSpec(memory_space=pl.ANY)
IN_HBM = pl.BlockSpec(memory_space=pltpu.HBM)
IN_VMEM = pl.BlockSpec(memory_space=pltpu.VMEM)
PARAMS = pltpu.CompilerParams(vmem_limit_bytes=VMEM_LIMIT)


def transport(part, *given):
    factor = pltpu.VMEM((STEP * 8, LANES), F32)
    return pl.pallas_call(
        functools.partial(transport_kernel, part),
        out_shape=jax.ShapeDtypeStruct((GROUPS, DEPTH, LANES), F32),
        in_specs=[IN_HBM] * 4 + [IN_HBM if part == INNER else ANYWHERE] * (len(given) - 4),
        out_specs=IN_VMEM,
        scratch_shapes=[
            pltpu.VMEM(((NTR + 3) * slots_of(part) * STEP, LANES), F32),
            factor,
            factor,
            factor,
            factor,
            pltpu.VMEM((STEP * 16, LANES), F32),
            pltpu.SemaphoreType.DMA((12 * TILES,)),
        ],
        compiler_params=PARAMS,
    )(*given)


def remap_outer(data, table):
    return pl.pallas_call(
        remap_rows,
        out_shape=jax.ShapeDtypeStruct((GROUPS * DEPTH, LANES), F32),
        in_specs=[IN_VMEM] * 2,
        out_specs=IN_VMEM,
        compiler_params=PARAMS,
    )(data.reshape(GROUPS * DEPTH, LANES), table).reshape(GROUPS, DEPTH, LANES)


def remap_inner(given, table):
    held = pltpu.VMEM((GROUPS * DEPTH, LANES), F32)
    return pl.pallas_call(
        remap_kernel,
        out_shape=jax.ShapeDtypeStruct((GROUPS, DEPTH, LANES), F32),
        in_specs=[ANYWHERE] * 4 + [IN_VMEM],
        out_specs=ANYWHERE,
        scratch_shapes=[held, held, pltpu.SemaphoreType.DMA((GROUPS,))],
        compiler_params=PARAMS,
    )(*given, table)


def collect(part, given, *result):
    scratch = [pltpu.VMEM((FIELDS * 8 * STEP, LANES), F32), pltpu.SemaphoreType.DMA((2 * TILES,))]
    if part == INNER:
        scratch = [pltpu.VMEM((GROUPS, DEPTH, LANES), F32)] + scratch
    return pl.pallas_call(
        functools.partial(collect_kernel, part),
        out_shape=jax.ShapeDtypeStruct((FIELDS, ROWS, LEVS, LONS), F32),
        in_specs=[ANYWHERE] * 4 if part == INNER else [IN_VMEM, ANYWHERE],
        out_specs=ANYWHERE,
        scratch_shapes=scratch,
        input_output_aliases={} if part == INNER else {1: 0},
        compiler_params=PARAMS,
    )(*given, *result)


def exchange(data):
    return lax.all_to_all(data, "lev", split_axis=0, concat_axis=0, tiled=True)


def hop(blocks, evens_along_z):
    lats = lax.axis_size("lat")
    moved = {}
    for a in (2, 3, 1):
        pairs = []
        for lat in range(lats):
            along_z = (lat % 2 == 0) == evens_along_z
            for lev in range(GROUPS):
                target = lev ^ a if along_z else (lev + 4 * a) % GROUPS
                pairs.append((lat * GROUPS + lev, lat * GROUPS + target))
        moved[a] = lax.ppermute(blocks[a], ("lat", "lev"), pairs)
    return [blocks[0]] + [moved[a] for a in range(1, 4)]


def first_hop(data, back=False):
    return hop([data[4 * a : 4 * a + 4] for a in range(4)], not back)


def second_hop(rows, back=False):
    return hop([jnp.stack([rows[a][b] for a in range(4)]) for b in range(4)], back)


def after(values, *others):
    return lax.optimization_barrier((values, others))[0]


def shards(tracers, thickness, courant_x, courant_y, level_index, level_offset, level_phase):
    own = [pltpu.with_memory_space_constraint(x, pltpu.HBM) for x in (tracers, thickness, courant_x, courant_y)]
    rim = pltpu.HBM((NTR + 1, 2, LEVS, LONS), F32)
    inside, across = pl.pallas_call(
        halo_kernel,
        out_shape=(rim, rim),
        in_specs=[IN_HBM] * 3,
        out_specs=(IN_VMEM, IN_VMEM),
        scratch_shapes=[pltpu.SemaphoreType.DMA((2, 3))],
    )(own[0], own[1], own[3])
    lats = lax.axis_size("lat")
    to_core = [(i, i ^ 1) for i in range(lats)]
    to_chip = [(i, i + 1) for i in range(1, lats - 1, 2)] + [(i + 1, i) for i in range(1, lats - 1, 2)]
    first = pltpu.with_memory_space_constraint(inside, pltpu.HBM)
    inside, across = lax.ppermute(inside, "lat", to_core), lax.ppermute(across, "lat", to_chip)
    inner = transport(INNER, *own, first)
    table = jax.ShapeDtypeStruct((2 * GROUPS * 16, LANES), F32)
    inner_table, outer_table = pl.pallas_call(
        target_kernel,
        out_shape=(table, table),
        in_specs=[IN_VMEM] * 3,
        out_specs=(IN_VMEM, IN_VMEM),
        compiler_params=PARAMS,
    )(level_index, level_offset, level_phase)
    outer = transport(OUTER, *own, inside, across, outer_table)
    inner = first_hop(inner)
    inner, outer = second_hop(after(inner, outer)), exchange(outer)
    inner = remap_inner(inner, inner_table)
    outer = remap_outer(after(outer, inner), outer_table)
    inner = first_hop(inner, True)
    inner, outer = second_hop(after(inner, outer), True), exchange(outer)
    return collect(OUTER, [outer], collect(INNER, inner))


def solution(mesh):
    in_specs = (
        P(None, "lat", "lev", None),
        P("lat", "lev", None),
        P("lat", "lev", None),
        P("lat", "lev", None),
        P(None, "lat", "lev"),
        P(None, "lat", "lev"),
        P(None, "lat", "lev"),
    )
    out_specs = P(None, "lat", "lev", None)
    return jax.shard_map(shards, mesh=mesh, in_specs=in_specs, out_specs=out_specs, check_vma=False)
```

```python
import functools

import jax
import jax.numpy as jnp
from jax import lax
from jax.experimental import pallas as pl
from jax.experimental.pallas import tpu as pltpu
from jax.sharding import PartitionSpec as P

F32 = jnp.float32
NTR = 9
FIELDS = NTR + 1
PAIRS = FIELDS // 2
ROWS = 16
LEVS = 2
LANES = 128
TILES = 9
LONS = LANES * TILES
CHUNK = 72
GROUPS = 16
STEP = TILES * LEVS
VMEM_LIMIT = 40 * 1024 * 1024

INNER, OUTER = 1, 2

REST = PAIRS * LEVS * 8
BLOCKS = (PAIRS + 3) // 4
DEPTH = REST + BLOCKS * 8

THICK, NORTH, EAST = NTR, NTR + 1, NTR + 2


def slots_of(part):
    return 8 + 4 * part


def lane_index():
    return lax.broadcasted_iota(jnp.int32, (8, LANES), 1)


def row_index():
    return lax.broadcasted_iota(jnp.int32, (8, LANES), 0)


def turn(x, shift, axis):
    shift = shift % x.shape[axis]
    return x if shift == 0 else pltpu.roll(x, shift, axis)


def west_of(tiles, lane):
    rolled = [turn(x, 1, 1) for x in tiles]
    return [jnp.where(lane == 0, rolled[c - 1], rolled[c]) for c in range(TILES)]


def east_of(tiles, lane):
    rolled = [turn(x, -1, 1) for x in tiles]
    return [jnp.where(lane == LANES - 1, rolled[(c + 1) % TILES], rolled[c]) for c in range(TILES)]


def span_of(group):
    return divmod(CHUNK * group, LANES)


def pick(x, where):
    return jnp.take_along_axis(x, where, axis=0, mode="promise_in_bounds")


def on_odd_row():
    return (lax.axis_index("lat") & 1) == 1


def halo_kernel(tracers, thickness, courant_y, inside, across, sem):
    odd = on_odd_row()
    copies = []
    for edge, (out, first) in enumerate(((inside, jnp.where(odd, 0, ROWS - 2)), (across, jnp.where(odd, ROWS - 2, 0)))):
        rows = pl.ds(first, 2)
        copies.append(pltpu.make_async_copy(tracers.at[:, rows], out.at[pl.ds(0, NTR)], sem.at[edge, 0]))
        row = jnp.where(first == 0, 0, ROWS - 1)
        copies.append(pltpu.make_async_copy(thickness.at[row], out.at[NTR, 0], sem.at[edge, 1]))
        copies.append(pltpu.make_async_copy(courant_y.at[row], out.at[NTR, 1], sem.at[edge, 2]))
    for copy in copies:
        copy.start()
    for copy in copies:
        copy.wait()


def transport_kernel(part, *refs):
    if part == OUTER:
        tracers, thickness, courant_x, courant_y, inside, across, _, out, held, mx, ax, my, ay, fy, sem = refs
    else:
        tracers, thickness, courant_x, courant_y, _, out, held, mx, ax, my, ay, fy, sem = refs
    chunk = slots_to(False) if part == INNER else list(range(GROUPS))
    slots = slots_of(part)
    lane, row = lane_index(), row_index()
    view = held.reshape(NTR + 3, slots // part, part, TILES, LEVS, LANES)
    copies = []

    def bring(source, target):
        copies.append(pltpu.make_async_copy(source, target, sem.at[len(copies)]))

    for c in range(TILES):
        cut = pl.ds(LANES * c, LANES)
        runs = ((2, 12, 0, 0),) if part == INNER else ((0, 6, 2, 0), (10, 6, 0, 1))
        for first, size, at, run in runs:
            own, into = pl.ds(first, size), pl.ds(at, size)
            bring(tracers.at[:, own, :, cut], view.at[pl.ds(0, NTR), into, run, c])
            for array, source in ((THICK, thickness), (NORTH, courant_y), (EAST, courant_x)):
                bring(source.at[own, :, cut], view.at[array, into, run, c])
    for copy in copies:
        copy.start()
    if part == OUTER:

        def bring_halos(low, high):
            for c in range(TILES):
                cut = pl.ds(LANES * c, LANES)
                bring(low.at[pl.ds(0, NTR), :, :, cut], view.at[pl.ds(0, NTR), pl.ds(0, 2), 0, c])
                bring(low.at[NTR, 0, :, cut], view.at[THICK, 1, 0, c])
                bring(high.at[pl.ds(0, NTR), :, :, cut], view.at[pl.ds(0, NTR), pl.ds(6, 2), 1, c])
                bring(high.at[NTR, :, :, cut], view.at[pl.ds(THICK, 2), 6, 1, c])
            return copies[-4 * TILES :]

        odd = on_odd_row()

        @pl.when(odd)
        def _():
            for copy in bring_halos(inside, across):
                copy.start()

        del copies[-4 * TILES :]
        halos = bring_halos(across, inside)

        @pl.when(jnp.logical_not(odd))
        def _():
            for copy in halos:
                copy.start()

    for g in range(GROUPS):
        out[g, pl.ds(REST, 8 * BLOCKS), :] = jnp.zeros((8 * BLOCKS, LANES), F32)
    for copy in copies:
        copy.wait()

    def rows_of(array, shift, c, l):
        start = (array * slots + (2 + shift) * part) * STEP + c * LEVS + l
        return held[pl.ds(start, 8, stride=STEP), :]

    def past(array, shift):
        return held[pl.ds((array * slots + 8 + (2 + shift) * part) * STEP, part * STEP), :]

    def place(l, c):
        return pl.ds((c * LEVS + l) * 8, 8)

    def faces(l, c, shift):
        return pl.ds((c * LEVS + l) * 16 + shift, 8)

    def keep_past(values):
        for run in range(part):
            fy[pl.ds(8 + run, STEP, stride=16), :] = values[run * STEP : (run + 1) * STEP]

    def factors(courant, before, after):
        mass = jnp.where(courant > 0, courant * before, courant * after)
        return mass, mass * jnp.where(courant > 0, 0.25 - 0.25 * courant, -0.25 - 0.25 * courant)

    for l in range(LEVS):
        thick = [rows_of(THICK, 0, c, l) for c in range(TILES)]
        west = west_of(thick, lane)
        for c in range(TILES):
            mx[place(l, c), :], ax[place(l, c), :] = factors(rows_of(EAST, 0, c, l), west[c], thick[c])
            courant = rows_of(NORTH, 0, c, l)
            if part == OUTER:
                courant = jnp.where((row > 0) | (lax.axis_index("lat") > 0), courant, 0.0)
            my[place(l, c), :], ay[place(l, c), :] = factors(courant, rows_of(THICK, -1, c, l), thick[c])
    past_mass, past_tilt = factors(past(NORTH, 0), past(THICK, -1), past(THICK, 0))

    def air():
        keep_past(past_mass)
        for l in range(LEVS):
            for c in range(TILES):
                fy[faces(l, c, 0), :] = my[place(l, c), :]
        tiles = []
        for l in range(LEVS):
            flux = [mx[place(l, c), :] for c in range(TILES)]
            flux_e = east_of(flux, lane)
            tiles.append(
                [
                    rows_of(THICK, 0, c, l) + (flux[c] - flux_e[c]) + (my[place(l, c), :] - fy[faces(l, c, part), :])
                    for c in range(TILES)
                ]
            )
        return tiles

    def tracer(array):
        past_q = [past(array, shift) for shift in (-2, -1, 0, 1)]
        up = past_mass > 0
        value = jnp.where(up, past_q[1], past_q[2])
        rise = jnp.where(up, past_q[2] - past_q[0], past_q[3] - past_q[1])
        keep_past(past_mass * value + past_tilt * rise)
        tiles = []
        for l in range(LEVS):
            q = [rows_of(array, 0, c, l) for c in range(TILES)]
            qw = west_of(q, lane)
            qe = east_of(q, lane)
            d = [qe[c] - qw[c] for c in range(TILES)]
            dw = west_of(d, lane)
            flux = []
            for c in range(TILES):
                mass = mx[place(l, c), :]
                up = mass > 0
                flux.append(mass * jnp.where(up, qw[c], q[c]) + ax[place(l, c), :] * jnp.where(up, dw[c], d[c]))
            flux_e = east_of(flux, lane)
            now = []
            for c in range(TILES):
                mass = my[place(l, c), :]
                up = mass > 0
                q2, q1, q3 = (rows_of(array, shift, c, l) for shift in (-2, -1, 1))
                value = jnp.where(up, q1, q[c])
                rise = jnp.where(up, q[c] - q2, q3 - q1)
                flux_y = mass * value + ay[place(l, c), :] * rise
                fy[faces(l, c, 0), :] = flux_y
                now.append(rows_of(THICK, 0, c, l) * q[c] + (flux[c] - flux_e[c]) + flux_y)
            tiles.append(now)
        return [[tiles[l][c] - fy[faces(l, c, part), :] for c in range(TILES)] for l in range(LEVS)]

    def two(pair, _):
        first = tracer(2 * pair)
        send_block(pair, first, tracer(2 * pair + 1))
        return 0

    def send_block(pair, first, second):
        block = REST
        for l in range(LEVS):
            slot = l * 4 + pair
            for g in range(GROUPS):
                pack(g, l, pl.multiple_of((pair * LEVS + l) * 8, 8), block, slot, first, second)

    def pack(g, l, at, block, slot, first, second):
        t, o = span_of(g)
        a = turn(first[l][t], -o, 1)
        b = turn(second[l][t], CHUNK - o, 1)
        if o + CHUNK > LANES:
            a = jnp.where(lane < LANES - o, a, turn(first[l][t + 1], -o, 1))
            lon = jnp.where(lane >= CHUNK, lane - CHUNK, lane + (LANES - CHUNK))
            b = jnp.where(lon < LANES - o, b, turn(second[l][t + 1], CHUNK - o, 1))
        out[chunk[g], pl.ds(at, 8), :] = jnp.where(lane < CHUNK, a, b)
        moved = pltpu.roll(b, slot * 16, 1)
        last = pl.ds(block, 8)
        out[chunk[g], last, :] = jnp.where((lane >> 4) == slot, moved, out[chunk[g], last, :])

    lax.fori_loop(0, PAIRS - 1, two, 0)
    first, second = tracer(NTR - 1), air()
    for l in range(LEVS):
        for g in range(GROUPS):
            pack(g, l, ((PAIRS - 1) * LEVS + l) * 8, REST + 8, l * 4, first, second)


def target_kernel(index, offset, phase, inner, outer):
    lane = lane_index()
    blank = jnp.zeros((8, LANES - CHUNK), F32)
    for ref in (inner, outer):
        ref[pl.ds(0, 16), :] = jnp.zeros((16, LANES), F32)
    for n in range(2 * GROUPS - 1):
        at = (n + 1) * 16
        main, tail = [], []
        for h in range(2):
            rows = pl.ds(8 * h, 8)
            part = (offset[n, rows, :].astype(F32) + phase[n, rows, :]) * (1.0 / 32.0)
            x = jnp.concatenate([index[n, rows, :].astype(F32) + part, blank], 1)
            moved = turn(x, CHUNK, 1)
            main.append(jnp.where(lane < CHUNK, x, moved))
            last = jnp.where(lane < 16, moved, 0.0)
            last = last + turn(last, 16, 1)
            tail.append(last + turn(last, 32, 1))
        other = [turn(x, 64, 1) for x in tail]
        inner[pl.ds(at, 4), :] = main[0][4:]
        inner[pl.ds(at + 4, 4), :] = main[1][:4]
        inner[pl.ds(at + 8, 8), :] = turn(tail[0], 4, 0) + other[1]
        outer[pl.ds(at, 4, stride=2), :] = main[0][:4]
        outer[pl.ds(at + 1, 4, stride=2), :] = main[1][4:]
        outer[pl.ds(at + 8, 2, stride=2), :] = (tail[0] + turn(other[0], -2, 0))[:2]
        outer[pl.ds(at + 9, 2, stride=2), :] = (tail[1] + turn(other[1], -2, 0))[4:6]


def remap_rows(data, table, out):
    lane, row = lane_index(), row_index()

    def targets(tile):
        found = []
        for parity in range(2):
            for half in range(2):
                start = (parity + 16 * half) * 16 + tile
                position = table[pl.ds(start, 8, stride=32), :]
                s = jnp.minimum(position.astype(jnp.int32), 2 * GROUPS - 1)
                f = position - s.astype(F32)
                square = f * f * 0.5
                cubic = 3.0 * square - f * f * f
                found.append(((s >> 1) & 7, s >= 16, (s & 1) == 1, f, square, cubic))
        return found

    def columns(even, odd, found):
        back = [turn(x, 1, 0) for x in odd]
        before = [jnp.where(row == 0, even[0], back[0]), jnp.where(row == 0, back[0], back[1])]
        left = [0.5 * (before[i] + even[i]) for i in range(2)]
        ahead = [turn(x, -1, 0) for x in left]
        right = [jnp.where(row == 7, ahead[1], ahead[0]), jnp.where(row == 7, odd[1], ahead[1])]
        pair = [even[i] + odd[i] for i in range(2)]
        run = list(pair)
        for shift in (1, 2, 4):
            run = [x + jnp.where(row >= shift, turn(x, shift, 0), 0.0) for x in run]
        half_sum = jnp.broadcast_to(run[0][7:8], (8, LANES))
        total = half_sum + run[1][7:8]
        below = [run[0] - pair[0], (run[1] - pair[1]) + half_sum]
        edges = []
        for where, high, is_odd, f, square, cubic in found:
            le, ri, ev, od, be = (
                jnp.where(high, pick(x[1], where), pick(x[0], where)) for x in (left, right, even, odd, below)
            )
            middle = 0.5 * (ev + od)
            lo = jnp.where(is_odd, middle, le)
            hi = jnp.where(is_odd, ri, middle)
            m = jnp.where(is_odd, od, ev)
            base = be + jnp.where(is_odd, ev, 0.0)
            edges.append(base + lo * f + (hi - lo) * square + ((m + m) - (lo + hi)) * cubic)
        ev0, ev1, od0, od1 = edges
        next0, next1 = turn(ev0, -1, 0), turn(ev1, -1, 0)
        new_even = [od0 - ev0, od1 - ev1]
        new_odd = [jnp.where(row == 7, next1, next0) - od0, jnp.where(row == 7, total, next1) - od1]
        return new_even, new_odd

    def span(start, half):
        return pl.ds(start + half * 8 * DEPTH, 8, stride=DEPTH)

    def main(tile, _):
        found = targets(tile)
        for pair in range(PAIRS):
            at = [(pair * LEVS + l) * 8 + tile for l in range(LEVS)]
            even, odd = ([data[span(at[l], half), :] for half in range(2)] for l in range(LEVS))
            new = columns(even, odd, found)
            for l in range(LEVS):
                for half in range(2):
                    out[span(at[l], half), :] = new[l][half]
        return 0

    lax.fori_loop(0, 8, main, 0)

    def tail(tile, _):
        found = targets(8 + tile)
        for block in range(BLOCKS):
            at = [REST + 8 * block + tile, REST + 8 * block + tile + 4]
            a, b = ([data[span(at[i], half), :] for half in range(2)] for i in range(2))
            even = [jnp.where(lane < 64, a[half], turn(b[half], 64, 1)) for half in range(2)]
            odd = [jnp.where(lane < 64, turn(a[half], 64, 1), b[half]) for half in range(2)]
            even, odd = columns(even, odd, found)
            for half in range(2):
                out[span(at[0], half), :] = jnp.where(lane < 64, even[half], turn(odd[half], 64, 1))
                out[span(at[1], half), :] = jnp.where(lane < 64, turn(even[half], 64, 1), odd[half])
        return 0

    lax.fori_loop(0, 4, tail, 0)


def place_of(back):
    lev = lax.axis_index("lev")
    return lev >> 2, lev & 3, on_odd_row() != back


def slots_to(back):
    y, z, y_first = place_of(back)
    slots = []
    for g in range(GROUPS):
        j, k = ((g >> 2) - y) & 3, (g & 3) ^ z
        slots.append(jnp.where(y_first, 4 * j + k, 4 * k + j))
    return slots


def gather_chunks(back, given, target, sem):
    y, z, y_first = place_of(back)
    copies = []
    for a in range(4):
        for b in range(4):
            j, k = jnp.where(y_first, a, b), jnp.where(y_first, b, a)
            place = ((y - j) & 3) * 4 + (z ^ k)
            copies.append(pltpu.make_async_copy(given[b].at[a], target(place), sem.at[4 * a + b]))
    for copy in copies:
        copy.start()
    for copy in copies:
        copy.wait()


def remap_kernel(*refs):
    given, (table, out, data, new, sem) = refs[:4], refs[4:]

    def rows(place):
        return pl.ds(pl.multiple_of(place * DEPTH, 8), DEPTH)

    gather_chunks(False, given, lambda place: data.at[rows(place)], sem)
    remap_rows(data, table, new)
    copies = []
    for g, slot in enumerate(slots_to(True)):
        copies.append(pltpu.make_async_copy(new.at[rows(g)], out.at[slot], sem.at[g]))
    for copy in copies:
        copy.start()
    for copy in copies:
        copy.wait()


def collect_kernel(part, *refs):
    if part == OUTER:
        data, _, out, flat, sem = refs
    else:
        given, (out, data, flat, sem) = refs[:4], refs[-4:]
        gather_chunks(True, given, lambda place: data.at[place], sem)
    lane = lane_index()

    def unpack(pair, at, block, slot):
        for l in range(LEVS):
            pieces = []
            for g in range(GROUPS):
                _, o = span_of(g)
                main = data[g, at(l), :]
                tail = pltpu.roll(data[g, pl.ds(block, 8), :], LANES - (l * 4 + slot) * 16, 1)
                mixed = jnp.where(lane < 16, tail, main)
                pieces.append((turn(main, o, 1), turn(mixed, o - CHUNK, 1)))
            for second in range(2):
                for c in range(TILES):
                    value = None
                    for g in range(GROUPS):
                        start = CHUNK * g - LANES * c
                        if start >= LANES or start + CHUNK <= 0:
                            continue
                        piece = pieces[g][second]
                        value = piece if value is None else jnp.where(lane >= start, piece, value)
                    flat[pl.ds((2 * pair + second) * 8 * STEP + c * LEVS + l, 8, stride=STEP), :] = value

    def one(pair, _):
        unpack(pair, lambda l: pl.ds(pl.multiple_of((pair * LEVS + l) * 8, 8), 8), REST, pair)
        return 0

    lax.fori_loop(0, PAIRS - 1, one, 0)
    unpack(PAIRS - 1, lambda l: pl.ds(((PAIRS - 1) * LEVS + l) * 8, 8), REST + 8, 0)
    view = flat.reshape(FIELDS, 8 // part, part, TILES, LEVS, LANES)
    copies = []
    for c in range(TILES):
        cut = pl.ds(LANES * c, LANES)
        for run, first in enumerate((4,) if part == INNER else (0, 12)):
            target = out.at[:, pl.ds(first, 8 // part), :, cut]
            copies.append(pltpu.make_async_copy(view.at[:, :, run, c], target, sem.at[len(copies)]))
    for copy in copies:
        copy.start()
    for copy in copies:
        copy.wait()


ANYWHERE = pl.BlockSpec(memory_space=pl.ANY)
IN_HBM = pl.BlockSpec(memory_space=pltpu.HBM)
IN_VMEM = pl.BlockSpec(memory_space=pltpu.VMEM)
PARAMS = pltpu.CompilerParams(vmem_limit_bytes=VMEM_LIMIT)


def transport(part, *given):
    factor = pltpu.VMEM((STEP * 8, LANES), F32)
    return pl.pallas_call(
        functools.partial(transport_kernel, part),
        out_shape=jax.ShapeDtypeStruct((GROUPS, DEPTH, LANES), F32),
        in_specs=[IN_HBM] * 4 + [IN_HBM if part == INNER else ANYWHERE] * (len(given) - 4),
        out_specs=IN_VMEM,
        scratch_shapes=[
            pltpu.VMEM(((NTR + 3) * slots_of(part) * STEP, LANES), F32),
            factor,
            factor,
            factor,
            factor,
            pltpu.VMEM((STEP * 16, LANES), F32),
            pltpu.SemaphoreType.DMA((12 * TILES,)),
        ],
        compiler_params=PARAMS,
    )(*given)


def remap_outer(data, table):
    return pl.pallas_call(
        remap_rows,
        out_shape=jax.ShapeDtypeStruct((GROUPS * DEPTH, LANES), F32),
        in_specs=[IN_VMEM] * 2,
        out_specs=IN_VMEM,
        compiler_params=PARAMS,
    )(data.reshape(GROUPS * DEPTH, LANES), table).reshape(GROUPS, DEPTH, LANES)


def remap_inner(given, table):
    held = pltpu.VMEM((GROUPS * DEPTH, LANES), F32)
    return pl.pallas_call(
        remap_kernel,
        out_shape=jax.ShapeDtypeStruct((GROUPS, DEPTH, LANES), F32),
        in_specs=[ANYWHERE] * 4 + [IN_VMEM],
        out_specs=ANYWHERE,
        scratch_shapes=[held, held, pltpu.SemaphoreType.DMA((GROUPS,))],
        compiler_params=PARAMS,
    )(*given, table)


def collect(part, given, *result):
    scratch = [pltpu.VMEM((FIELDS * 8 * STEP, LANES), F32), pltpu.SemaphoreType.DMA((2 * TILES,))]
    if part == INNER:
        scratch = [pltpu.VMEM((GROUPS, DEPTH, LANES), F32)] + scratch
    return pl.pallas_call(
        functools.partial(collect_kernel, part),
        out_shape=jax.ShapeDtypeStruct((FIELDS, ROWS, LEVS, LONS), F32),
        in_specs=[ANYWHERE] * 4 if part == INNER else [IN_VMEM, ANYWHERE],
        out_specs=ANYWHERE,
        scratch_shapes=scratch,
        input_output_aliases={} if part == INNER else {1: 0},
        compiler_params=PARAMS,
    )(*given, *result)


def exchange(data):
    return lax.all_to_all(data, "lev", split_axis=0, concat_axis=0, tiled=True)


def hop(blocks, evens_along_z):
    lats = lax.axis_size("lat")
    moved = {}
    for a in (2, 3, 1):
        pairs = []
        for lat in range(lats):
            along_z = (lat % 2 == 0) == evens_along_z
            for lev in range(GROUPS):
                target = lev ^ a if along_z else (lev + 4 * a) % GROUPS
                pairs.append((lat * GROUPS + lev, lat * GROUPS + target))
        moved[a] = lax.ppermute(blocks[a], ("lat", "lev"), pairs)
    return [blocks[0]] + [moved[a] for a in range(1, 4)]


def first_hop(data, back=False):
    return hop([data[4 * a : 4 * a + 4] for a in range(4)], not back)


def second_hop(rows, back=False):
    return hop([jnp.stack([rows[a][b] for a in range(4)]) for b in range(4)], back)


def after(values, *others):
    return lax.optimization_barrier((values, others))[0]


def shards(tracers, thickness, courant_x, courant_y, level_index, level_offset, level_phase):
    own = [pltpu.with_memory_space_constraint(x, pltpu.HBM) for x in (tracers, thickness, courant_x, courant_y)]
    rim = pltpu.HBM((NTR + 1, 2, LEVS, LONS), F32)
    inside, across = pl.pallas_call(
        halo_kernel,
        out_shape=(rim, rim),
        in_specs=[IN_HBM] * 3,
        out_specs=(IN_VMEM, IN_VMEM),
        scratch_shapes=[pltpu.SemaphoreType.DMA((2, 3))],
    )(own[0], own[1], own[3])
    lats = lax.axis_size("lat")
    to_core = [(i, i ^ 1) for i in range(lats)]
    to_chip = [(i, i + 1) for i in range(1, lats - 1, 2)] + [(i + 1, i) for i in range(1, lats - 1, 2)]
    first = pltpu.with_memory_space_constraint(inside, pltpu.HBM)
    inside, across = lax.ppermute(inside, "lat", to_core), lax.ppermute(across, "lat", to_chip)
    inner = transport(INNER, *own, first)
    table = jax.ShapeDtypeStruct((2 * GROUPS * 16, LANES), F32)
    inner_table, outer_table = pl.pallas_call(
        target_kernel,
        out_shape=(table, table),
        in_specs=[IN_VMEM] * 3,
        out_specs=(IN_VMEM, IN_VMEM),
        compiler_params=PARAMS,
    )(level_index, level_offset, level_phase)
    outer = transport(OUTER, *own, inside, across, outer_table)
    inner = first_hop(after(inner, inside, across))
    inner, outer = second_hop(after(inner, outer)), exchange(outer)
    inner = remap_inner(inner, inner_table)
    outer = remap_outer(after(outer, inner), outer_table)
    inner = first_hop(inner, True)
    inner, outer = second_hop(after(inner, outer), True), exchange(outer)
    return collect(OUTER, [outer], collect(INNER, inner))


def solution(mesh):
    in_specs = (
        P(None, "lat", "lev", None),
        P("lat", "lev", None),
        P("lat", "lev", None),
        P("lat", "lev", None),
        P(None, "lat", "lev"),
        P(None, "lat", "lev"),
        P(None, "lat", "lev"),
    )
    out_specs = P(None, "lat", "lev", None)
    return jax.shard_map(shards, mesh=mesh, in_specs=in_specs, out_specs=out_specs, check_vma=False)
```
